32 devices in a mesh: leaf: 4 (over x, core), turn: 8 (over z, y).
Axes of the slice: x: 2, y: 2, z: 4, core: 2. Of those that a mesh axis runs over, the one named last changes fastest.
Arguments:
- echoes: bfloat16 [2048, 64, 256], P(('leaf', 'turn')), may hold values from -6 to 6
- chirp: bfloat16 [2, 128], replicated, may hold values from -0.375 to 0.375
- taps: int32 [2, 2, 128, 8], replicated, may hold values from 0 to 127, as said below
- slots: int32 [4, 8], P('leaf'), may hold values from 0 to 7, each once within a row
Outputs:
- image: bfloat16 [128, 64, 256], P('leaf', 'turn')
The draws below stay inside these ranges and needn't reach their ends.
Inputs may be any that keep to these rules, and one draw needn't show every extreme that they name: Each row of taps is 8 consecutive beam indices starting at a - 4 + s with s from -3 to 3, clipped to the beams. Each row of slots is a permutation.
All inputs are finite; a program needn't handle non-finite values.
Results may differ from the reference program's by a relative error of at most 0.008.
Values may be sent and summed in bfloat16 or wider, within the bound.
No kernel may reach another device: no remote copies, remote signals or barrier semaphores. Data moves between devices by JAX's collectives and lax.ppermute only.
A program may use at most 128 MiB of HBM per device.

```python
import math
from functools import partial
import jax
import jax.numpy as jnp
from jax import lax

CHIRP = 128
SUBP = 64
BEAMS = 128
TAPS = 8
PG = 512
NSUB = 8
PULSES = 2048
NBLK = 64
LEVELS = 2
N_LEAF = 4


def draw_taps(key, part):
    shifts = jax.random.randint(key, (LEVELS, 2, BEAMS), -3, 4).astype(jnp.int32)
    base = jnp.arange(BEAMS, dtype=jnp.int32)[:, None] + jnp.arange(TAPS, dtype=jnp.int32)[None, :] - TAPS // 2
    return jnp.clip(base[None, None] + shifts[..., None], 0, BEAMS - 1).astype(jnp.int32)


def levels(rng, shape, pieces, low, top_value):
    def one(position, parts):
        draws = jax.random.uniform(jax.random.fold_in(jax.random.fold_in(rng, 6), position), (parts,), jnp.float32, low / len(pieces), top_value / len(pieces))
        return jnp.repeat(jnp.exp(draws), shape[position] // parts).reshape((-1,) + (1,) * (len(shape) - position - 1))

    loudness = one(*pieces[0])
    for cut in pieces[1:]:
        loudness = loudness * one(*cut)
    return loudness


def scatter_about(stream_key, extent, spread, limit, cuts=(), held_as=jnp.bfloat16):
    result = spread * jax.random.normal(stream_key, extent, jnp.float32)
    if cuts:
        result = result * levels(stream_key, extent, cuts, -0.22, 0.18)
    return jnp.clip(result, -limit, limit).astype(held_as)


def setup_inputs(seed: int = 0) -> dict:
    keys = jax.random.split(jax.random.key(seed), 5)
    return {
        "echoes": scatter_about(keys[0], (PULSES, NBLK, 2 * CHIRP), 1.0, 6.0, ((0, 32),)),
        "chirp": scatter_about(keys[1], (2, CHIRP), (2 * CHIRP) ** -0.5, 0.375),
        "taps": draw_taps(jax.random.fold_in(keys[4], 71), 0),
        "slots": jax.vmap(lambda own: jax.random.permutation(own, NSUB))(jax.random.split(keys[3], N_LEAF)).reshape((N_LEAF, NSUB)).astype(jnp.int32),
    }


WEIGHTS = (-1.0 / 32, 3.0 / 32, -7.0 / 32, 21.0 / 32, 21.0 / 32, -7.0 / 32, 3.0 / 32, -1.0 / 32)

def chirp_matrices(chirp):
    width = chirp.shape[1]
    rows = jnp.arange(width, dtype=jnp.int32)[:, None]
    cols = jnp.arange(width, dtype=jnp.int32)[None, :]
    offset = jnp.remainder(rows - cols, width)
    picks = (offset[:, :, None] == jnp.arange(width, dtype=jnp.int32)[None, None, :]).astype(jnp.float32)
    table = jnp.einsum('jik,ck->cji', picks, chirp.astype(jnp.float32), precision=lax.Precision.HIGHEST)
    lower = rows >= cols

    def complex_block(mask):
        real_part = jnp.where(mask, table[0], 0.0)
        imag_part = jnp.where(mask, table[1], 0.0)
        upper_half = jnp.concatenate([real_part, imag_part], axis=1)
        lower_half = jnp.concatenate([-imag_part, real_part], axis=1)
        return jnp.concatenate([upper_half, lower_half], axis=0).astype(jnp.bfloat16)
    return (complex_block(lower), complex_block(jnp.logical_not(lower)))

def compress(blocks, following, first_matrix, second_matrix):
    width = blocks.shape[-1]
    total = jnp.dot(blocks.reshape(-1, width), first_matrix, preferred_element_type=jnp.float32)
    total = total + jnp.dot(following.reshape(-1, width), second_matrix, preferred_element_type=jnp.float32)
    return total.astype(jnp.bfloat16).reshape(blocks.shape)

def steering(slot_row, beams, sub_len):
    count = slot_row.shape[0]
    beam = jnp.arange(beams, dtype=jnp.int32)[:, None, None]
    place = jnp.arange(sub_len, dtype=jnp.int32)[None, None, :]
    slot = slot_row.astype(jnp.int32)[None, :, None]
    period = 8 * sub_len
    phase_int = jnp.remainder((2 * beam + 1 - beams) * (2 * place + 1 - sub_len) + 3 * (beam + 1) * (2 * slot + 1) * (2 * place + 1), period)
    angle = phase_int.astype(jnp.float32) * (2.0 * math.pi / period)
    scale = 1.0 / math.sqrt(2.0 * count * sub_len)
    cos_part = (jnp.cos(angle) * scale).reshape(beams, count * sub_len)
    sin_part = (jnp.sin(angle) * scale).reshape(beams, count * sub_len)
    first = jnp.stack([cos_part, -sin_part], axis=1)
    second = jnp.stack([sin_part, cos_part], axis=1)
    return jnp.stack([first, second], axis=1).astype(jnp.bfloat16)

def backproject(data, steer):
    pulses, blocks, width = data.shape
    split = data.reshape(pulses, blocks, 2, width // 2)
    out = jnp.einsum('aecp,pbcj->abej', steer.astype(jnp.float32), split.astype(jnp.float32))
    return out.astype(jnp.bfloat16).reshape(steer.shape[0], blocks, width)

def merge_step(level_taps, level, side, first_block, child):
    beams, blocks, width = child.shape
    half = width // 2
    weights = jnp.array(WEIGHTS, jnp.float32)
    cells = jnp.arange(beams, dtype=jnp.int32)
    beam = cells[:, None, None]
    bins = (first_block * half + jnp.arange(blocks * half, dtype=jnp.int32)).reshape(1, blocks, half)
    picks = (level_taps[side][:, :, None] == cells[None, None, :]).astype(jnp.float32)
    matrix = jnp.einsum('atk,t->ak', picks, weights, precision=lax.Precision.HIGHEST)
    moved = jnp.dot(matrix, child.astype(jnp.float32).reshape(beams, -1), precision=lax.Precision.HIGHEST).reshape(beams, blocks, 2, half)
    sign = 2 * side - 1
    phase_int = jnp.remainder((2 * beam + 1 - beams) * (bins + 1) * (sign * (level + 2)) + beam * beam * (side + 1), 4096)
    angle = phase_int.astype(jnp.float32) * (2.0 * math.pi / 4096)
    cos_part = jnp.cos(angle)
    sin_part = jnp.sin(angle)
    real_part = cos_part * moved[:, :, 0] - sin_part * moved[:, :, 1]
    imag_part = cos_part * moved[:, :, 1] + sin_part * moved[:, :, 0]
    return jnp.stack([real_part, imag_part], axis=2).reshape(beams, blocks, width)

def merge_pair(level_taps, level, first_block, left, right):
    return merge_step(level_taps, level, 0, first_block, left) + merge_step(level_taps, level, 1, first_block, right)

def reference(echoes, chirp, taps, slots):
    first_matrix, second_matrix = chirp_matrices(chirp)
    width = echoes.shape[2]
    groups = echoes.reshape(N_LEAF, PG, NBLK, width)

    def one_group(pair):
        block, slot_row = pair
        following = jnp.concatenate([block[:, 1:], jnp.zeros((PG, 1, width), jnp.bfloat16)], axis=1)
        compressed = compress(block, following, first_matrix, second_matrix)
        return backproject(compressed, steering(slot_row, BEAMS, SUBP))
    images = lax.map(one_group, (groups, slots)).astype(jnp.float32)
    for level in range(LEVELS):
        step_fn = jax.vmap(partial(merge_pair, taps[level], level, 0))
        images = step_fn(images[0::2], images[1::2])
    return images[0].astype(jnp.bfloat16)
```

```python
import functools
import math

import jax
import jax.numpy as jnp
from jax import lax
from jax.experimental import pallas as pl
from jax.experimental.pallas import tpu as pltpu
from jax.sharding import Mesh, PartitionSpec as P

WEIGHTS = (-1.0 / 32, 3.0 / 32, -7.0 / 32, 21.0 / 32, 21.0 / 32, -7.0 / 32, 3.0 / 32, -1.0 / 32)
PERIOD = 4096


def unit(phase_int, period):
    angle = jnp.remainder(phase_int, period).astype(jnp.float32) * (2.0 * math.pi / period)
    return jnp.cos(angle), jnp.sin(angle)


def compress_kernel(dims, chirp_ref, echo_ref, out_ref, weights, sums, carry):
    leaf, ty, inner, pulses, half = dims
    blocks = leaf * ty * inner

    @pl.when(pl.program_id(0) == 0)
    def _():
        rows = lax.broadcasted_iota(jnp.int32, (half, half), 0)
        cols = lax.broadcasted_iota(jnp.int32, (half, half), 1)
        taps = chirp_ref[...].astype(jnp.float32)
        tables = []
        for c in range(2):
            wide = jnp.broadcast_to(taps[c : c + 1], (half, half))
            tables.append(pltpu.roll(wide, 0, 1, stride=1, stride_axis=0).T)
        for m, mask in enumerate((rows >= cols, rows < cols)):
            re, im = (jnp.where(mask, t, 0.0) for t in tables)
            top = jnp.concatenate([re, im], axis=1)
            low = jnp.concatenate([-im, re], axis=1)
            full = jnp.concatenate([top, low], axis=0)
            weights[:, m * 2 * half : (m + 1) * 2 * half] = full.astype(jnp.bfloat16)
        carry[...] = jnp.zeros_like(carry)

    data = echo_ref[...].reshape(pulses * blocks, 2 * half)
    for n in range(4):
        sums[n] = jnp.dot(
            data, weights[:, n * half : (n + 1) * half], preferred_element_type=jnp.float32
        )
    for y in range(ty):
        for l in range(leaf):
            for i in range(inner):
                b = (y * leaf + l) * inner + i
                for c in range(2):
                    total = sums[c, pl.ds(b, pulses, stride=blocks), :]
                    if b + 1 < blocks:
                        total += sums[2 + c, pl.ds(b + 1, pulses, stride=blocks), :]
                    else:
                        total += carry[c]
                    out_ref[l, y, 0, i, :, c * half : (c + 1) * half] = total.astype(jnp.bfloat16)
    for c in range(2):
        carry[c] = sums[2 + c, pl.ds(0, pulses, stride=blocks), :]


def compress(echoes, chirp, leaf, tz, ty):
    pulses, blocks, width = echoes.shape
    half = width // 2
    inner = blocks // (leaf * tz * ty)
    per = leaf * ty * inner
    return pl.pallas_call(
        functools.partial(compress_kernel, (leaf, ty, inner, pulses, half)),
        grid=(tz,),
        in_specs=[
            pl.BlockSpec((2, half), lambda z: (0, 0)),
            pl.BlockSpec((pulses, per, width), lambda z: (0, tz - 1 - z, 0)),
        ],
        out_specs=pl.BlockSpec(
            (leaf, ty, 1, inner, pulses, width), lambda z: (0, 0, tz - 1 - z, 0, 0, 0)
        ),
        out_shape=jax.ShapeDtypeStruct((leaf, ty, tz, inner, pulses, width), jnp.bfloat16),
        scratch_shapes=[
            pltpu.VMEM((width, 2 * width), jnp.bfloat16),
            pltpu.VMEM((4, pulses * per, half), jnp.float32),
            pltpu.VMEM((2, pulses, half), jnp.float32),
        ],
        compiler_params=pltpu.CompilerParams(vmem_limit_bytes=48 * 2**20),
        cost_estimate=pl.CostEstimate(
            flops=4 * pulses * blocks * width * width,
            bytes_accessed=4 * pulses * blocks * width,
            transcendentals=0,
        ),
        name="compress",
    )(chirp, echoes)


def image_kernel(dims, data_ref, steer_ref, interp_ref, phase_ref, out_ref):
    leaf, ty, inner, pulses, half, beams, levels = dims
    wide = inner * half

    def turned(phase, re, im):
        c, s = phase
        return c * re - s * im, c * im + s * re

    def total(left, right):
        return left[0] + right[0], left[1] + right[1]

    current = []
    cos, sin = phase_ref[0, 0], phase_ref[0, 1]
    for l in range(leaf):
        parts = []
        for y in range(ty):
            for c in range(2):
                cols = slice(c * half, (c + 1) * half)
                parts.append(
                    jnp.concatenate([data_ref[l, y, 0, i, :, cols] for i in range(inner)], axis=1)
                )
        raw = jnp.dot(
            steer_ref[l], jnp.concatenate(parts, axis=0), preferred_element_type=jnp.float32
        )
        side = turned((cos, sin if l & 1 else -sin), raw[:beams], raw[beams:])
        if l & 1:
            current[-1] = total(current[-1], side)
        else:
            current.append(side)
    for level in range(1, levels):
        merged = []
        for n, (re, im) in enumerate(current):
            side = n & 1
            both = jnp.concatenate([re, im], axis=1)
            high = both.astype(jnp.bfloat16)
            low = (both - high.astype(jnp.float32)).astype(jnp.bfloat16)
            moved = jnp.dot(
                interp_ref[level - 1, side],
                jnp.concatenate([high, low], axis=0),
                preferred_element_type=jnp.float32,
            )
            at = 2 + 4 * (level - 1) + 2 * side
            phase = (phase_ref[0, at], phase_ref[0, at + 1])
            moved = turned(phase, moved[:, :wide], moved[:, wide:])
            if side:
                merged[-1] = total(merged[-1], moved)
            else:
                merged.append(moved)
        current = merged
    rows = beams // leaf
    for c in range(2):
        image = current[0][c].astype(jnp.bfloat16)
        for l in range(leaf):
            for i in range(inner):
                out_ref[l, 0, i, :, c * half : (c + 1) * half] = image[
                    l * rows : (l + 1) * rows, i * half : (i + 1) * half
                ]


def backproject(data, steer, interp, phases):
    leaf, ty, tz, inner, pulses, width = data.shape
    half = width // 2
    beams = steer.shape[1] // 2
    levels = leaf.bit_length() - 1
    rows = beams // leaf
    tables = phases.shape[1]
    flops = 4 * beams * leaf * ty * pulses * tz * inner * width
    return pl.pallas_call(
        functools.partial(image_kernel, (leaf, ty, inner, pulses, half, beams, levels)),
        grid=(tz,),
        in_specs=[
            pl.BlockSpec((leaf, ty, 1, inner, pulses, width), lambda z: (0, 0, z, 0, 0, 0)),
            pl.BlockSpec(steer.shape, lambda z: (0, 0, 0)),
            pl.BlockSpec(interp.shape, lambda z: (0, 0, 0, 0)),
            pl.BlockSpec((1, tables, beams, inner * half), lambda z: (z, 0, 0, 0)),
        ],
        out_specs=pl.BlockSpec((leaf, 1, inner, rows, width), lambda z: (0, z, 0, 0, 0)),
        out_shape=jax.ShapeDtypeStruct((leaf, tz, inner, rows, width), jnp.bfloat16),
        compiler_params=pltpu.CompilerParams(vmem_limit_bytes=48 * 2**20),
        cost_estimate=pl.CostEstimate(
            flops=flops, bytes_accessed=2 * data.size + 4 * phases.size, transcendentals=0
        ),
        name="image",
    )(data, steer, interp, phases)


def sum_kernel(dims, parts_ref, out_ref, rows_ref):
    leaf, tz, inner, rows, width = dims
    blocks = leaf * inner
    for l in range(leaf):
        for i in range(inner):
            acc = parts_ref[l, 0, i].astype(jnp.float32)
            for z in range(1, tz):
                acc += parts_ref[l, z, i].astype(jnp.float32)
            for c in range(2):
                cols = slice(c * width // 2, (c + 1) * width // 2)
                rows_ref[c, pl.ds(l * inner + i, rows, stride=blocks), :] = acc[:, cols]
    both = jnp.concatenate([rows_ref[0], rows_ref[1]], axis=1)
    out_ref[...] = both.reshape(rows, blocks, width).astype(jnp.bfloat16)


def reduce_parts(parts):
    leaf, tz, inner, rows, width = parts.shape
    blocks = leaf * inner
    return pl.pallas_call(
        functools.partial(sum_kernel, parts.shape),
        out_shape=jax.ShapeDtypeStruct((rows, blocks, width), jnp.bfloat16),
        scratch_shapes=[pltpu.VMEM((2, rows * blocks, width // 2), jnp.float32)],
        name="sum_parts",
    )(parts)


def interpolation(taps, beams):
    cells = jnp.arange(beams, dtype=jnp.int32)
    weights = jnp.array(WEIGHTS, jnp.float32)
    picks = taps[..., None] == cells
    return jnp.where(picks, weights[:, None], 0.0).sum(axis=-2)


def steering(slots, matrices, beams, pulses, scale):
    leaf, ty = slots.shape
    beam = jnp.arange(beams, dtype=jnp.int32)[None, :, None, None]
    place = jnp.arange(pulses, dtype=jnp.int32)
    slot = slots[:, None, :, None]
    cos, sin = unit(
        (2 * beam + 1 - beams) * (2 * place + 1 - pulses)
        + 3 * (beam + 1) * (2 * slot + 1) * (2 * place + 1),
        8 * pulses,
    )
    pair = jnp.stack([cos * scale, sin * scale], axis=3).astype(jnp.bfloat16)
    pair = pair.reshape(leaf // 2, 2, beams, ty * 2 * pulses)
    moved = jnp.einsum(
        "cab,kcbn->kcan",
        matrices.astype(jnp.bfloat16),
        pair,
        preferred_element_type=jnp.float32,
    ).reshape(leaf, beams, ty, 2, pulses)
    re, im = moved[:, :, :, 0], moved[:, :, :, 1]
    row = jnp.arange(beams, dtype=jnp.int32)
    side = (jnp.arange(leaf, dtype=jnp.int32) & 1)[:, None]
    c, s = (t[:, :, None, None] for t in unit(row * row * (side + 1), PERIOD))
    re, im = c * re - s * im, c * im + s * re
    top = jnp.stack([re, -im], axis=3)
    low = jnp.stack([im, re], axis=3)
    full = jnp.concatenate([top, low], axis=1)
    return full.reshape(leaf, 2 * beams, ty * 2 * pulses).astype(jnp.bfloat16)


def phase_tables(first, steps, tz, inner, half, beams, levels):
    row = jnp.arange(beams, dtype=jnp.int32)[None, :, None]
    place = jnp.arange(inner * half, dtype=jnp.int32)[None, None, :]
    z = jnp.arange(tz, dtype=jnp.int32)[:, None, None]
    bins = first + z * steps + place + 1
    lean = (2 * row + 1 - beams) * bins
    tables = list(unit(2 * lean, PERIOD))
    for level in range(1, levels):
        for side in range(2):
            tables += unit((2 * side - 1) * (level + 2) * lean + row * row * (side + 1), PERIOD)
    return jnp.stack(tables, axis=1)


def per_device(leaf, tz, ty, echoes, chirp, taps, slots):
    pulses, blocks, width = echoes.shape
    half = width // 2
    beams = taps.shape[2]
    levels = leaf.bit_length() - 1
    inner = blocks // (leaf * tz * ty)
    sent = compress(echoes, chirp, leaf, tz, ty)
    data = lax.all_to_all(
        sent.reshape((leaf * ty,) + sent.shape[2:]), ("leaf", "ty"), 0, 0, tiled=True
    ).reshape(sent.shape)

    own_leaf, own_z, own_y = (lax.axis_index(name) for name in ("leaf", "tz", "ty"))
    all_slots = lax.all_gather(slots, "leaf", axis=0, tiled=True)
    own_slots = lax.dynamic_slice_in_dim(all_slots, own_z * ty, ty, 1)
    matrices = interpolation(taps, beams)
    scale = 1.0 / math.sqrt(2.0 * all_slots.shape[1] * pulses)
    steer = steering(own_slots, matrices[0], beams, pulses, scale)
    interp = jnp.concatenate([matrices[1:]] * 2, axis=-1).astype(jnp.bfloat16)
    first = (own_y * leaf + own_leaf) * inner * half
    phases = phase_tables(first, ty * leaf * inner * half, tz, inner, half, beams, levels)

    parts = backproject(data, steer, interp, phases)
    parts = lax.all_to_all(
        parts.reshape((leaf * tz,) + parts.shape[2:]), ("leaf", "tz"), 0, 0, tiled=True
    ).reshape(parts.shape)
    return reduce_parts(parts)


def solution(mesh):
    leaf, turn = mesh.shape["leaf"], mesh.shape["turn"]
    ty = 1 << (turn.bit_length() - 1) // 2
    tz = turn // ty
    fine = Mesh(mesh.devices.reshape(leaf, tz, ty), ("leaf", "tz", "ty"))
    placed = (P(("leaf", "tz", "ty"), None, None), P(), P(), P("leaf", None))
    return jax.shard_map(
        functools.partial(per_device, leaf, tz, ty),
        mesh=fine,
        in_specs=placed,
        out_specs=P("leaf", ("tz", "ty"), None),
        check_vma=False,
    )
```

```python
import functools
import math

import jax
import jax.numpy as jnp
from jax import lax
from jax.experimental import pallas as pl
from jax.experimental.pallas import tpu as pltpu
from jax.sharding import Mesh, PartitionSpec as P

WEIGHTS = (-1.0 / 32, 3.0 / 32, -7.0 / 32, 21.0 / 32, 21.0 / 32, -7.0 / 32, 3.0 / 32, -1.0 / 32)
PERIOD = 4096


def unit(phase_int, period):
    angle = jnp.remainder(phase_int, period).astype(jnp.float32) * (2.0 * math.pi / period)
    return jnp.cos(angle), jnp.sin(angle)


def compress_kernel(dims, chirp_ref, echo_ref, out_ref, weights, sums, carry):
    leaf, ty, inner, pulses, half = dims
    blocks = leaf * ty * inner

    @pl.when((pl.program_id(0) == 0) & (pl.program_id(1) == 0))
    def _():
        rows = lax.broadcasted_iota(jnp.int32, (half, half), 0)
        cols = lax.broadcasted_iota(jnp.int32, (half, half), 1)
        taps = chirp_ref[...].astype(jnp.float32)
        tables = []
        for c in range(2):
            wide = jnp.broadcast_to(taps[c : c + 1], (half, half))
            tables.append(pltpu.roll(wide, 0, 1, stride=1, stride_axis=0).T)
        for m, mask in enumerate((rows >= cols, rows < cols)):
            re, im = (jnp.where(mask, t, 0.0) for t in tables)
            top = jnp.concatenate([re, im], axis=1)
            low = jnp.concatenate([-im, re], axis=1)
            full = jnp.concatenate([top, low], axis=0)
            weights[:, m * 2 * half : (m + 1) * 2 * half] = full.astype(jnp.bfloat16)
        carry[...] = jnp.zeros_like(carry)

    data = echo_ref[...].reshape(pulses * blocks, 2 * half)
    for n in range(4):
        sums[n] = jnp.dot(
            data, weights[:, n * half : (n + 1) * half], preferred_element_type=jnp.float32
        )
    for y in range(ty):
        for l in range(leaf):
            for i in range(inner):
                b = (y * leaf + l) * inner + i
                for c in range(2):
                    total = sums[c, pl.ds(b, pulses, stride=blocks), :]
                    if b + 1 < blocks:
                        total += sums[2 + c, pl.ds(b + 1, pulses, stride=blocks), :]
                    else:
                        total += carry[c]
                    out_ref[l, y, 0, i, :, c * half : (c + 1) * half] = total.astype(jnp.bfloat16)
    for c in range(2):
        carry[c] = sums[2 + c, pl.ds(0, pulses, stride=blocks), :]


def compress(echoes, chirp, leaf, tz, ty):
    pulses, blocks, width = echoes.shape
    half = width // 2
    inner = blocks // (leaf * tz * ty)
    each = min(2, ty)
    cuts = ty // each
    per = leaf * each * inner
    return pl.pallas_call(
        functools.partial(compress_kernel, (leaf, each, inner, pulses, half)),
        grid=(tz, cuts),
        in_specs=[
            pl.BlockSpec((2, half), lambda z, y: (0, 0)),
            pl.BlockSpec(
                (pulses, per, width), lambda z, y: (0, (tz - 1 - z) * cuts + cuts - 1 - y, 0)
            ),
        ],
        out_specs=pl.BlockSpec(
            (leaf, each, 1, inner, pulses, width),
            lambda z, y: (0, cuts - 1 - y, tz - 1 - z, 0, 0, 0),
        ),
        out_shape=jax.ShapeDtypeStruct((leaf, ty, tz, inner, pulses, width), jnp.bfloat16),
        scratch_shapes=[
            pltpu.VMEM((width, 2 * width), jnp.bfloat16),
            pltpu.VMEM((4, pulses * per, half), jnp.float32),
            pltpu.VMEM((2, pulses, half), jnp.float32),
        ],
        compiler_params=pltpu.CompilerParams(vmem_limit_bytes=60 * 2**20),
        cost_estimate=pl.CostEstimate(
            flops=4 * pulses * blocks * width * width,
            bytes_accessed=4 * pulses * blocks * width,
            transcendentals=0,
        ),
        name="compress",
    )(chirp, echoes)


def image_kernel(dims, data_ref, steer_ref, interp_ref, base_ref, step_ref, out_ref):
    leaf, ty, inner, pulses, half, beams, levels = dims
    wide = inner * half

    def turned(phase, re, im):
        c, s = phase
        return c * re - s * im, c * im + s * re

    def total(left, right):
        return left[0] + right[0], left[1] + right[1]

    def phase(level, at, sign):
        base = [jnp.concatenate([base_ref[0, at + n]] * inner, axis=1) for n in range(2)]
        return turned(base, step_ref[level, 0], sign * step_ref[level, 1])

    current = []
    cos, sin = phase(0, 0, 1.0)
    for l in range(leaf):
        parts = []
        for y in range(ty):
            for c in range(2):
                cols = slice(c * half, (c + 1) * half)
                parts.append(
                    jnp.concatenate([data_ref[l, y, 0, i, :, cols] for i in range(inner)], axis=1)
                )
        raw = jnp.dot(
            steer_ref[l], jnp.concatenate(parts, axis=0), preferred_element_type=jnp.float32
        )
        side = turned((cos, sin if l & 1 else -sin), raw[:beams], raw[beams:])
        if l & 1:
            current[-1] = total(current[-1], side)
        else:
            current.append(side)
    for level in range(1, levels):
        merged = []
        for n, (re, im) in enumerate(current):
            side = n & 1
            both = jnp.concatenate([re, im], axis=1)
            high = both.astype(jnp.bfloat16)
            low = (both - high.astype(jnp.float32)).astype(jnp.bfloat16)
            moved = jnp.dot(
                interp_ref[level - 1, side],
                jnp.concatenate([high, low], axis=0),
                preferred_element_type=jnp.float32,
            )
            at = 2 + 4 * (level - 1) + 2 * side
            moved = turned(
                phase(level, at, 2.0 * side - 1.0), moved[:, :wide], moved[:, wide:]
            )
            if side:
                merged[-1] = total(merged[-1], moved)
            else:
                merged.append(moved)
        current = merged
    rows = beams // leaf
    for c in range(2):
        image = current[0][c].astype(jnp.bfloat16)
        for l in range(leaf):
            for i in range(inner):
                out_ref[l, 0, i, :, c * half : (c + 1) * half] = image[
                    l * rows : (l + 1) * rows, i * half : (i + 1) * half
                ]


def backproject(data, steer, interp, base, step):
    leaf, ty, tz, inner, pulses, width = data.shape
    half = width // 2
    beams = steer.shape[1] // 2
    levels = leaf.bit_length() - 1
    rows = beams // leaf
    flops = 4 * beams * leaf * ty * pulses * tz * inner * width
    return pl.pallas_call(
        functools.partial(image_kernel, (leaf, ty, inner, pulses, half, beams, levels)),
        grid=(tz,),
        in_specs=[
            pl.BlockSpec((leaf, ty, 1, inner, pulses, width), lambda z: (0, 0, z, 0, 0, 0)),
            pl.BlockSpec(steer.shape, lambda z: (0, 0, 0)),
            pl.BlockSpec(interp.shape, lambda z: (0, 0, 0, 0)),
            pl.BlockSpec((1,) + base.shape[1:], lambda z: (z, 0, 0, 0)),
            pl.BlockSpec(step.shape, lambda z: (0, 0, 0, 0)),
        ],
        out_specs=pl.BlockSpec((leaf, 1, inner, rows, width), lambda z: (0, z, 0, 0, 0)),
        out_shape=jax.ShapeDtypeStruct((leaf, tz, inner, rows, width), jnp.bfloat16),
        compiler_params=pltpu.CompilerParams(vmem_limit_bytes=60 * 2**20),
        cost_estimate=pl.CostEstimate(
            flops=flops, bytes_accessed=2 * data.size + 4 * base.size, transcendentals=0
        ),
        name="image",
    )(data, steer, interp, base, step)


def sum_kernel(dims, parts_ref, out_ref, rows_ref):
    leaf, tz, inner, rows, width = dims
    blocks = leaf * inner
    for l in range(leaf):
        for i in range(inner):
            acc = parts_ref[l, 0, i].astype(jnp.float32)
            for z in range(1, tz):
                acc += parts_ref[l, z, i].astype(jnp.float32)
            for c in range(2):
                cols = slice(c * width // 2, (c + 1) * width // 2)
                rows_ref[c, pl.ds(l * inner + i, rows, stride=blocks), :] = acc[:, cols]
    both = jnp.concatenate([rows_ref[0], rows_ref[1]], axis=1)
    out_ref[...] = both.reshape(rows, blocks, width).astype(jnp.bfloat16)


def reduce_parts(parts):
    leaf, tz, inner, rows, width = parts.shape
    blocks = leaf * inner
    return pl.pallas_call(
        functools.partial(sum_kernel, parts.shape),
        out_shape=jax.ShapeDtypeStruct((rows, blocks, width), jnp.bfloat16),
        scratch_shapes=[pltpu.VMEM((2, rows * blocks, width // 2), jnp.float32)],
        name="sum_parts",
    )(parts)


def interpolation(taps, beams):
    cells = jnp.arange(beams, dtype=jnp.int32)
    weights = jnp.array(WEIGHTS, jnp.float32)
    picks = taps[..., None] == cells
    return jnp.where(picks, weights[:, None], 0.0).sum(axis=-2)


def steering(slots, matrices, beams, pulses, scale):
    leaf, ty = slots.shape
    beam = jnp.arange(beams, dtype=jnp.int32)[None, :, None, None]
    place = jnp.arange(pulses, dtype=jnp.int32)
    slot = slots[:, None, :, None]
    cos, sin = unit(
        (2 * beam + 1 - beams) * (2 * place + 1 - pulses)
        + 3 * (beam + 1) * (2 * slot + 1) * (2 * place + 1),
        8 * pulses,
    )
    pair = jnp.stack([cos * scale, sin * scale], axis=3).astype(jnp.bfloat16)
    pair = pair.reshape(leaf // 2, 2, beams, ty * 2 * pulses)
    moved = jnp.einsum(
        "cab,kcbn->kcan",
        matrices.astype(jnp.bfloat16),
        pair,
        preferred_element_type=jnp.float32,
    ).reshape(leaf, beams, ty, 2, pulses)
    re, im = moved[:, :, :, 0], moved[:, :, :, 1]
    row = jnp.arange(beams, dtype=jnp.int32)
    side = (jnp.arange(leaf, dtype=jnp.int32) & 1)[:, None]
    c, s = (t[:, :, None, None] for t in unit(row * row * (side + 1), PERIOD))
    re, im = c * re - s * im, c * im + s * re
    top = jnp.stack([re, -im], axis=3)
    low = jnp.stack([im, re], axis=3)
    full = jnp.concatenate([top, low], axis=1)
    return full.reshape(leaf, 2 * beams, ty * 2 * pulses).astype(jnp.bfloat16)


def phase_tables(first, steps, tz, inner, half, beams, levels):
    row = jnp.arange(beams, dtype=jnp.int32)
    lean = 2 * row + 1 - beams
    start = first + jnp.arange(tz, dtype=jnp.int32)[:, None] * steps
    base = list(unit(2 * lean * start, PERIOD))
    for level in range(1, levels):
        for side in range(2):
            base += unit(
                (2 * side - 1) * (level + 2) * lean * start + row * row * (side + 1), PERIOD
            )
    base = jnp.stack(base, axis=1)[..., None]
    place = jnp.arange(inner * half, dtype=jnp.int32) + 1
    level = jnp.arange(levels, dtype=jnp.int32)[:, None, None]
    step = jnp.stack(unit((level + 2) * lean[:, None] * place, PERIOD), axis=1)
    return jnp.broadcast_to(base, base.shape[:-1] + (half,)), step


def per_device(leaf, tz, ty, echoes, chirp, taps, slots):
    pulses, blocks, width = echoes.shape
    half = width // 2
    beams = taps.shape[2]
    levels = leaf.bit_length() - 1
    inner = blocks // (leaf * tz * ty)
    own_leaf, own_z, own_y = (lax.axis_index(name) for name in ("leaf", "tz", "ty"))
    own_slot = lax.dynamic_slice_in_dim(slots, own_z * ty + own_y, 1, 1)
    own_slots = lax.all_to_all(
        jnp.broadcast_to(own_slot[:, :, None], (leaf * ty, 1, 128)), ("leaf", "ty"), 0, 0, tiled=True
    )
    sent = compress(echoes, chirp, leaf, tz, ty)
    sent, own_slots = lax.optimization_barrier((sent, own_slots))
    own_slots = own_slots[:, 0, 0].reshape(leaf, ty)
    data = lax.all_to_all(
        sent.reshape((leaf * ty,) + sent.shape[2:]), ("leaf", "ty"), 0, 0, tiled=True
    ).reshape(sent.shape)

    matrices = interpolation(taps, beams)
    scale = 1.0 / math.sqrt(2.0 * slots.shape[1] * pulses)
    steer = steering(own_slots, matrices[0], beams, pulses, scale)
    interp = jnp.concatenate([matrices[1:]] * 2, axis=-1).astype(jnp.bfloat16)
    first = (own_y * leaf + own_leaf) * inner * half
    base, step = phase_tables(first, ty * leaf * inner * half, tz, inner, half, beams, levels)

    parts = backproject(data, steer, interp, base, step)
    parts = lax.all_to_all(
        parts.reshape((leaf * tz,) + parts.shape[2:]), ("leaf", "tz"), 0, 0, tiled=True
    ).reshape(parts.shape)
    return reduce_parts(parts)


def solution(mesh):
    leaf, turn = mesh.shape["leaf"], mesh.shape["turn"]
    ty = 1 << turn.bit_length() // 2
    tz = turn // ty
    fine = Mesh(mesh.devices.reshape(leaf, tz, ty), ("leaf", "tz", "ty"))
    placed = (P(("leaf", "tz", "ty"), None, None), P(), P(), P("leaf", None))
    return jax.shard_map(
        functools.partial(per_device, leaf, tz, ty),
        mesh=fine,
        in_specs=placed,
        out_specs=P("leaf", ("tz", "ty"), None),
        check_vma=False,
    )
```

```python
import functools
import math

import jax
import jax.numpy as jnp
from jax import lax
from jax.experimental import pallas as pl
from jax.experimental.pallas import tpu as pltpu
from jax.sharding import PartitionSpec as P

WEIGHTS = (-1.0 / 32, 3.0 / 32, -7.0 / 32, 21.0 / 32, 21.0 / 32, -7.0 / 32, 3.0 / 32, -1.0 / 32)
PERIOD = 4096
VMEM_BYTES = 56 * 2**20
SCALARS = pl.BlockSpec(memory_space=pltpu.SMEM)


def bits_of(count):
    return count.bit_length() - 1


def swapped(array, axis, bit):
    return lax.ppermute(array, axis, [(i, i ^ 1 << bit) for i in range(lax.axis_size(axis))])


def unit(phase_int, period):
    angle = jnp.remainder(phase_int, period).astype(jnp.float32) * (2.0 * math.pi / period)
    return jnp.cos(angle), jnp.sin(angle)


def compress_kernel(
    dims, own_ref, chirp_ref, echo_ref, keep_y, send_y, keep_z, send_z, weights, sums, carry
):
    each, pulses, half = dims
    tile = 2 * each
    blocks = 2 * tile
    mids = pl.num_programs(2)
    mid = mids - 1 - pl.program_id(2)
    near = 1 - pl.program_id(1)

    @pl.when((pl.program_id(0) == 0) & (pl.program_id(1) == 0) & (pl.program_id(2) == 0))
    def _():
        rows = lax.broadcasted_iota(jnp.int32, (half, half), 0)
        cols = lax.broadcasted_iota(jnp.int32, (half, half), 1)
        taps = chirp_ref[...].astype(jnp.float32)
        tables = []
        for c in range(2):
            wide = jnp.broadcast_to(taps[c : c + 1], (half, half))
            tables.append(pltpu.roll(wide, 0, 1, stride=1, stride_axis=0).T)
        for m, mask in enumerate((rows >= cols, rows < cols)):
            re, im = (jnp.where(mask, t, 0.0) for t in tables)
            top = jnp.concatenate([re, im], axis=1)
            low = jnp.concatenate([-im, re], axis=1)
            full = jnp.concatenate([top, low], axis=0)
            weights[:, m * 2 * half : (m + 1) * 2 * half] = full.astype(jnp.bfloat16)
        carry[...] = jnp.zeros_like(carry)

    data = echo_ref[...].reshape(pulses * blocks, 2 * half)
    for n in range(4):
        sums[n] = jnp.dot(
            data, weights[:, n * half : (n + 1) * half], preferred_element_type=jnp.float32
        )

    def filtered(b, last=False):
        parts = []
        for c in range(2):
            own = sums[c, pl.ds(b, pulses, stride=blocks), :]
            after = carry[c] if last else sums[2 + c, pl.ds(b + 1, pulses, stride=blocks), :]
            parts.append((own + after).astype(jnp.bfloat16))
        return jnp.concatenate(parts, axis=1)

    own_u = own_ref[0]
    for i in range(each):
        keep_y[0, 0, 0, i] = filtered(own_u * tile + i)
        send_y[0, 0, 0, i] = filtered((1 - own_u) * tile + i)

    def far_chain(out_ref):
        for u in range(2):
            for i in range(each):
                b = u * tile + each + i
                out_ref[0, mid, u, i] = filtered(b, b + 1 == blocks)

    @pl.when(near == own_ref[1])
    def _():
        far_chain(keep_z)

    @pl.when(near != own_ref[1])
    def _():
        far_chain(send_z)

    for c in range(2):
        carry[c] = sums[2 + c, pl.ds(0, pulses, stride=blocks), :]


def compress(own, chirp, echoes, high, mids):
    pulses, blocks, width = echoes.shape
    half = width // 2
    each = blocks // (8 * high * mids)
    shape_y = (high, 2, mids, each, pulses, width)
    shape_z = (high, mids, 2, each, pulses, width)
    spec_y = pl.BlockSpec(
        (1, 1, 1) + shape_y[3:], lambda h, v, m: (high - 1 - h, 1 - v, mids - 1 - m, 0, 0, 0)
    )
    spec_z = pl.BlockSpec((1,) + shape_z[1:], lambda h, v, m: (high - 1 - h, 0, 0, 0, 0, 0))
    return pl.pallas_call(
        functools.partial(compress_kernel, (each, pulses, half)),
        grid=(high, 2, mids),
        in_specs=[
            SCALARS,
            pl.BlockSpec((2, half), lambda h, v, m: (0, 0)),
            pl.BlockSpec(
                (pulses, 4 * each, width),
                lambda h, v, m: (0, ((high - 1 - h) * 2 + 1 - v) * mids + mids - 1 - m, 0),
            ),
        ],
        out_specs=[spec_y, spec_y, spec_z, spec_z],
        out_shape=[
            jax.ShapeDtypeStruct(s, jnp.bfloat16) for s in (shape_y, shape_y, shape_z, shape_z)
        ],
        scratch_shapes=[
            pltpu.VMEM((width, 2 * width), jnp.bfloat16),
            pltpu.VMEM((4, pulses * 4 * each, half), jnp.float32),
            pltpu.VMEM((2, pulses, half), jnp.float32),
        ],
        compiler_params=pltpu.CompilerParams(vmem_limit_bytes=VMEM_BYTES),
        cost_estimate=pl.CostEstimate(
            flops=4 * pulses * blocks * width * width,
            bytes_accessed=4 * pulses * blocks * width,
            transcendentals=0,
        ),
        name="compress",
    )(own, chirp, echoes)


def image_kernel(
    dims, own_ref, keep_ref, got_ref, steer_ref, interp_ref, base_ref, step_ref, out_keep, out_send
):
    leaf, each, half, beams, levels = dims
    rows = beams // leaf
    pair = 2
    own = own_ref[0]

    def turned(phase, re, im):
        c, s = phase
        return c * re - s * im, c * im + s * re

    bases = []
    for n in range(2 * levels):
        bases.append(jnp.broadcast_to(base_ref[0, n : n + 1, :], (half, beams)).T)
    for at in range(0, each, pair):
        parts = []
        for ref in (keep_ref, got_ref):
            for c in range(2):
                cols = slice(c * half, (c + 1) * half)
                parts.append(
                    jnp.concatenate([ref[0, at + i, :, cols] for i in range(pair)], axis=1)
                )
        raw = jnp.dot(
            steer_ref[...], jnp.concatenate(parts, axis=0), preferred_element_type=jnp.float32
        )
        re, im = raw[:beams], raw[beams:]
        for level in range(levels):
            if level:
                both = jnp.concatenate([re, im], axis=1)
                big = both.astype(jnp.bfloat16)
                low = (both - big.astype(jnp.float32)).astype(jnp.bfloat16)
                moved = jnp.dot(
                    interp_ref[level - 1],
                    jnp.concatenate([big, low], axis=0),
                    preferred_element_type=jnp.float32,
                )
                re, im = moved[:, : pair * half], moved[:, pair * half :]
            sides = []
            for i in range(pair):
                lanes = slice((at + i) * half, (at + i + 1) * half)
                phase = turned(
                    (bases[2 * level], bases[2 * level + 1]),
                    step_ref[level, 0, :, lanes],
                    step_ref[level, 1, :, lanes],
                )
                cut = slice(i * half, (i + 1) * half)
                sides.append(turned(phase, re[:, cut], im[:, cut]))
            re, im = (jnp.concatenate([s[c] for s in sides], axis=1) for c in range(2))
        for i in range(pair):
            cut = slice(i * half, (i + 1) * half)
            for g in range(leaf // 2):
                for side in range(2):
                    first = (2 * g + side) * rows
                    value = jnp.concatenate(
                        [t[first : first + rows, cut] for t in (re, im)], axis=1
                    )

                    @pl.when(own == side)
                    def _(value=value, g=g, i=i):
                        out_keep[g, 0, at + i] = value

                    @pl.when(own != side)
                    def _(value=value, g=g, i=i):
                        out_send[g, 0, at + i] = value.astype(jnp.bfloat16)


def backproject(own, keep, got, steer, interp, base, step, leaf):
    count, each, pulses, width = keep.shape
    half = width // 2
    beams = steer.shape[0] // 2
    levels = bits_of(leaf)
    rows = beams // leaf
    shape = (leaf // 2, count, each, rows, width)
    out_spec = pl.BlockSpec((leaf // 2, 1) + shape[2:], lambda n: (0, n, 0, 0, 0))
    in_spec = pl.BlockSpec((1, each, pulses, width), lambda n: (n, 0, 0, 0))
    return pl.pallas_call(
        functools.partial(image_kernel, (leaf, each, half, beams, levels)),
        grid=(count,),
        in_specs=[
            SCALARS,
            in_spec,
            in_spec,
            pl.BlockSpec(steer.shape, lambda n: (0, 0)),
            pl.BlockSpec(interp.shape, lambda n: (0, 0, 0)),
            pl.BlockSpec((1,) + base.shape[1:], lambda n: (n, 0, 0)),
            pl.BlockSpec(step.shape, lambda n: (0, 0, 0, 0)),
        ],
        out_specs=[out_spec, out_spec],
        out_shape=[
            jax.ShapeDtypeStruct(shape, jnp.float32),
            jax.ShapeDtypeStruct(shape, jnp.bfloat16),
        ],
        compiler_params=pltpu.CompilerParams(vmem_limit_bytes=VMEM_BYTES),
        cost_estimate=pl.CostEstimate(
            flops=12 * beams * pulses * keep.shape[0] * each * width,
            bytes_accessed=4 * keep.size + 6 * shape[0] * count * each * rows * width,
            transcendentals=0,
        ),
        name="image",
    )(own, keep, got, steer, interp, base, step)


def fold_kernel(own_ref, keep_ref, got_ref, out_keep, out_send):
    own = own_ref[0]
    for a in range(keep_ref.shape[0]):
        out_send[a] = (
            keep_ref[a, 1 - own] + got_ref[a, 1 - own].astype(jnp.float32)
        ).astype(jnp.bfloat16)
        out_keep[a] = keep_ref[a, own] + got_ref[a, own].astype(jnp.float32)


def fold(own, keep, got):
    shape = keep.shape[:1] + keep.shape[2:]
    return pl.pallas_call(
        fold_kernel,
        in_specs=[SCALARS] + [pl.BlockSpec(memory_space=pltpu.VMEM)] * 2,
        out_specs=[pl.BlockSpec(memory_space=pltpu.VMEM)] * 2,
        out_shape=[
            jax.ShapeDtypeStruct(shape, jnp.float32),
            jax.ShapeDtypeStruct(shape, jnp.bfloat16),
        ],
        compiler_params=pltpu.CompilerParams(vmem_limit_bytes=VMEM_BYTES),
        cost_estimate=pl.CostEstimate(
            flops=keep.size, bytes_accessed=9 * keep.size, transcendentals=0
        ),
        name="fold",
    )(own, keep, got)


def last_kernel(keep_y, got_y, keep_z, got_z, out_ref, rows_ref):
    each, rows, width = keep_y.shape
    blocks = 2 * each
    for n, (keep, got) in enumerate(((keep_y, got_y), (keep_z, got_z))):
        for i in range(each):
            value = keep[i] + got[i].astype(jnp.float32)
            for c in range(2):
                cols = slice(c * width // 2, (c + 1) * width // 2)
                rows_ref[c, pl.ds(n * each + i, rows, stride=blocks), :] = value[:, cols]
    both = jnp.concatenate([rows_ref[0], rows_ref[1]], axis=1)
    out_ref[...] = both.reshape(rows, blocks, width).astype(jnp.bfloat16)


def last_sum(keep_y, got_y, keep_z, got_z):
    each, rows, width = keep_y.shape
    return pl.pallas_call(
        last_kernel,
        out_shape=jax.ShapeDtypeStruct((rows, 2 * each, width), jnp.bfloat16),
        scratch_shapes=[pltpu.VMEM((2, rows * 2 * each, width // 2), jnp.float32)],
        name="last_sum",
    )(keep_y, got_y, keep_z, got_z)


def interpolation(taps, beams):
    cells = jnp.arange(beams, dtype=jnp.int32)
    weights = jnp.array(WEIGHTS, jnp.float32)
    picks = taps[..., None] == cells
    return jnp.where(picks, weights[:, None], 0.0).sum(axis=-2)


def steering(slots, matrix, side, beams, pulses, scale):
    count = slots.shape[0]
    beam = jnp.arange(beams, dtype=jnp.int32)[:, None, None]
    place = jnp.arange(pulses, dtype=jnp.int32)
    slot = slots[None, :, None]
    cos, sin = unit(
        (2 * beam + 1 - beams) * (2 * place + 1 - pulses)
        + 3 * (beam + 1) * (2 * slot + 1) * (2 * place + 1),
        8 * pulses,
    )
    pair = jnp.concatenate([cos * scale, sin * scale], axis=2).astype(jnp.bfloat16)
    moved = jnp.dot(
        matrix.astype(jnp.bfloat16),
        pair.reshape(beams, count * 2 * pulses),
        preferred_element_type=jnp.float32,
    ).reshape(beams, count, 2 * pulses)
    re, im = moved[:, :, :pulses], moved[:, :, pulses:]
    row = jnp.arange(beams, dtype=jnp.int32)
    c, s = (t[:, None, None] for t in unit(row * row * (side + 1), PERIOD))
    re, im = c * re - s * im, c * im + s * re
    top = jnp.concatenate([re, -im], axis=2)
    low = jnp.concatenate([im, re], axis=2)
    return jnp.concatenate([top, low], axis=0).astype(jnp.bfloat16)


def bit(value, at):
    return value >> at & 1


def per_device(echoes, chirp, taps, slots):
    leaf, turn = lax.axis_size("leaf"), lax.axis_size("turn")
    pulses, blocks, width = echoes.shape
    half = width // 2
    beams = taps.shape[2]
    levels = bits_of(leaf)
    far = (bits_of(turn) + 1) // 2 - 1 if turn > 4 else 1
    mids = 1 << far - 1
    high = turn >> far + 1
    each = blocks // (2 * turn)
    rows = beams // leaf
    own_leaf, own_turn = lax.axis_index("leaf"), lax.axis_index("turn")

    def scalar(value):
        return jnp.asarray(value, jnp.int32).reshape(1)

    own_bits = jnp.concatenate([scalar(bit(own_turn, 0)), scalar(bit(own_turn, far))])
    keep_y, send_y, keep_z, send_z = compress(own_bits, chirp, echoes, high, mids)
    got_y = swapped(send_y, "turn", 0)
    got_z = swapped(send_z, "turn", far)

    own_sides = [bit(own_leaf, level) for level in range(levels)]
    own_taps = jnp.stack(
        [lax.dynamic_index_in_dim(taps[n], own_sides[n], 0, False) for n in range(levels)]
    )
    matrices = interpolation(own_taps, beams)
    scale = 1.0 / math.sqrt(2.0 * slots.shape[1] * pulses)
    own_slots = jnp.concatenate(
        [
            lax.dynamic_index_in_dim(slots[0], own_turn ^ other, 0, True)
            for other in (0, 1, 1 << far)
        ]
    )
    steer = steering(own_slots, matrices[0], own_sides[0], beams, pulses, scale)
    steer_y = steer[:, :2].reshape(2 * beams, 4 * pulses)
    steer_z = jnp.concatenate([steer[:, :1], steer[:, 2:]], axis=1).reshape(2 * beams, 4 * pulses)
    interp = jnp.concatenate([matrices[1:]] * 2, axis=-1).astype(jnp.bfloat16)

    row = jnp.arange(beams, dtype=jnp.int32)
    lean = 2 * row + 1 - beams
    place = jnp.arange(each * half, dtype=jnp.int32) + 1
    slopes = jnp.stack([(2 * own_sides[n] - 1) * (n + 2) for n in range(levels)])
    step = jnp.stack(unit(slopes[:, None, None] * lean[:, None] * place, PERIOD), axis=1)
    squares = jnp.stack(
        [row * row * (own_sides[n] + 1) * (1 if n else 0) for n in range(levels)]
    )

    def bases(tiles, shift):
        start = ((tiles * 2 + shift) * each * half)[:, None, None]
        both = jnp.stack(unit(slopes[:, None] * lean * start + squares, PERIOD), axis=2)
        return both.reshape(tiles.shape[0], 2 * levels, beams)

    count = turn // 2
    index = jnp.arange(count, dtype=jnp.int32)
    tiles_y = 2 * index + bit(own_turn, 0)
    low_part = index & (1 << far) - 1
    tiles_z = ((index >> far) * 2 + bit(own_turn, far)) * (1 << far) + low_part

    own_core = scalar(bit(own_leaf, 0))
    final = []
    for name, keep, got, steer_own, tiles in (
        ("y", keep_y, got_y, steer_y, tiles_y),
        ("z", keep_z, got_z, steer_z, tiles_z),
    ):
        shape = (count, each, pulses, width)
        base = bases(tiles, 0 if name == "y" else 1)
        kept, sent = backproject(
            own_core, keep.reshape(shape), got.reshape(shape), steer_own, interp, base, step, leaf
        )
        gone = 0 if name == "y" else far
        leading = [("leaf", b) for b in range(levels - 1, 0, -1)]
        leading += [("turn", b) for b in range(bits_of(turn) - 1, -1, -1) if b != gone]
        order = [("leaf", b) for b in range(1, levels)]
        rest = [("turn", b) for b in range(bits_of(turn)) if b not in (0, far)]
        order = order + [("turn", far)] if name == "y" else [("turn", 0)] + order
        arrived = swapped(sent, "leaf", 0)
        for axis, b in order + rest:
            at = leading.index((axis, b))
            before, after = 1 << at, (1 << len(leading) - at - 1) * each
            leading.pop(at)
            split = (before, 2, after, rows, width)
            own = scalar(bit(own_leaf if axis == "leaf" else own_turn, b))
            kept, sent = fold(own, kept.reshape(split), arrived.reshape(split))
            arrived = swapped(sent, axis, b)
        final += [kept.reshape(each, rows, width), arrived.reshape(each, rows, width)]
    return last_sum(*final)


def solution(mesh):
    placed = (P(("leaf", "turn"), None, None), P(), P(), P("leaf", None))
    return jax.shard_map(
        per_device, mesh=mesh, in_specs=placed, out_specs=P("leaf", "turn", None), check_vma=False
    )
```

```python
import functools
import math

import jax
import jax.numpy as jnp
from jax import lax
from jax.experimental import pallas as pl
from jax.experimental.pallas import tpu as pltpu
from jax.sharding import PartitionSpec as P

WEIGHTS = (-1.0 / 32, 3.0 / 32, -7.0 / 32, 21.0 / 32, 21.0 / 32, -7.0 / 32, 3.0 / 32, -1.0 / 32)
PERIOD = 4096
VMEM_BYTES = 56 * 2**20
SCALARS = pl.BlockSpec(memory_space=pltpu.SMEM)


def bits_of(count):
    return count.bit_length() - 1


def swapped(array, axis, bit):
    return lax.ppermute(array, axis, [(i, i ^ 1 << bit) for i in range(lax.axis_size(axis))])


def unit(phase_int, period):
    angle = jnp.remainder(phase_int, period).astype(jnp.float32) * (2.0 * math.pi / period)
    return jnp.cos(angle), jnp.sin(angle)


def compress_kernel(
    dims, own_ref, chirp_ref, echo_ref, keep_y, send_y, keep_z, send_z, weights, sums, carry
):
    each, pulses, half = dims
    tile = 2 * each
    blocks = 2 * tile
    mids = pl.num_programs(2)
    mid = mids - 1 - pl.program_id(2)
    near = 1 - pl.program_id(1)

    @pl.when((pl.program_id(0) == 0) & (pl.program_id(1) == 0) & (pl.program_id(2) == 0))
    def _():
        rows = lax.broadcasted_iota(jnp.int32, (half, half), 0)
        cols = lax.broadcasted_iota(jnp.int32, (half, half), 1)
        taps = chirp_ref[...].astype(jnp.float32)
        tables = []
        for c in range(2):
            wide = jnp.broadcast_to(taps[c : c + 1], (half, half))
            tables.append(pltpu.roll(wide, 0, 1, stride=1, stride_axis=0).T)
        for m, mask in enumerate((rows >= cols, rows < cols)):
            re, im = (jnp.where(mask, t, 0.0) for t in tables)
            top = jnp.concatenate([re, im], axis=1)
            low = jnp.concatenate([-im, re], axis=1)
            full = jnp.concatenate([top, low], axis=0)
            weights[:, m * 2 * half : (m + 1) * 2 * half] = full.astype(jnp.bfloat16)
        carry[...] = jnp.zeros_like(carry)

    data = echo_ref[...].reshape(pulses * blocks, 2 * half)
    for n in range(4):
        sums[n] = jnp.dot(
            data, weights[:, n * half : (n + 1) * half], preferred_element_type=jnp.float32
        )

    def filtered(b, last=False):
        parts = []
        for c in range(2):
            own = sums[c, pl.ds(b, pulses, stride=blocks), :]
            after = carry[c] if last else sums[2 + c, pl.ds(b + 1, pulses, stride=blocks), :]
            parts.append((own + after).astype(jnp.bfloat16))
        return jnp.concatenate(parts, axis=1)

    own_u = own_ref[0]
    for i in range(each):
        keep_y[0, 0, 0, i] = filtered(own_u * tile + i)
        send_y[0, 0, 0, i] = filtered((1 - own_u) * tile + i)

    def far_chain(out_ref):
        for u in range(2):
            for i in range(each):
                b = u * tile + each + i
                out_ref[0, mid, u, i] = filtered(b, b + 1 == blocks)

    @pl.when(near == own_ref[1])
    def _():
        far_chain(keep_z)

    @pl.when(near != own_ref[1])
    def _():
        far_chain(send_z)

    for c in range(2):
        carry[c] = sums[2 + c, pl.ds(0, pulses, stride=blocks), :]


def compress(own, chirp, echoes, high, mids):
    pulses, blocks, width = echoes.shape
    half = width // 2
    each = blocks // (8 * high * mids)
    shape_y = (high, 2, mids, each, pulses, width)
    shape_z = (high, mids, 2, each, pulses, width)
    spec_y = pl.BlockSpec(
        (1, 1, 1) + shape_y[3:], lambda h, v, m: (high - 1 - h, 1 - v, mids - 1 - m, 0, 0, 0)
    )
    spec_z = pl.BlockSpec((1,) + shape_z[1:], lambda h, v, m: (high - 1 - h, 0, 0, 0, 0, 0))
    return pl.pallas_call(
        functools.partial(compress_kernel, (each, pulses, half)),
        grid=(high, 2, mids),
        in_specs=[
            SCALARS,
            pl.BlockSpec((2, half), lambda h, v, m: (0, 0)),
            pl.BlockSpec(
                (pulses, 4 * each, width),
                lambda h, v, m: (0, ((high - 1 - h) * 2 + 1 - v) * mids + mids - 1 - m, 0),
            ),
        ],
        out_specs=[spec_y, spec_y, spec_z, spec_z],
        out_shape=[
            jax.ShapeDtypeStruct(s, jnp.bfloat16) for s in (shape_y, shape_y, shape_z, shape_z)
        ],
        scratch_shapes=[
            pltpu.VMEM((width, 2 * width), jnp.bfloat16),
            pltpu.VMEM((4, pulses * 4 * each, half), jnp.float32),
            pltpu.VMEM((2, pulses, half), jnp.float32),
        ],
        compiler_params=pltpu.CompilerParams(vmem_limit_bytes=VMEM_BYTES),
        cost_estimate=pl.CostEstimate(
            flops=4 * pulses * blocks * width * width,
            bytes_accessed=4 * pulses * blocks * width,
            transcendentals=0,
        ),
        name="compress",
    )(own, chirp, echoes)


def image_kernel(
    dims, own_ref, keep_ref, got_ref, steer_ref, interp_ref, base_ref, step_ref, out_keep, out_send
):
    leaf, each, half, beams, levels = dims
    rows = beams // leaf
    pair = 2
    own = own_ref[0]

    def turned(phase, re, im):
        c, s = phase
        return c * re - s * im, c * im + s * re

    bases = []
    for n in range(2 * levels):
        bases.append(jnp.broadcast_to(base_ref[0, n : n + 1, :], (half, beams)).T)
    for at in range(0, each, pair):
        parts = []
        for ref in (keep_ref, got_ref):
            for c in range(2):
                cols = slice(c * half, (c + 1) * half)
                parts.append(
                    jnp.concatenate([ref[0, at + i, :, cols] for i in range(pair)], axis=1)
                )
        raw = jnp.dot(
            steer_ref[...], jnp.concatenate(parts, axis=0), preferred_element_type=jnp.float32
        )
        re, im = raw[:beams], raw[beams:]
        for level in range(levels):
            if level:
                both = jnp.concatenate([re, im], axis=1)
                big = both.astype(jnp.bfloat16)
                low = (both - big.astype(jnp.float32)).astype(jnp.bfloat16)
                moved = jnp.dot(
                    interp_ref[level - 1],
                    jnp.concatenate([big, low], axis=0),
                    preferred_element_type=jnp.float32,
                )
                re, im = moved[:, : pair * half], moved[:, pair * half :]
            sides = []
            for i in range(pair):
                lanes = slice((at + i) * half, (at + i + 1) * half)
                phase = turned(
                    (bases[2 * level], bases[2 * level + 1]),
                    step_ref[level, 0, :, lanes],
                    step_ref[level, 1, :, lanes],
                )
                cut = slice(i * half, (i + 1) * half)
                sides.append(turned(phase, re[:, cut], im[:, cut]))
            re, im = (jnp.concatenate([s[c] for s in sides], axis=1) for c in range(2))
        for i in range(pair):
            cut = slice(i * half, (i + 1) * half)
            for g in range(leaf // 2):
                for side in range(2):
                    first = (2 * g + side) * rows
                    value = jnp.concatenate(
                        [t[first : first + rows, cut] for t in (re, im)], axis=1
                    )

                    @pl.when(own == side)
                    def _(value=value, g=g, i=i):
                        out_keep[g, 0, at + i] = value

                    @pl.when(own != side)
                    def _(value=value, g=g, i=i):
                        out_send[g, 0, at + i] = value.astype(jnp.bfloat16)


def backproject(own, keep, got, steer, interp, base, step, leaf):
    count, each, pulses, width = keep.shape
    half = width // 2
    beams = steer.shape[0] // 2
    levels = bits_of(leaf)
    rows = beams // leaf
    shape = (leaf // 2, count, each, rows, width)
    out_spec = pl.BlockSpec((leaf // 2, 1) + shape[2:], lambda n: (0, n, 0, 0, 0))
    in_spec = pl.BlockSpec((1, each, pulses, width), lambda n: (n, 0, 0, 0))
    return pl.pallas_call(
        functools.partial(image_kernel, (leaf, each, half, beams, levels)),
        grid=(count,),
        in_specs=[
            SCALARS,
            in_spec,
            in_spec,
            pl.BlockSpec(steer.shape, lambda n: (0, 0)),
            pl.BlockSpec(interp.shape, lambda n: (0, 0, 0)),
            pl.BlockSpec((1,) + base.shape[1:], lambda n: (n, 0, 0)),
            pl.BlockSpec(step.shape, lambda n: (0, 0, 0, 0)),
        ],
        out_specs=[out_spec, out_spec],
        out_shape=[
            jax.ShapeDtypeStruct(shape, jnp.float32),
            jax.ShapeDtypeStruct(shape, jnp.bfloat16),
        ],
        compiler_params=pltpu.CompilerParams(vmem_limit_bytes=16 * 2**20),
        cost_estimate=pl.CostEstimate(
            flops=12 * beams * pulses * keep.shape[0] * each * width,
            bytes_accessed=4 * keep.size + 6 * shape[0] * count * each * rows * width,
            transcendentals=0,
        ),
        name="image",
    )(own, keep, got, steer, interp, base, step)


def fold(own, keep, got):
    def half(at):
        kept, came = (lax.dynamic_index_in_dim(a, at, 1, False) for a in (keep, got))
        return kept + came.astype(jnp.float32)

    return half(own), half(1 - own).astype(jnp.bfloat16)


def last_kernel(keep_y, got_y, keep_z, got_z, out_ref, rows_ref):
    each, rows, width = keep_y.shape
    blocks = 2 * each
    for n, (keep, got) in enumerate(((keep_y, got_y), (keep_z, got_z))):
        for i in range(each):
            value = keep[i] + got[i].astype(jnp.float32)
            for c in range(2):
                cols = slice(c * width // 2, (c + 1) * width // 2)
                rows_ref[c, pl.ds(n * each + i, rows, stride=blocks), :] = value[:, cols]
    both = jnp.concatenate([rows_ref[0], rows_ref[1]], axis=1)
    out_ref[...] = both.reshape(rows, blocks, width).astype(jnp.bfloat16)


def last_sum(keep_y, got_y, keep_z, got_z):
    each, rows, width = keep_y.shape
    return pl.pallas_call(
        last_kernel,
        out_shape=jax.ShapeDtypeStruct((rows, 2 * each, width), jnp.bfloat16),
        scratch_shapes=[pltpu.VMEM((2, rows * 2 * each, width // 2), jnp.float32)],
        compiler_params=pltpu.CompilerParams(vmem_limit_bytes=8 * 2**20),
        name="last_sum",
    )(keep_y, got_y, keep_z, got_z)


def interpolation(taps, beams):
    cells = jnp.arange(beams, dtype=jnp.int32)
    weights = jnp.array(WEIGHTS, jnp.float32)
    picks = taps[..., None] == cells
    return jnp.where(picks, weights[:, None], 0.0).sum(axis=-2)


def steering(slots, matrix, side, beams, pulses, scale):
    count = slots.shape[0]
    beam = jnp.arange(beams, dtype=jnp.int32)[:, None, None]
    place = jnp.arange(pulses, dtype=jnp.int32)
    slot = slots[None, :, None]
    cos, sin = unit(
        (2 * beam + 1 - beams) * (2 * place + 1 - pulses)
        + 3 * (beam + 1) * (2 * slot + 1) * (2 * place + 1),
        8 * pulses,
    )
    pair = jnp.concatenate([cos * scale, sin * scale], axis=2).astype(jnp.bfloat16)
    moved = jnp.dot(
        matrix.astype(jnp.bfloat16),
        pair.reshape(beams, count * 2 * pulses),
        preferred_element_type=jnp.float32,
    ).reshape(beams, count, 2 * pulses)
    re, im = moved[:, :, :pulses], moved[:, :, pulses:]
    row = jnp.arange(beams, dtype=jnp.int32)
    c, s = (t[:, None, None] for t in unit(row * row * (side + 1), PERIOD))
    re, im = c * re - s * im, c * im + s * re
    top = jnp.concatenate([re, -im], axis=2)
    low = jnp.concatenate([im, re], axis=2)
    return jnp.concatenate([top, low], axis=0).astype(jnp.bfloat16)


def bit(value, at):
    return value >> at & 1


def per_device(echoes, chirp, taps, slots):
    leaf, turn = lax.axis_size("leaf"), lax.axis_size("turn")
    pulses, blocks, width = echoes.shape
    half = width // 2
    beams = taps.shape[2]
    levels = bits_of(leaf)
    far = (bits_of(turn) + 1) // 2 - 1 if turn > 4 else 1
    mids = 1 << far - 1
    high = turn >> far + 1
    each = blocks // (2 * turn)
    rows = beams // leaf
    own_leaf, own_turn = lax.axis_index("leaf"), lax.axis_index("turn")

    def scalar(value):
        return jnp.asarray(value, jnp.int32).reshape(1)

    own_bits = jnp.concatenate([scalar(bit(own_turn, 0)), scalar(bit(own_turn, far))])
    keep_y, send_y, keep_z, send_z = compress(own_bits, chirp, echoes, high, mids)
    got_y = swapped(send_y, "turn", 0)
    got_z = swapped(send_z, "turn", far)

    own_sides = [bit(own_leaf, level) for level in range(levels)]
    own_taps = jnp.stack(
        [lax.dynamic_index_in_dim(taps[n], own_sides[n], 0, False) for n in range(levels)]
    )
    matrices = interpolation(own_taps, beams)
    scale = 1.0 / math.sqrt(2.0 * slots.shape[1] * pulses)
    own_slots = jnp.concatenate(
        [
            lax.dynamic_index_in_dim(slots[0], own_turn ^ other, 0, True)
            for other in (0, 1, 1 << far)
        ]
    )
    steer = steering(own_slots, matrices[0], own_sides[0], beams, pulses, scale)
    steer_y = steer[:, :2].reshape(2 * beams, 4 * pulses)
    steer_z = jnp.concatenate([steer[:, :1], steer[:, 2:]], axis=1).reshape(2 * beams, 4 * pulses)
    interp = jnp.concatenate([matrices[1:]] * 2, axis=-1).astype(jnp.bfloat16)

    row = jnp.arange(beams, dtype=jnp.int32)
    lean = 2 * row + 1 - beams
    place = jnp.arange(each * half, dtype=jnp.int32) + 1
    slopes = jnp.stack([(2 * own_sides[n] - 1) * (n + 2) for n in range(levels)])
    step = jnp.stack(unit(slopes[:, None, None] * lean[:, None] * place, PERIOD), axis=1)
    squares = jnp.stack(
        [row * row * (own_sides[n] + 1) * (1 if n else 0) for n in range(levels)]
    )

    def bases(tiles, shift):
        start = ((tiles * 2 + shift) * each * half)[:, None, None]
        both = jnp.stack(unit(slopes[:, None] * lean * start + squares, PERIOD), axis=2)
        return both.reshape(tiles.shape[0], 2 * levels, beams)

    count = turn // 2
    index = jnp.arange(count, dtype=jnp.int32)
    tiles_y = 2 * index + bit(own_turn, 0)
    low_part = index & (1 << far) - 1
    tiles_z = ((index >> far) * 2 + bit(own_turn, far)) * (1 << far) + low_part

    own_core = scalar(bit(own_leaf, 0))
    final = []
    for name, keep, got, steer_own, tiles in (
        ("y", keep_y, got_y, steer_y, tiles_y),
        ("z", keep_z, got_z, steer_z, tiles_z),
    ):
        shape = (count, each, pulses, width)
        base = bases(tiles, 0 if name == "y" else 1)
        kept, sent = backproject(
            own_core, keep.reshape(shape), got.reshape(shape), steer_own, interp, base, step, leaf
        )
        gone = 0 if name == "y" else far
        leading = [("leaf", b) for b in range(levels - 1, 0, -1)]
        leading += [("turn", b) for b in range(bits_of(turn) - 1, -1, -1) if b != gone]
        order = [("leaf", b) for b in range(1, levels)]
        rest = [("turn", b) for b in range(bits_of(turn)) if b not in (0, far)]
        order = order + [("turn", far)] if name == "y" else [("turn", 0)] + order
        arrived = swapped(sent, "leaf", 0)
        for axis, b in order + rest:
            at = leading.index((axis, b))
            before, after = 1 << at, (1 << len(leading) - at - 1) * each
            leading.pop(at)
            split = (before, 2, after, rows, width)
            own = bit(own_leaf if axis == "leaf" else own_turn, b)
            kept, sent = fold(own, kept.reshape(split), arrived.reshape(split))
            arrived = swapped(sent, axis, b)
        final += [kept.reshape(each, rows, width), arrived.reshape(each, rows, width)]
    return last_sum(*final)


def solution(mesh):
    placed = (P(("leaf", "turn"), None, None), P(), P(), P("leaf", None))
    return jax.shard_map(
        per_device, mesh=mesh, in_specs=placed, out_specs=P("leaf", "turn", None), check_vma=False
    )
```

```python
import functools
import math

import jax
import jax.numpy as jnp
from jax import lax
from jax.experimental import pallas as pl
from jax.experimental.pallas import tpu as pltpu
from jax.sharding import PartitionSpec as P

WEIGHTS = (-1.0 / 32, 3.0 / 32, -7.0 / 32, 21.0 / 32, 21.0 / 32, -7.0 / 32, 3.0 / 32, -1.0 / 32)
PERIOD = 4096
VMEM_BYTES = 56 * 2**20


def bits_of(count):
    return count.bit_length() - 1


def swapped(array, axis, bit):
    return lax.ppermute(array, axis, [(i, i ^ 1 << bit) for i in range(lax.axis_size(axis))])


def unit(phase_int, period):
    angle = jnp.remainder(phase_int, period).astype(jnp.float32) * (2.0 * math.pi / period)
    return jnp.cos(angle), jnp.sin(angle)


def own_bit(axis, at):
    return lax.axis_index(axis) >> at & 1


def compress_kernel(
    dims, chirp_ref, edge_ref, echo_ref, keep_ref, send_ref, edge_out, weights, rows_ref, carry
):
    tile, pulses, half, near_chain, axis_bit = dims
    blocks = 2 * tile
    pitch = blocks + 1
    mid = pl.num_programs(2) - 1 - pl.program_id(2)
    near = 1 - pl.program_id(1)
    own = own_bit("turn", axis_bit)

    @pl.when((pl.program_id(0) == 0) & (pl.program_id(1) == 0) & (pl.program_id(2) == 0))
    def _():
        rows = lax.broadcasted_iota(jnp.int32, (half, half), 0)
        cols = lax.broadcasted_iota(jnp.int32, (half, half), 1)
        taps = chirp_ref[...].astype(jnp.float32)
        tables = []
        for c in range(2):
            wide = jnp.broadcast_to(taps[c : c + 1], (half, half))
            tables.append(pltpu.roll(wide, 0, 1, stride=1, stride_axis=0).T)
        for m, mask in enumerate((rows >= cols, rows < cols)):
            re, im = (jnp.where(mask, t, 0.0) for t in tables)
            top = jnp.concatenate([re, im], axis=1)
            low = jnp.concatenate([-im, re], axis=1)
            full = jnp.concatenate([top, low], axis=0)
            weights[m * 2 * half : (m + 1) * 2 * half, :] = full.astype(jnp.bfloat16)
        carry[...] = edge_ref[...]

    for p in range(pulses):
        for c in range(2):
            rows_ref[c, p * pitch : p * pitch + blocks, :] = echo_ref[
                p, :, c * half : (c + 1) * half
            ].astype(jnp.float32)
    turned = []
    for b in range(blocks):
        parts = [rows_ref[c, pl.ds(b, pulses, stride=pitch), :] for c in range(2)]
        turned.append(jnp.concatenate(parts, axis=1).astype(jnp.bfloat16))
    turned.append(carry[...])
    current = jnp.concatenate(turned[:-1], axis=0)
    after = jnp.concatenate(turned[1:], axis=0)
    total = jnp.dot(
        jnp.concatenate([current, after], axis=1),
        weights[...],
        preferred_element_type=jnp.float32,
    ).astype(jnp.bfloat16)
    carry[...] = turned[0]
    edge_out[...] = turned[0]

    if near_chain:
        for side in range(2):

            @pl.when(own == side)
            def _(side=side):
                for b in range(blocks):
                    ref = keep_ref if b // tile == side else send_ref
                    ref[0, 0, 0, b % tile] = total[b * pulses : (b + 1) * pulses]
    else:
        for ref, mine in ((keep_ref, True), (send_ref, False)):

            @pl.when((near == own) == mine)
            def _(ref=ref):
                for b in range(blocks):
                    ref[0, mid, b // tile, b % tile] = total[b * pulses : (b + 1) * pulses]


def compress(chirp, edge, echoes, high, mids, near_chain, axis_bit, first_high):
    pulses, blocks, width = echoes.shape
    half = width // 2
    tile = blocks // lax.axis_size("turn")
    if near_chain:
        shape = (high, 2, mids, tile, pulses, width)
        spec = pl.BlockSpec(
            (1, 1, 1) + shape[3:], lambda h, v, m: (high - 1 - h, 1 - v, mids - 1 - m, 0, 0, 0)
        )
    else:
        shape = (high, mids, 2, tile, pulses, width)
        spec = pl.BlockSpec((1,) + shape[1:], lambda h, v, m: (high - 1 - h, 0, 0, 0, 0, 0))
    edge_spec = pl.BlockSpec((pulses, width), lambda h, v, m: (0, 0))

    def chunk(h, v, m):
        return 0, ((first_high + high - 1 - h) * 2 + 1 - v) * mids + mids - 1 - m, 0

    return pl.pallas_call(
        functools.partial(compress_kernel, (tile, pulses, half, near_chain, axis_bit)),
        grid=(high, 2, mids),
        in_specs=[
            pl.BlockSpec((2, half), lambda h, v, m: (0, 0)),
            edge_spec,
            pl.BlockSpec((pulses, 2 * tile, width), chunk),
        ],
        out_specs=[spec, spec, edge_spec],
        out_shape=[
            jax.ShapeDtypeStruct(s, jnp.bfloat16) for s in (shape, shape, (pulses, width))
        ],
        scratch_shapes=[
            pltpu.VMEM((2 * width, width), jnp.bfloat16),
            pltpu.VMEM((2, pulses * (2 * tile + 1), half), jnp.float32),
            pltpu.VMEM((pulses, width), jnp.bfloat16),
        ],
        compiler_params=pltpu.CompilerParams(vmem_limit_bytes=VMEM_BYTES),
        cost_estimate=pl.CostEstimate(
            flops=2 * pulses * blocks * width * width,
            bytes_accessed=2 * pulses * blocks * width,
            transcendentals=0,
        ),
        name="compress",
    )(chirp, edge, echoes)


def image_kernel(dims, data_ref, steer_ref, interp_ref, base_ref, step_ref, out_keep, out_send):
    leaf, each, half, beams, levels = dims
    rows = beams // leaf
    pair = 2
    piece = rows

    def turned(phase, re, im):
        c, s = phase
        return c * re - s * im, c * im + s * re

    bases = []
    for n in range(2 * levels):
        bases.append(jnp.broadcast_to(base_ref[0, n : n + 1, :], (half, beams)).T)

    def phased(level, block, first, re, im):
        cut = slice(first, first + piece)
        lanes = slice(block * half, (block + 1) * half)
        phase = turned(
            (bases[2 * level][cut], bases[2 * level + 1][cut]),
            step_ref[level, 0, cut, lanes],
            step_ref[level, 1, cut, lanes],
        )
        return turned(phase, re, im)

    for at in range(0, each, pair):
        parts = []
        for n in range(2):
            for c in range(2):
                cols = slice(c * half, (c + 1) * half)
                parts.append(
                    jnp.concatenate([data_ref[n, 0, at + i, :, cols] for i in range(pair)], axis=1)
                )
        raw = jnp.dot(
            steer_ref[...], jnp.concatenate(parts, axis=0), preferred_element_type=jnp.float32
        )
        re, im = raw[:beams], raw[beams:]
        for level in range(levels):
            columns = []
            for i in range(pair):
                lanes = slice(i * half, (i + 1) * half)
                pieces = []
                for first in range(0, beams, piece):
                    cut = slice(first, first + piece)
                    both = phased(level, at + i, first, re[cut, lanes], im[cut, lanes])
                    if level == levels - 1:
                        both = jnp.concatenate(both, axis=1)
                        g = first // rows
                        if g < leaf // 2:
                            out_keep[g, 0, at + i] = both
                        else:
                            out_send[g - leaf // 2, 0, at + i] = both.astype(jnp.bfloat16)
                        continue
                    both = jnp.concatenate(both, axis=1)
                    big = both.astype(jnp.bfloat16)
                    low = (both - big.astype(jnp.float32)).astype(jnp.bfloat16)
                    pieces.append((big, low))
                if pieces:
                    columns.append(
                        jnp.concatenate([p[0] for p in pieces] + [p[1] for p in pieces], axis=0)
                    )
            if columns:
                moved = jnp.dot(
                    interp_ref[level],
                    jnp.concatenate(columns, axis=1),
                    preferred_element_type=jnp.float32,
                )
                cuts = [moved[:, n * half : (n + 1) * half] for n in range(2 * pair)]
                re = jnp.concatenate(cuts[0::2], axis=1)
                im = jnp.concatenate(cuts[1::2], axis=1)


def backproject(data, steer, interp, base, step, leaf):
    _, count, each, pulses, width = data.shape
    half = width // 2
    beams = steer.shape[0] // 2
    rows = beams // leaf
    shape = (leaf // 2, count, each, rows, width)
    out_spec = pl.BlockSpec((leaf // 2, 1) + shape[2:], lambda n: (0, n, 0, 0, 0))
    return pl.pallas_call(
        functools.partial(image_kernel, (leaf, each, half, beams, bits_of(leaf))),
        grid=(count,),
        in_specs=[
            pl.BlockSpec((2, 1, each, pulses, width), lambda n: (0, n, 0, 0, 0)),
            pl.BlockSpec(steer.shape, lambda n: (0, 0)),
            pl.BlockSpec(interp.shape, lambda n: (0, 0, 0)),
            pl.BlockSpec((1,) + base.shape[1:], lambda n: (n, 0, 0)),
            pl.BlockSpec(step.shape, lambda n: (0, 0, 0, 0)),
        ],
        out_specs=[out_spec, out_spec],
        out_shape=[
            jax.ShapeDtypeStruct(shape, jnp.float32),
            jax.ShapeDtypeStruct(shape, jnp.bfloat16),
        ],
        compiler_params=pltpu.CompilerParams(vmem_limit_bytes=16 * 2**20),
        cost_estimate=pl.CostEstimate(
            flops=12 * beams * pulses * count * each * width,
            bytes_accessed=2 * data.size + 6 * count * each * beams * width // 2,
            transcendentals=0,
        ),
        name="image",
    )(data, steer, interp, base, step)


def fold(own, keep, got):
    def half(at):
        kept, came = (lax.dynamic_index_in_dim(a, at, 1, False) for a in (keep, got))
        return kept + came.astype(jnp.float32)

    return half(own), half(1 - own).astype(jnp.bfloat16)


def last_kernel(keep_ref, got_ref, out_ref, rows_ref):
    blocks, rows, width = keep_ref.shape
    for i in range(blocks):
        value = keep_ref[i] + got_ref[i].astype(jnp.float32)
        for c in range(2):
            cols = slice(c * width // 2, (c + 1) * width // 2)
            rows_ref[c, pl.ds(i, rows, stride=blocks), :] = value[:, cols]
    both = jnp.concatenate([rows_ref[0], rows_ref[1]], axis=1)
    out_ref[...] = both.reshape(rows, blocks, width).astype(jnp.bfloat16)


def last_sum(keep, got):
    blocks, rows, width = keep.shape
    return pl.pallas_call(
        last_kernel,
        out_shape=jax.ShapeDtypeStruct((rows, blocks, width), jnp.bfloat16),
        scratch_shapes=[pltpu.VMEM((2, rows * blocks, width // 2), jnp.float32)],
        compiler_params=pltpu.CompilerParams(vmem_limit_bytes=8 * 2**20),
        name="last_sum",
    )(keep, got)


def interpolation(taps, beams):
    cells = jnp.arange(beams, dtype=jnp.int32)
    weights = jnp.array(WEIGHTS, jnp.float32)
    picks = taps[..., None] == cells
    return jnp.where(picks, weights[:, None], 0.0).sum(axis=-2)


def steering(slots, matrix, side, beams, pulses, scale):
    count = slots.shape[0]
    beam = jnp.arange(beams, dtype=jnp.int32)[:, None, None]
    place = jnp.arange(pulses, dtype=jnp.int32)
    slot = slots[None, :, None]
    cos, sin = unit(
        (2 * beam + 1 - beams) * (2 * place + 1 - pulses)
        + 3 * (beam + 1) * (2 * slot + 1) * (2 * place + 1),
        8 * pulses,
    )
    pair = jnp.concatenate([cos * scale, sin * scale], axis=2).astype(jnp.bfloat16)
    moved = jnp.dot(
        matrix.astype(jnp.bfloat16),
        pair.reshape(beams, count * 2 * pulses),
        preferred_element_type=jnp.float32,
    ).reshape(beams, count, 2 * pulses)
    re, im = moved[:, :, :pulses], moved[:, :, pulses:]
    row = jnp.arange(beams, dtype=jnp.int32)
    c, s = (t[:, None, None] for t in unit(row * row * (side + 1), PERIOD))
    re, im = c * re - s * im, c * im + s * re
    top = jnp.concatenate([re, -im], axis=2)
    low = jnp.concatenate([im, re], axis=2)
    return jnp.concatenate([top, low], axis=0).astype(jnp.bfloat16)


def bit(value, at):
    return value >> at & 1


def per_device(echoes, chirp, taps, slots):
    leaf, turn = lax.axis_size("leaf"), lax.axis_size("turn")
    pulses, blocks, width = echoes.shape
    half = width // 2
    beams = taps.shape[2]
    levels = bits_of(leaf)
    far = (bits_of(turn) + 1) // 2 - 1
    top = bits_of(turn) - 1
    mids = 1 << far - 1
    high = turn >> far + 2
    tile = blocks // turn
    each = tile // 2
    rows = beams // leaf
    own_leaf, own_turn = lax.axis_index("leaf"), lax.axis_index("turn")

    edge = jnp.zeros((pulses, width), jnp.bfloat16)
    keep_y, send_y, edge = compress(chirp, edge, echoes, high, mids, True, 0, high)
    got_y = swapped(send_y, "turn", 0)
    keep_z, send_z, _ = compress(chirp, edge, echoes, high, mids, False, far, 0)
    got_z = swapped(send_z, "turn", far)

    own_sides = [bit(own_leaf, level) for level in range(levels)]
    row = jnp.arange(beams, dtype=jnp.int32)
    part, place = row // rows, row % rows
    group = 2 * (part % (leaf // 2)) + (part // (leaf // 2) ^ own_sides[0])
    orders = [row] * (levels - 1) + [group * rows + place]
    own_taps = [
        lax.dynamic_index_in_dim(taps[n], own_sides[n], 0, False) for n in range(levels)
    ]
    cores = own_taps[-1].reshape(leaf // 2, 2, rows, -1)
    cores = [
        lax.dynamic_index_in_dim(cores, own_sides[0] ^ n, 1, False).reshape(beams // 2, -1)
        for n in range(2)
    ]
    own_taps[-1] = jnp.concatenate(cores, axis=0)
    matrices = interpolation(jnp.stack(own_taps), beams)
    interp = jnp.concatenate([matrices[1:]] * 2, axis=-1).astype(jnp.bfloat16)
    scale = 1.0 / math.sqrt(2.0 * slots.shape[1] * pulses)
    wanted = own_turn ^ jnp.array([0, 1, 1 << far], jnp.int32)
    picked = jnp.arange(slots.shape[1], dtype=jnp.int32) == wanted[:, None]
    own_slots = jnp.where(picked, slots, 0).sum(axis=1)
    steer = steering(own_slots, matrices[0], own_sides[0], beams, pulses, scale)
    steer_y = steer[:, :2].reshape(2 * beams, 4 * pulses)
    steer_z = jnp.concatenate([steer[:, :1], steer[:, 2:]], axis=1).reshape(2 * beams, 4 * pulses)

    leans = jnp.stack([2 * order + 1 - beams for order in orders])
    bins = jnp.arange(each * half, dtype=jnp.int32) + 1
    slopes = jnp.stack([(2 * own_sides[n] - 1) * (n + 2) for n in range(levels)])[:, None] * leans
    step = jnp.stack(unit(slopes[:, :, None] * bins, PERIOD), axis=1)
    squares = jnp.stack(
        [orders[n] * orders[n] * (own_sides[n] + 1) * (1 if n else 0) for n in range(levels)]
    )

    def bases(tiles):
        parts = (2 * tiles[:, None] + jnp.arange(2, dtype=jnp.int32)).reshape(-1)
        start = (parts * each * half)[:, None, None]
        both = jnp.stack(unit(slopes * start + squares, PERIOD), axis=2)
        return both.reshape(parts.shape[0], 2 * levels, beams)

    index = jnp.arange(turn // 4, dtype=jnp.int32)
    tiles_y = turn // 2 + 2 * index + bit(own_turn, 0)
    low_part = index & (1 << far) - 1
    tiles_z = ((index >> far) * 2 + bit(own_turn, far)) * (1 << far) + low_part

    final = []
    for name, keep, got, steer_own, tiles in (
        ("y", keep_y, got_y, steer_y, tiles_y),
        ("z", keep_z, got_z, steer_z, tiles_z),
    ):
        shape = (turn // 2, each, pulses, width)
        data = jnp.stack([keep.reshape(shape), got.reshape(shape)])
        kept, sent = backproject(data, steer_own, interp, bases(tiles), step, leaf)
        gone = 0 if name == "y" else far
        leading = [("leaf", b) for b in range(levels - 1, 0, -1)]
        leading += [("turn", b) for b in range(top - 1, -1, -1) if b != gone]
        order = [("leaf", b) for b in range(1, levels)]
        rest = [("turn", b) for b in range(top) if b not in (0, far)]
        order = order + [("turn", far)] if name == "y" else [("turn", 0)] + order
        arrived = swapped(sent, "leaf", 0)
        for axis, b in order + rest:
            at = leading.index((axis, b))
            before, after = 1 << at, (1 << len(leading) - at - 1) * tile
            leading.pop(at)
            split = (before, 2, after, rows, width)
            own = bit(own_leaf if axis == "leaf" else own_turn, b)
            kept, sent = fold(own, kept.reshape(split), arrived.reshape(split))
            arrived = swapped(sent, axis, b)
        shape = (tile, rows, width)
        final.append(kept.reshape(shape) + arrived.reshape(shape).astype(jnp.float32))
    upper = bit(own_turn, top) == 1
    kept = jnp.where(upper, final[0], final[1])
    sent = jnp.where(upper, final[1], final[0]).astype(jnp.bfloat16)
    return last_sum(kept, swapped(sent, "turn", top))


def solution(mesh):
    placed = (P(("leaf", "turn"), None, None), P(), P(), P("leaf", None))
    return jax.shard_map(
        per_device, mesh=mesh, in_specs=placed, out_specs=P("leaf", "turn", None), check_vma=False
    )
```

```python
import functools
import math

import jax
import jax.numpy as jnp
from jax import lax
from jax.experimental import pallas as pl
from jax.experimental.pallas import tpu as pltpu
from jax.sharding import PartitionSpec as P

WEIGHTS = (-1.0 / 32, 3.0 / 32, -7.0 / 32, 21.0 / 32, 21.0 / 32, -7.0 / 32, 3.0 / 32, -1.0 / 32)
PERIOD = 4096
VMEM_BYTES = 56 * 2**20


def bits_of(count):
    return count.bit_length() - 1


def swapped(array, axis, bit):
    return lax.ppermute(array, axis, [(i, i ^ 1 << bit) for i in range(lax.axis_size(axis))])


def unit(phase_int, period):
    angle = jnp.remainder(phase_int, period).astype(jnp.float32) * (2.0 * math.pi / period)
    return jnp.cos(angle), jnp.sin(angle)


def own_bit(axis, at):
    return lax.axis_index(axis) >> at & 1


def compress_kernel(dims, has_edge, chirp_ref, echo_ref, *refs):
    edge_ref, refs = (refs[0], refs[1:]) if has_edge else (None, refs)
    keep_ref, send_ref, edge_out, weights, rows_ref, carry = refs
    tile, pulses, half, near_chain, axis_bit = dims
    blocks = 2 * tile
    pitch = blocks + 1
    mid = pl.num_programs(2) - 1 - pl.program_id(2)
    near = 1 - pl.program_id(1)
    own = own_bit("turn", axis_bit)

    set_of_pulses = pl.program_id(3)
    start = (pl.program_id(0) == 0) & (pl.program_id(1) == 0) & (pl.program_id(2) == 0)

    @pl.when(start)
    def _():
        carry[set_of_pulses] = edge_ref[...] if has_edge else jnp.zeros_like(carry[0])

    @pl.when(start & (set_of_pulses == 0))
    def _():
        rows = lax.broadcasted_iota(jnp.int32, (half, half), 0)
        cols = lax.broadcasted_iota(jnp.int32, (half, half), 1)
        taps = chirp_ref[...].astype(jnp.float32)
        tables = []
        for c in range(2):
            wide = jnp.broadcast_to(taps[c : c + 1], (half, half))
            tables.append(pltpu.roll(wide, 0, 1, stride=1, stride_axis=0).T)
        for m, mask in enumerate((rows >= cols, rows < cols)):
            re, im = (jnp.where(mask, t, 0.0) for t in tables)
            top = jnp.concatenate([re, im], axis=1)
            low = jnp.concatenate([-im, re], axis=1)
            full = jnp.concatenate([top, low], axis=0)
            weights[m * 2 * half : (m + 1) * 2 * half, :] = full.astype(jnp.bfloat16)

    for p in range(pulses):
        for c in range(2):
            rows_ref[c, p * pitch : p * pitch + blocks, :] = echo_ref[
                p, :, c * half : (c + 1) * half
            ].astype(jnp.float32)
    turned = []
    for b in range(blocks):
        parts = [rows_ref[c, pl.ds(b, pulses, stride=pitch), :] for c in range(2)]
        turned.append(jnp.concatenate(parts, axis=1).astype(jnp.bfloat16))
    turned.append(carry[set_of_pulses])
    current = jnp.concatenate(turned[:-1], axis=0)
    after = jnp.concatenate(turned[1:], axis=0)
    total = jnp.dot(
        jnp.concatenate([current, after], axis=1),
        weights[...],
        preferred_element_type=jnp.float32,
    ).astype(jnp.bfloat16)
    carry[set_of_pulses] = turned[0]
    edge_out[...] = turned[0]

    if near_chain:
        for side in range(2):

            @pl.when(own == side)
            def _(side=side):
                for b in range(blocks):
                    ref = keep_ref if b // tile == side else send_ref
                    ref[0, 0, 0, b % tile] = total[b * pulses : (b + 1) * pulses]
    else:
        for ref, mine in ((keep_ref, True), (send_ref, False)):

            @pl.when((near == own) == mine)
            def _(ref=ref):
                for b in range(blocks):
                    span = pl.ds(pl.multiple_of(set_of_pulses * pulses, pulses), pulses)
                    ref[0, mid, b // tile, b % tile, span] = total[b * pulses : (b + 1) * pulses]


def compress(chirp, edge, echoes, high, mids, near_chain, axis_bit, first_high):
    pulses, blocks, width = echoes.shape
    half = width // 2
    tile = blocks // lax.axis_size("turn")
    cuts = 2
    some = pulses // cuts
    if near_chain:
        shape = (high, 2, mids, tile, pulses, width)
        spec = pl.BlockSpec(
            (1, 1, 1, tile, some, width),
            lambda h, v, m, p: (high - 1 - h, 1 - v, mids - 1 - m, 0, p, 0),
        )
    else:
        shape = (high, mids, 2, tile, pulses, width)
        spec = pl.BlockSpec(
            (1, mids, 2, tile, pulses, width), lambda h, v, m, p: (high - 1 - h, 0, 0, 0, 0, 0)
        )
    edge_spec = pl.BlockSpec((some, width), lambda h, v, m, p: (p, 0))

    def chunk(h, v, m, p):
        return p, ((first_high + high - 1 - h) * 2 + 1 - v) * mids + mids - 1 - m, 0

    in_specs = [
        pl.BlockSpec((2, half), lambda h, v, m, p: (0, 0)),
        pl.BlockSpec((some, 2 * tile, width), chunk),
    ]
    operands = [chirp, echoes]
    if edge is not None:
        in_specs.append(edge_spec)
        operands.append(edge)
    dims = (tile, some, half, near_chain, axis_bit)
    return pl.pallas_call(
        functools.partial(compress_kernel, dims, edge is not None),
        grid=(high, 2, mids, cuts),
        in_specs=in_specs,
        out_specs=[spec, spec, edge_spec],
        out_shape=[
            jax.ShapeDtypeStruct(s, jnp.bfloat16) for s in (shape, shape, (pulses, width))
        ],
        scratch_shapes=[
            pltpu.VMEM((2 * width, width), jnp.bfloat16),
            pltpu.VMEM((2, some * (2 * tile + 1), half), jnp.float32),
            pltpu.VMEM((cuts, some, width), jnp.bfloat16),
        ],
        compiler_params=pltpu.CompilerParams(vmem_limit_bytes=VMEM_BYTES),
        cost_estimate=pl.CostEstimate(
            flops=2 * pulses * blocks * width * width,
            bytes_accessed=2 * pulses * blocks * width,
            transcendentals=0,
        ),
        name="compress",
    )(*operands)


def image_kernel(dims, data_ref, steer_ref, interp_ref, base_ref, step_ref, out_keep, out_send):
    leaf, each, half, beams, levels = dims
    rows = beams // leaf
    pair = 2
    piece = rows

    def turned(phase, re, im):
        c, s = phase
        return c * re - s * im, c * im + s * re

    bases = []
    for n in range(2 * levels):
        bases.append(jnp.broadcast_to(base_ref[0, n : n + 1, :], (half, beams)).T)

    def phased(level, block, first, re, im):
        cut = slice(first, first + piece)
        lanes = slice(block * half, (block + 1) * half)
        phase = turned(
            (bases[2 * level][cut], bases[2 * level + 1][cut]),
            step_ref[level, 0, cut, lanes],
            step_ref[level, 1, cut, lanes],
        )
        return turned(phase, re, im)

    for at in range(0, each, pair):
        parts = []
        for n in range(2):
            for c in range(2):
                cols = slice(c * half, (c + 1) * half)
                parts.append(
                    jnp.concatenate([data_ref[n, 0, at + i, :, cols] for i in range(pair)], axis=1)
                )
        raw = jnp.dot(
            steer_ref[...], jnp.concatenate(parts, axis=0), preferred_element_type=jnp.float32
        )
        re, im = raw[:beams], raw[beams:]
        for level in range(levels):
            columns = []
            for i in range(pair):
                lanes = slice(i * half, (i + 1) * half)
                pieces = []
                for first in range(0, beams, piece):
                    cut = slice(first, first + piece)
                    both = phased(level, at + i, first, re[cut, lanes], im[cut, lanes])
                    if level == levels - 1:
                        both = jnp.concatenate(both, axis=1)
                        g = first // rows
                        if g < leaf // 2:
                            out_keep[g, 0, at + i] = both
                        else:
                            out_send[g - leaf // 2, 0, at + i] = both.astype(jnp.bfloat16)
                        continue
                    both = jnp.concatenate(both, axis=1)
                    big = both.astype(jnp.bfloat16)
                    low = (both - big.astype(jnp.float32)).astype(jnp.bfloat16)
                    pieces.append((big, low))
                if pieces:
                    columns.append(
                        jnp.concatenate([p[0] for p in pieces] + [p[1] for p in pieces], axis=0)
                    )
            if columns:
                moved = jnp.dot(
                    interp_ref[level],
                    jnp.concatenate(columns, axis=1),
                    preferred_element_type=jnp.float32,
                )
                cuts = [moved[:, n * half : (n + 1) * half] for n in range(2 * pair)]
                re = jnp.concatenate(cuts[0::2], axis=1)
                im = jnp.concatenate(cuts[1::2], axis=1)


def backproject(data, steer, interp, base, step, leaf):
    _, count, each, pulses, width = data.shape
    half = width // 2
    beams = steer.shape[0] // 2
    rows = beams // leaf
    shape = (leaf // 2, count, each, rows, width)
    out_spec = pl.BlockSpec((leaf // 2, 1) + shape[2:], lambda n: (0, n, 0, 0, 0))
    return pl.pallas_call(
        functools.partial(image_kernel, (leaf, each, half, beams, bits_of(leaf))),
        grid=(count,),
        in_specs=[
            pl.BlockSpec((2, 1, each, pulses, width), lambda n: (0, n, 0, 0, 0)),
            pl.BlockSpec(steer.shape, lambda n: (0, 0)),
            pl.BlockSpec(interp.shape, lambda n: (0, 0, 0)),
            pl.BlockSpec((1,) + base.shape[1:], lambda n: (n, 0, 0)),
            pl.BlockSpec(step.shape, lambda n: (0, 0, 0, 0)),
        ],
        out_specs=[out_spec, out_spec],
        out_shape=[
            jax.ShapeDtypeStruct(shape, jnp.float32),
            jax.ShapeDtypeStruct(shape, jnp.bfloat16),
        ],
        compiler_params=pltpu.CompilerParams(vmem_limit_bytes=16 * 2**20),
        cost_estimate=pl.CostEstimate(
            flops=12 * beams * pulses * count * each * width,
            bytes_accessed=2 * data.size + 6 * count * each * beams * width // 2,
            transcendentals=0,
        ),
        name="image",
    )(data, steer, interp, base, step)


def total_of(terms):
    total = terms[0]
    for term in terms[1:]:
        total = total + term.astype(jnp.float32)
    return total


def fold(own, terms, split):
    def half(at):
        return [lax.dynamic_index_in_dim(t.reshape(split), at, 1, False) for t in terms]

    return half(own), total_of(half(1 - own)).astype(jnp.bfloat16)


def last_kernel(keep_ref, got_ref, out_ref, rows_ref):
    blocks, rows, width = keep_ref.shape
    for i in range(blocks):
        value = keep_ref[i] + got_ref[i].astype(jnp.float32)
        for c in range(2):
            cols = slice(c * width // 2, (c + 1) * width // 2)
            rows_ref[c, pl.ds(i, rows, stride=blocks), :] = value[:, cols]
    both = jnp.concatenate([rows_ref[0], rows_ref[1]], axis=1)
    out_ref[...] = both.reshape(rows, blocks, width).astype(jnp.bfloat16)


def last_sum(keep, got):
    blocks, rows, width = keep.shape
    return pl.pallas_call(
        last_kernel,
        out_shape=jax.ShapeDtypeStruct((rows, blocks, width), jnp.bfloat16),
        scratch_shapes=[pltpu.VMEM((2, rows * blocks, width // 2), jnp.float32)],
        compiler_params=pltpu.CompilerParams(vmem_limit_bytes=8 * 2**20),
        name="last_sum",
    )(keep, got)


def interpolation(taps, beams):
    cells = jnp.arange(beams, dtype=jnp.int32)
    weights = jnp.array(WEIGHTS, jnp.float32)
    picks = taps[..., None] == cells
    return jnp.where(picks, weights[:, None], 0.0).sum(axis=-2)


def steering(slots, matrix, side, beams, pulses, scale):
    count = slots.shape[0]
    beam = jnp.arange(beams, dtype=jnp.int32)[:, None, None]
    place = jnp.arange(pulses, dtype=jnp.int32)
    slot = slots[None, :, None]
    cos, sin = unit(
        (2 * beam + 1 - beams) * (2 * place + 1 - pulses)
        + 3 * (beam + 1) * (2 * slot + 1) * (2 * place + 1),
        8 * pulses,
    )
    pair = jnp.concatenate([cos * scale, sin * scale], axis=2).astype(jnp.bfloat16)
    moved = jnp.dot(
        matrix.astype(jnp.bfloat16),
        pair.reshape(beams, count * 2 * pulses),
        preferred_element_type=jnp.float32,
    ).reshape(beams, count, 2 * pulses)
    re, im = moved[:, :, :pulses], moved[:, :, pulses:]
    row = jnp.arange(beams, dtype=jnp.int32)
    c, s = (t[:, None, None] for t in unit(row * row * (side + 1), PERIOD))
    re, im = c * re - s * im, c * im + s * re
    top = jnp.concatenate([re, -im], axis=2)
    low = jnp.concatenate([im, re], axis=2)
    return jnp.concatenate([top, low], axis=0).astype(jnp.bfloat16)


def bit(value, at):
    return value >> at & 1


def per_device(echoes, chirp, taps, slots):
    leaf, turn = lax.axis_size("leaf"), lax.axis_size("turn")
    pulses, blocks, width = echoes.shape
    half = width // 2
    beams = taps.shape[2]
    levels = bits_of(leaf)
    far = (bits_of(turn) + 1) // 2 - 1
    top = bits_of(turn) - 1
    mids = 1 << far - 1
    high = turn >> far + 2
    tile = blocks // turn
    each = tile // 2
    rows = beams // leaf
    own_leaf, own_turn = lax.axis_index("leaf"), lax.axis_index("turn")

    keep_y, send_y, edge = compress(chirp, None, echoes, high, mids, True, 0, high)
    got_y = swapped(send_y, "turn", 0)
    keep_z, send_z, _ = compress(chirp, edge, echoes, high, mids, False, far, 0)
    got_z = swapped(send_z, "turn", far)

    own_sides = [bit(own_leaf, level) for level in range(levels)]
    row = jnp.arange(beams, dtype=jnp.int32)
    part, place = row // rows, row % rows
    group = 2 * (part % (leaf // 2)) + (part // (leaf // 2) ^ own_sides[0])
    orders = [row] * (levels - 1) + [group * rows + place]
    own_taps = [
        lax.dynamic_index_in_dim(taps[n], own_sides[n], 0, False) for n in range(levels)
    ]
    cores = own_taps[-1].reshape(leaf // 2, 2, rows, -1)
    cores = [
        lax.dynamic_index_in_dim(cores, own_sides[0] ^ n, 1, False).reshape(beams // 2, -1)
        for n in range(2)
    ]
    own_taps[-1] = jnp.concatenate(cores, axis=0)
    matrices = interpolation(jnp.stack(own_taps), beams)
    interp = jnp.concatenate([matrices[1:]] * 2, axis=-1).astype(jnp.bfloat16)
    scale = 1.0 / math.sqrt(2.0 * slots.shape[1] * pulses)
    wanted = own_turn ^ jnp.array([0, 1, 1 << far], jnp.int32)
    picked = jnp.arange(slots.shape[1], dtype=jnp.int32) == wanted[:, None]
    own_slots = jnp.where(picked, slots, 0).sum(axis=1)
    steer = steering(own_slots, matrices[0], own_sides[0], beams, pulses, scale)
    steer_y = steer[:, :2].reshape(2 * beams, 4 * pulses)
    steer_z = jnp.concatenate([steer[:, :1], steer[:, 2:]], axis=1).reshape(2 * beams, 4 * pulses)

    leans = jnp.stack([2 * order + 1 - beams for order in orders])
    bins = jnp.arange(each * half, dtype=jnp.int32) + 1
    slopes = jnp.stack([(2 * own_sides[n] - 1) * (n + 2) for n in range(levels)])[:, None] * leans
    step = jnp.stack(unit(slopes[:, :, None] * bins, PERIOD), axis=1)
    squares = jnp.stack(
        [orders[n] * orders[n] * (own_sides[n] + 1) * (1 if n else 0) for n in range(levels)]
    )

    def bases(tiles):
        parts = (2 * tiles[:, None] + jnp.arange(2, dtype=jnp.int32)).reshape(-1)
        start = (parts * each * half)[:, None, None]
        both = jnp.stack(unit(slopes * start + squares, PERIOD), axis=2)
        return both.reshape(parts.shape[0], 2 * levels, beams)

    index = jnp.arange(turn // 4, dtype=jnp.int32)
    tiles_y = turn // 2 + 2 * index + bit(own_turn, 0)
    low_part = index & (1 << far) - 1
    tiles_z = ((index >> far) * 2 + bit(own_turn, far)) * (1 << far) + low_part

    final = []
    for name, keep, got, steer_own, tiles in (
        ("y", keep_y, got_y, steer_y, tiles_y),
        ("z", keep_z, got_z, steer_z, tiles_z),
    ):
        shape = (turn // 2, each, pulses, width)
        data = jnp.stack([keep.reshape(shape), got.reshape(shape)])
        kept, sent = backproject(data, steer_own, interp, bases(tiles), step, leaf)
        gone = 0 if name == "y" else far
        leading = [("leaf", b) for b in range(levels - 1, 0, -1)]
        leading += [("turn", b) for b in range(top - 1, -1, -1) if b != gone]
        order = [("leaf", b) for b in range(1, levels)]
        rest = [("turn", b) for b in range(top) if b not in (0, far)]
        order = order + [("turn", far)] if name == "y" else [("turn", 0)] + order
        terms = [kept, swapped(sent, "leaf", 0)]
        for axis, b in order + rest:
            at = leading.index((axis, b))
            before, after = 1 << at, (1 << len(leading) - at - 1) * tile
            leading.pop(at)
            own = bit(own_leaf if axis == "leaf" else own_turn, b)
            terms, sent = fold(own, terms, (before, 2, after, rows, width))
            terms.append(swapped(sent, axis, b))
        final.append(total_of([t.reshape(tile, rows, width) for t in terms]))
    upper = bit(own_turn, top) == 1
    kept = jnp.where(upper, final[0], final[1])
    sent = jnp.where(upper, final[1], final[0]).astype(jnp.bfloat16)
    return last_sum(kept, swapped(sent, "turn", top))


def solution(mesh):
    placed = (P(("leaf", "turn"), None, None), P(), P(), P("leaf", None))
    return jax.shard_map(
        per_device, mesh=mesh, in_specs=placed, out_specs=P("leaf", "turn", None), check_vma=False
    )
```

```python
import functools
import math

import jax
import jax.numpy as jnp
from jax import lax
from jax.experimental import pallas as pl
from jax.experimental.pallas import tpu as pltpu
from jax.sharding import PartitionSpec as P

WEIGHTS = (-1.0 / 32, 3.0 / 32, -7.0 / 32, 21.0 / 32, 21.0 / 32, -7.0 / 32, 3.0 / 32, -1.0 / 32)
PERIOD = 4096
VMEM_BYTES = 56 * 2**20


def bits_of(count):
    return count.bit_length() - 1


def swapped(array, axis, bit):
    return lax.ppermute(array, axis, [(i, i ^ 1 << bit) for i in range(lax.axis_size(axis))])


def unit(phase_int, period):
    angle = jnp.remainder(phase_int, period).astype(jnp.float32) * (2.0 * math.pi / period)
    return jnp.cos(angle), jnp.sin(angle)


def own_bit(axis, at):
    return lax.axis_index(axis) >> at & 1


def compress_kernel(dims, chirp_ref, echo_ref, *refs):
    tile, pulses, half, far = dims
    keep_y, send_y, keep_z, send_z, weights, rows_ref, carry = refs
    blocks = 2 * tile
    pitch = blocks + 1
    high = pl.num_programs(0)
    mid = pl.num_programs(2) - 1 - pl.program_id(2)
    near = 1 - pl.program_id(1)
    upper = pl.program_id(0) < high // 2

    @pl.when((pl.program_id(0) == 0) & (pl.program_id(1) == 0) & (pl.program_id(2) == 0))
    def _():
        rows = lax.broadcasted_iota(jnp.int32, (half, half), 0)
        cols = lax.broadcasted_iota(jnp.int32, (half, half), 1)
        taps = chirp_ref[...].astype(jnp.float32)
        tables = []
        for c in range(2):
            wide = jnp.broadcast_to(taps[c : c + 1], (half, half))
            tables.append(pltpu.roll(wide, 0, 1, stride=1, stride_axis=0).T)
        for m, mask in enumerate((rows >= cols, rows < cols)):
            re, im = (jnp.where(mask, t, 0.0) for t in tables)
            top = jnp.concatenate([re, im], axis=1)
            low = jnp.concatenate([-im, re], axis=1)
            full = jnp.concatenate([top, low], axis=0)
            weights[m * 2 * half : (m + 1) * 2 * half, :] = full.astype(jnp.bfloat16)
        carry[...] = jnp.zeros_like(carry)

    for p in range(pulses):
        for c in range(2):
            rows_ref[c, p * pitch : p * pitch + blocks, :] = echo_ref[
                p, :, c * half : (c + 1) * half
            ].astype(jnp.float32)
    turned = []
    for b in range(blocks):
        parts = [rows_ref[c, pl.ds(b, pulses, stride=pitch), :] for c in range(2)]
        turned.append(jnp.concatenate(parts, axis=1).astype(jnp.bfloat16))
    turned.append(carry[...])
    current = jnp.concatenate(turned[:-1], axis=0)
    after = jnp.concatenate(turned[1:], axis=0)
    total = jnp.dot(
        jnp.concatenate([current, after], axis=1),
        weights[...],
        preferred_element_type=jnp.float32,
    ).astype(jnp.bfloat16)
    carry[...] = turned[0]

    for side in range(2):

        @pl.when(upper & (own_bit("turn", 0) == side))
        def _(side=side):
            for b in range(blocks):
                ref = keep_y if b // tile == side else send_y
                ref[0, 0, 0, b % tile] = total[b * pulses : (b + 1) * pulses]

    for ref, mine in ((keep_z, True), (send_z, False)):

        @pl.when(jnp.logical_not(upper) & ((near == own_bit("turn", far)) == mine))
        def _(ref=ref):
            for b in range(blocks):
                ref[0, mid, b // tile, b % tile] = total[b * pulses : (b + 1) * pulses]


def compress(chirp, echoes, high, mids, far):
    pulses, blocks, width = echoes.shape
    half = width // 2
    tile = blocks // lax.axis_size("turn")
    each = high // 2
    shape_y = (each, 2, mids, tile, pulses, width)
    shape_z = (each, mids, 2, tile, pulses, width)

    def place_y(h, v, m):
        over = h >= each
        spot = (each - 1 - h, 1 - v, mids - 1 - m)
        return tuple(jnp.where(over, 0, x) for x in spot) + (0, 0, 0)

    def place_z(h, v, m):
        return jnp.minimum(high - 1 - h, each - 1), 0, 0, 0, 0, 0

    spec_y = pl.BlockSpec((1, 1, 1) + shape_y[3:], place_y)
    spec_z = pl.BlockSpec((1,) + shape_z[1:], place_z)

    def chunk(h, v, m):
        return 0, ((high - 1 - h) * 2 + 1 - v) * mids + mids - 1 - m, 0

    return pl.pallas_call(
        functools.partial(compress_kernel, (tile, pulses, half, far)),
        grid=(high, 2, mids),
        in_specs=[
            pl.BlockSpec((2, half), lambda h, v, m: (0, 0)),
            pl.BlockSpec((pulses, 2 * tile, width), chunk),
        ],
        out_specs=[spec_y, spec_y, spec_z, spec_z],
        out_shape=[
            jax.ShapeDtypeStruct(s, jnp.bfloat16) for s in (shape_y, shape_y, shape_z, shape_z)
        ],
        scratch_shapes=[
            pltpu.VMEM((2 * width, width), jnp.bfloat16),
            pltpu.VMEM((2, pulses * (2 * tile + 1), half), jnp.float32),
            pltpu.VMEM((pulses, width), jnp.bfloat16),
        ],
        compiler_params=pltpu.CompilerParams(vmem_limit_bytes=VMEM_BYTES),
        cost_estimate=pl.CostEstimate(
            flops=4 * pulses * blocks * width * width,
            bytes_accessed=4 * pulses * blocks * width,
            transcendentals=0,
        ),
        name="compress",
    )(chirp, echoes)


def image_kernel(dims, data_ref, steer_ref, interp_ref, base_ref, step_ref, out_keep, out_send):
    leaf, each, half, beams, levels = dims
    rows = beams // leaf
    pair = 2
    piece = rows

    def turned(phase, re, im):
        c, s = phase
        return c * re - s * im, c * im + s * re

    bases = []
    for n in range(2 * levels):
        bases.append(jnp.broadcast_to(base_ref[0, n : n + 1, :], (half, beams)).T)

    def phased(level, block, first, re, im):
        cut = slice(first, first + piece)
        lanes = slice(block * half, (block + 1) * half)
        phase = turned(
            (bases[2 * level][cut], bases[2 * level + 1][cut]),
            step_ref[level, 0, cut, lanes],
            step_ref[level, 1, cut, lanes],
        )
        return turned(phase, re, im)

    for at in range(0, each, pair):
        parts = []
        for n in range(2):
            for c in range(2):
                cols = slice(c * half, (c + 1) * half)
                parts.append(
                    jnp.concatenate([data_ref[n, 0, at + i, :, cols] for i in range(pair)], axis=1)
                )
        raw = jnp.dot(
            steer_ref[...], jnp.concatenate(parts, axis=0), preferred_element_type=jnp.float32
        )
        re, im = raw[:beams], raw[beams:]
        for level in range(levels):
            columns = []
            for i in range(pair):
                lanes = slice(i * half, (i + 1) * half)
                pieces = []
                for first in range(0, beams, piece):
                    cut = slice(first, first + piece)
                    both = phased(level, at + i, first, re[cut, lanes], im[cut, lanes])
                    if level == levels - 1:
                        both = jnp.concatenate(both, axis=1)
                        g = first // rows
                        if g < leaf // 2:
                            out_keep[g, 0, at + i] = both
                        else:
                            out_send[g - leaf // 2, 0, at + i] = both.astype(jnp.bfloat16)
                        continue
                    both = jnp.concatenate(both, axis=1)
                    big = both.astype(jnp.bfloat16)
                    low = (both - big.astype(jnp.float32)).astype(jnp.bfloat16)
                    pieces.append((big, low))
                if pieces:
                    columns.append(
                        jnp.concatenate([p[0] for p in pieces] + [p[1] for p in pieces], axis=0)
                    )
            if columns:
                moved = jnp.dot(
                    interp_ref[level],
                    jnp.concatenate(columns, axis=1),
                    preferred_element_type=jnp.float32,
                )
                cuts = [moved[:, n * half : (n + 1) * half] for n in range(2 * pair)]
                re = jnp.concatenate(cuts[0::2], axis=1)
                im = jnp.concatenate(cuts[1::2], axis=1)


def backproject(data, steer, interp, base, step, leaf):
    _, count, each, pulses, width = data.shape
    half = width // 2
    beams = steer.shape[0] // 2
    rows = beams // leaf
    shape = (leaf // 2, count, each, rows, width)
    out_spec = pl.BlockSpec((leaf // 2, 1) + shape[2:], lambda n: (0, n, 0, 0, 0))
    return pl.pallas_call(
        functools.partial(image_kernel, (leaf, each, half, beams, bits_of(leaf))),
        grid=(count,),
        in_specs=[
            pl.BlockSpec((2, 1, each, pulses, width), lambda n: (0, n, 0, 0, 0)),
            pl.BlockSpec(steer.shape, lambda n: (0, 0)),
            pl.BlockSpec(interp.shape, lambda n: (0, 0, 0)),
            pl.BlockSpec((1,) + base.shape[1:], lambda n: (n, 0, 0)),
            pl.BlockSpec(step.shape, lambda n: (0, 0, 0, 0)),
        ],
        out_specs=[out_spec, out_spec],
        out_shape=[
            jax.ShapeDtypeStruct(shape, jnp.float32),
            jax.ShapeDtypeStruct(shape, jnp.bfloat16),
        ],
        compiler_params=pltpu.CompilerParams(vmem_limit_bytes=16 * 2**20),
        cost_estimate=pl.CostEstimate(
            flops=12 * beams * pulses * count * each * width,
            bytes_accessed=2 * data.size + 6 * count * each * beams * width // 2,
            transcendentals=0,
        ),
        name="image",
    )(data, steer, interp, base, step)


def fold(own, keep, got):
    sums = [keep[:, n] + got[:, n].astype(jnp.float32) for n in range(2)]
    upper = own == 1
    sent = jnp.where(upper, sums[0], sums[1]).astype(jnp.bfloat16)
    return jnp.where(upper, sums[1], sums[0]), sent


def last_kernel(keep_ref, got_ref, out_ref, rows_ref):
    blocks, rows, width = keep_ref.shape
    for i in range(blocks):
        value = keep_ref[i] + got_ref[i].astype(jnp.float32)
        for c in range(2):
            cols = slice(c * width // 2, (c + 1) * width // 2)
            rows_ref[c, pl.ds(i, rows, stride=blocks), :] = value[:, cols]
    both = jnp.concatenate([rows_ref[0], rows_ref[1]], axis=1)
    out_ref[...] = both.reshape(rows, blocks, width).astype(jnp.bfloat16)


def last_sum(keep, got):
    blocks, rows, width = keep.shape
    return pl.pallas_call(
        last_kernel,
        out_shape=jax.ShapeDtypeStruct((rows, blocks, width), jnp.bfloat16),
        scratch_shapes=[pltpu.VMEM((2, rows * blocks, width // 2), jnp.float32)],
        compiler_params=pltpu.CompilerParams(vmem_limit_bytes=8 * 2**20),
        name="last_sum",
    )(keep, got)


def interpolation(taps, beams):
    cells = jnp.arange(beams, dtype=jnp.int32)
    weights = jnp.array(WEIGHTS, jnp.float32)
    picks = taps[..., None] == cells
    return jnp.where(picks, weights[:, None], 0.0).sum(axis=-2)


def steering(slots, matrix, side, beams, pulses, scale):
    count = slots.shape[0]
    beam = jnp.arange(beams, dtype=jnp.int32)[:, None, None]
    place = jnp.arange(pulses, dtype=jnp.int32)
    slot = slots[None, :, None]
    cos, sin = unit(
        (2 * beam + 1 - beams) * (2 * place + 1 - pulses)
        + 3 * (beam + 1) * (2 * slot + 1) * (2 * place + 1),
        8 * pulses,
    )
    pair = jnp.concatenate([cos * scale, sin * scale], axis=2).astype(jnp.bfloat16)
    moved = jnp.dot(
        matrix.astype(jnp.bfloat16),
        pair.reshape(beams, count * 2 * pulses),
        preferred_element_type=jnp.float32,
    ).reshape(beams, count, 2 * pulses)
    re, im = moved[:, :, :pulses], moved[:, :, pulses:]
    row = jnp.arange(beams, dtype=jnp.int32)
    c, s = (t[:, None, None] for t in unit(row * row * (side + 1), PERIOD))
    re, im = c * re - s * im, c * im + s * re
    top = jnp.concatenate([re, -im], axis=2)
    low = jnp.concatenate([im, re], axis=2)
    return jnp.concatenate([top, low], axis=0).astype(jnp.bfloat16)


def bit(value, at):
    return value >> at & 1


def per_device(echoes, chirp, taps, slots):
    leaf, turn = lax.axis_size("leaf"), lax.axis_size("turn")
    pulses, blocks, width = echoes.shape
    half = width // 2
    beams = taps.shape[2]
    levels = bits_of(leaf)
    far = (bits_of(turn) + 1) // 2 - 1
    top = bits_of(turn) - 1
    mids = 1 << far - 1
    high = turn >> far + 1
    tile = blocks // turn
    each = tile // 2
    rows = beams // leaf
    own_leaf, own_turn = lax.axis_index("leaf"), lax.axis_index("turn")

    keep_y, send_y, keep_z, send_z = compress(chirp, echoes, high, mids, far)
    got_y = swapped(send_y, "turn", 0)
    got_z = swapped(send_z, "turn", far)

    own_sides = [bit(own_leaf, level) for level in range(levels)]
    row = jnp.arange(beams, dtype=jnp.int32)
    part, place = row // rows, row % rows
    group = 2 * (part % (leaf // 2)) + (part // (leaf // 2) ^ own_sides[0])
    orders = [row] * (levels - 1) + [group * rows + place]
    own_taps = [
        lax.dynamic_index_in_dim(taps[n], own_sides[n], 0, False) for n in range(levels)
    ]
    cores = own_taps[-1].reshape(leaf // 2, 2, rows, -1)
    cores = [
        lax.dynamic_index_in_dim(cores, own_sides[0] ^ n, 1, False).reshape(beams // 2, -1)
        for n in range(2)
    ]
    own_taps[-1] = jnp.concatenate(cores, axis=0)
    matrices = interpolation(jnp.stack(own_taps), beams)
    interp = jnp.concatenate([matrices[1:]] * 2, axis=-1).astype(jnp.bfloat16)
    scale = 1.0 / math.sqrt(2.0 * slots.shape[1] * pulses)
    wanted = own_turn ^ jnp.array([0, 1, 1 << far], jnp.int32)
    picked = jnp.arange(slots.shape[1], dtype=jnp.int32) == wanted[:, None]
    own_slots = jnp.where(picked, slots, 0).sum(axis=1)
    steer = steering(own_slots, matrices[0], own_sides[0], beams, pulses, scale)
    steer_y = steer[:, :2].reshape(2 * beams, 4 * pulses)
    steer_z = jnp.concatenate([steer[:, :1], steer[:, 2:]], axis=1).reshape(2 * beams, 4 * pulses)

    leans = jnp.stack([2 * order + 1 - beams for order in orders])
    bins = jnp.arange(each * half, dtype=jnp.int32) + 1
    slopes = jnp.stack([(2 * own_sides[n] - 1) * (n + 2) for n in range(levels)])[:, None] * leans
    step = jnp.stack(unit(slopes[:, :, None] * bins, PERIOD), axis=1)
    squares = jnp.stack(
        [orders[n] * orders[n] * (own_sides[n] + 1) * (1 if n else 0) for n in range(levels)]
    )

    def bases(tiles):
        parts = (2 * tiles[:, None] + jnp.arange(2, dtype=jnp.int32)).reshape(-1)
        start = (parts * each * half)[:, None, None]
        both = jnp.stack(unit(slopes * start + squares, PERIOD), axis=2)
        return both.reshape(parts.shape[0], 2 * levels, beams)

    index = jnp.arange(turn // 4, dtype=jnp.int32)
    tiles_y = turn // 2 + 2 * index + bit(own_turn, 0)
    low_part = index & (1 << far) - 1
    tiles_z = ((index >> far) * 2 + bit(own_turn, far)) * (1 << far) + low_part

    final = []
    for name, keep, got, steer_own, tiles in (
        ("y", keep_y, got_y, steer_y, tiles_y),
        ("z", keep_z, got_z, steer_z, tiles_z),
    ):
        shape = (turn // 2, each, pulses, width)
        data = jnp.stack([keep.reshape(shape), got.reshape(shape)])
        kept, sent = backproject(data, steer_own, interp, bases(tiles), step, leaf)
        gone = 0 if name == "y" else far
        leading = [("leaf", b) for b in range(levels - 1, 0, -1)]
        leading += [("turn", b) for b in range(top - 1, -1, -1) if b != gone]
        order = [("leaf", b) for b in range(1, levels)]
        rest = [("turn", b) for b in range(top) if b not in (0, far)]
        order = order + [("turn", far)] if name == "y" else [("turn", 0)] + order
        arrived = swapped(sent, "leaf", 0)
        for axis, b in order + rest:
            at = leading.index((axis, b))
            before, after = 1 << at, (1 << len(leading) - at - 1) * tile
            leading.pop(at)
            split = (before, 2, after, rows, width)
            own = bit(own_leaf if axis == "leaf" else own_turn, b)
            kept, sent = fold(own, kept.reshape(split), arrived.reshape(split))
            arrived = swapped(sent, axis, b)
        shape = (tile, rows, width)
        final.append(kept.reshape(shape) + arrived.reshape(shape).astype(jnp.float32))
    upper = bit(own_turn, top) == 1
    kept = jnp.where(upper, final[0], final[1])
    sent = jnp.where(upper, final[1], final[0]).astype(jnp.bfloat16)
    return last_sum(kept, swapped(sent, "turn", top))


def solution(mesh):
    placed = (P(("leaf", "turn"), None, None), P(), P(), P("leaf", None))
    return jax.shard_map(
        per_device, mesh=mesh, in_specs=placed, out_specs=P("leaf", "turn", None), check_vma=False
    )
```

```python
import functools
import math

import jax
import jax.numpy as jnp
from jax import lax
from jax.experimental import pallas as pl
from jax.experimental.pallas import tpu as pltpu
from jax.sharding import PartitionSpec as P

WEIGHTS = (-1.0 / 32, 3.0 / 32, -7.0 / 32, 21.0 / 32, 21.0 / 32, -7.0 / 32, 3.0 / 32, -1.0 / 32)
PERIOD = 4096
VMEM_BYTES = 56 * 2**20


def bits_of(count):
    return count.bit_length() - 1


def bit(value, at):
    return value >> at & 1


def swapped(array, axis, bit):
    return lax.ppermute(array, axis, [(i, i ^ 1 << bit) for i in range(lax.axis_size(axis))])


def unit(phase_int, period):
    angle = jnp.remainder(phase_int, period).astype(jnp.float32) * (2.0 * math.pi / period)
    return jnp.cos(angle), jnp.sin(angle)


def compress_kernel(dims, has_edge, chirp_ref, echo_ref, *refs):
    tile, pulses, half, near_chain, far = dims
    edge_ref, refs = (refs[0], refs[1:]) if has_edge else (None, refs)
    keep_ref, send_ref, edge_out, weights, rows_ref, carry = refs
    blocks = 2 * tile
    pitch = blocks + 1
    mids = pl.num_programs(2)
    high = pl.num_programs(0)
    turn = lax.axis_index("turn")
    spot_h = (high - 1 - pl.program_id(0)) ^ (turn >> far + 1 & high - 1)
    spot_m = (mids - 1 - pl.program_id(2)) ^ (turn >> 1 & mids - 1)
    spot_v = (1 - pl.program_id(1)) ^ bit(turn, far)
    own_u = bit(turn, 0)

    @pl.when((pl.program_id(0) == 0) & (pl.program_id(1) == 0) & (pl.program_id(2) == 0))
    def _():
        rows = lax.broadcasted_iota(jnp.int32, (half, half), 0)
        cols = lax.broadcasted_iota(jnp.int32, (half, half), 1)
        taps = chirp_ref[...].astype(jnp.float32)
        tables = []
        for c in range(2):
            wide = jnp.broadcast_to(taps[c : c + 1], (half, half))
            tables.append(pltpu.roll(wide, 0, 1, stride=1, stride_axis=0).T)
        for m, mask in enumerate((rows >= cols, rows < cols)):
            re, im = (jnp.where(mask, t, 0.0) for t in tables)
            top = jnp.concatenate([re, im], axis=1)
            low = jnp.concatenate([-im, re], axis=1)
            full = jnp.concatenate([top, low], axis=0)
            weights[m * 2 * half : (m + 1) * 2 * half, :] = full.astype(jnp.bfloat16)
        carry[...] = edge_ref[...] if has_edge else jnp.zeros_like(carry)

    for p in range(pulses):
        for c in range(2):
            rows_ref[c, p * pitch : p * pitch + blocks, :] = echo_ref[
                p, :, c * half : (c + 1) * half
            ].astype(jnp.float32)
    turned = []
    for b in range(blocks):
        parts = [rows_ref[c, pl.ds(b, pulses, stride=pitch), :] for c in range(2)]
        turned.append(jnp.concatenate(parts, axis=1).astype(jnp.bfloat16))
    turned.append(carry[...])
    current = jnp.concatenate(turned[:-1], axis=0)
    after = jnp.concatenate(turned[1:], axis=0)
    total = jnp.dot(
        jnp.concatenate([current, after], axis=1),
        weights[...],
        preferred_element_type=jnp.float32,
    ).astype(jnp.bfloat16)
    carry[...] = turned[0]
    edge_out[...] = turned[0]

    def block(b):
        return total[b * pulses : (b + 1) * pulses]

    if near_chain:
        for side in range(2):

            @pl.when(own_u == side)
            def _(side=side):
                for b in range(blocks):
                    ref = keep_ref if b // tile == side else send_ref
                    ref[spot_h, spot_v, spot_m, b % tile] = block(b)
    else:
        for ref, mine in ((keep_ref, 0), (send_ref, 1)):

            @pl.when(spot_v == mine)
            def _(ref=ref):
                for b in range(blocks):
                    ref[spot_h, spot_m, b // tile ^ own_u, b % tile] = block(b)


def compress(chirp, edge, echoes, high, mids, near_chain, far, first_high):
    pulses, blocks, width = echoes.shape
    half = width // 2
    tile = blocks // lax.axis_size("turn")
    if near_chain:
        shape = (high, 2, mids, tile, pulses, width)
    else:
        shape = (high, mids, 2, tile, pulses, width)
    spec = pl.BlockSpec(shape, lambda h, v, m: (0, 0, 0, 0, 0, 0))
    edge_spec = pl.BlockSpec((pulses, width), lambda h, v, m: (0, 0))

    def chunk(h, v, m):
        return 0, ((first_high + high - 1 - h) * 2 + 1 - v) * mids + mids - 1 - m, 0

    in_specs = [
        pl.BlockSpec((2, half), lambda h, v, m: (0, 0)),
        pl.BlockSpec((pulses, 2 * tile, width), chunk),
    ]
    operands = [chirp, echoes]
    if edge is not None:
        in_specs.append(edge_spec)
        operands.append(edge)
    dims = (tile, pulses, half, near_chain, far)
    return pl.pallas_call(
        functools.partial(compress_kernel, dims, edge is not None),
        grid=(high, 2, mids),
        in_specs=in_specs,
        out_specs=[spec, spec, edge_spec],
        out_shape=[
            jax.ShapeDtypeStruct(s, jnp.bfloat16) for s in (shape, shape, (pulses, width))
        ],
        scratch_shapes=[
            pltpu.VMEM((2 * width, width), jnp.bfloat16),
            pltpu.VMEM((2, pulses * (2 * tile + 1), half), jnp.float32),
            pltpu.VMEM((pulses, width), jnp.bfloat16),
        ],
        compiler_params=pltpu.CompilerParams(vmem_limit_bytes=VMEM_BYTES),
        cost_estimate=pl.CostEstimate(
            flops=2 * pulses * blocks * width * width,
            bytes_accessed=2 * pulses * blocks * width,
            transcendentals=0,
        ),
        name="compress",
    )(*operands)


def image_kernel(dims, data_ref, steer_ref, interp_ref, base_ref, step_ref, out_keep, out_send):
    leaf, each, half, beams, levels = dims
    rows = beams // leaf
    pair = 2
    piece = rows

    def turned(phase, re, im):
        c, s = phase
        return c * re - s * im, c * im + s * re

    bases = []
    for n in range(2 * levels):
        bases.append(jnp.broadcast_to(base_ref[0, n : n + 1, :], (half, beams)).T)

    def phased(level, block, first, re, im):
        cut = slice(first, first + piece)
        lanes = slice(block * half, (block + 1) * half)
        phase = turned(
            (bases[2 * level][cut], bases[2 * level + 1][cut]),
            step_ref[level, 0, cut, lanes],
            step_ref[level, 1, cut, lanes],
        )
        return turned(phase, re, im)

    for at in range(0, each, pair):
        parts = []
        for n in range(2):
            for c in range(2):
                cols = slice(c * half, (c + 1) * half)
                parts.append(
                    jnp.concatenate([data_ref[n, 0, at + i, :, cols] for i in range(pair)], axis=1)
                )
        raw = jnp.dot(
            steer_ref[...], jnp.concatenate(parts, axis=0), preferred_element_type=jnp.float32
        )
        re, im = raw[:beams], raw[beams:]
        for level in range(levels):
            columns = []
            for i in range(pair):
                lanes = slice(i * half, (i + 1) * half)
                pieces = []
                for first in range(0, beams, piece):
                    cut = slice(first, first + piece)
                    both = phased(level, at + i, first, re[cut, lanes], im[cut, lanes])
                    if level == levels - 1:
                        both = jnp.concatenate(both, axis=1)
                        g = first // rows
                        if g < leaf // 2:
                            out_keep[g, 0, at + i] = both
                        else:
                            out_send[g - leaf // 2, 0, at + i] = both.astype(jnp.bfloat16)
                        continue
                    both = jnp.concatenate(both, axis=1)
                    big = both.astype(jnp.bfloat16)
                    low = (both - big.astype(jnp.float32)).astype(jnp.bfloat16)
                    pieces.append((big, low))
                if pieces:
                    columns.append(
                        jnp.concatenate([p[0] for p in pieces] + [p[1] for p in pieces], axis=0)
                    )
            if columns:
                moved = jnp.dot(
                    interp_ref[level],
                    jnp.concatenate(columns, axis=1),
                    preferred_element_type=jnp.float32,
                )
                cuts = [moved[:, n * half : (n + 1) * half] for n in range(2 * pair)]
                re = jnp.concatenate(cuts[0::2], axis=1)
                im = jnp.concatenate(cuts[1::2], axis=1)


def backproject(data, steer, interp, base, step, leaf):
    _, count, each, pulses, width = data.shape
    half = width // 2
    beams = steer.shape[0] // 2
    rows = beams // leaf
    shape = (leaf // 2, count, each, rows, width)
    out_spec = pl.BlockSpec((leaf // 2, 1) + shape[2:], lambda n: (0, n, 0, 0, 0))
    return pl.pallas_call(
        functools.partial(image_kernel, (leaf, each, half, beams, bits_of(leaf))),
        grid=(count,),
        in_specs=[
            pl.BlockSpec((2, 1, each, pulses, width), lambda n: (0, n, 0, 0, 0)),
            pl.BlockSpec(steer.shape, lambda n: (0, 0)),
            pl.BlockSpec(interp.shape, lambda n: (0, 0, 0)),
            pl.BlockSpec((1,) + base.shape[1:], lambda n: (n, 0, 0)),
            pl.BlockSpec(step.shape, lambda n: (0, 0, 0, 0)),
        ],
        out_specs=[out_spec, out_spec],
        out_shape=[
            jax.ShapeDtypeStruct(shape, jnp.float32),
            jax.ShapeDtypeStruct(shape, jnp.bfloat16),
        ],
        compiler_params=pltpu.CompilerParams(vmem_limit_bytes=10 * 2**20),
        cost_estimate=pl.CostEstimate(
            flops=12 * beams * pulses * count * each * width,
            bytes_accessed=2 * data.size + 6 * count * each * beams * width // 2,
            transcendentals=0,
        ),
        name="image",
    )(data, steer, interp, base, step)


def fold(keep, got):
    stay, gone = (keep[:, n] + got[:, n].astype(jnp.float32) for n in range(2))
    return stay, gone.astype(jnp.bfloat16)


def last_kernel(keep_ref, got_ref, out_ref, rows_ref):
    blocks, rows, width = keep_ref.shape
    for i in range(blocks):
        value = keep_ref[i] + got_ref[i].astype(jnp.float32)
        for c in range(2):
            cols = slice(c * width // 2, (c + 1) * width // 2)
            rows_ref[c, pl.ds(i, rows, stride=blocks), :] = value[:, cols]
    both = jnp.concatenate([rows_ref[0], rows_ref[1]], axis=1)
    out_ref[...] = both.reshape(rows, blocks, width).astype(jnp.bfloat16)


def last_sum(keep, got):
    blocks, rows, width = keep.shape
    return pl.pallas_call(
        last_kernel,
        out_shape=jax.ShapeDtypeStruct((rows, blocks, width), jnp.bfloat16),
        scratch_shapes=[pltpu.VMEM((2, rows * blocks, width // 2), jnp.float32)],
        compiler_params=pltpu.CompilerParams(vmem_limit_bytes=8 * 2**20),
        name="last_sum",
    )(keep, got)


def interpolation(taps, beams):
    cells = jnp.arange(beams, dtype=jnp.int32)
    weights = jnp.array(WEIGHTS, jnp.float32)
    picks = taps[..., None] == cells
    return jnp.where(picks, weights[:, None], 0.0).sum(axis=-2)


def steering(slots, matrix, side, beams, pulses, scale):
    count = slots.shape[0]
    beam = jnp.arange(beams, dtype=jnp.int32)[:, None, None]
    place = jnp.arange(pulses, dtype=jnp.int32)
    slot = slots[None, :, None]
    cos, sin = unit(
        (2 * beam + 1 - beams) * (2 * place + 1 - pulses)
        + 3 * (beam + 1) * (2 * slot + 1) * (2 * place + 1),
        8 * pulses,
    )
    pair = jnp.concatenate([cos * scale, sin * scale], axis=2).astype(jnp.bfloat16)
    moved = jnp.dot(
        matrix.astype(jnp.bfloat16),
        pair.reshape(beams, count * 2 * pulses),
        preferred_element_type=jnp.float32,
    ).reshape(beams, count, 2 * pulses)
    re, im = moved[:, :, :pulses], moved[:, :, pulses:]
    row = jnp.arange(beams, dtype=jnp.int32)
    c, s = (t[:, None, None] for t in unit(row * row * (side + 1), PERIOD))
    re, im = c * re - s * im, c * im + s * re
    top = jnp.concatenate([re, -im], axis=2)
    low = jnp.concatenate([im, re], axis=2)
    return jnp.concatenate([top, low], axis=0).astype(jnp.bfloat16)


def per_device(echoes, chirp, taps, slots):
    leaf, turn = lax.axis_size("leaf"), lax.axis_size("turn")
    pulses, blocks, width = echoes.shape
    half = width // 2
    beams = taps.shape[2]
    levels = bits_of(leaf)
    far = (bits_of(turn) + 1) // 2 - 1
    top = bits_of(turn) - 1
    mids = 1 << far - 1
    high = turn >> far + 2
    tile = blocks // turn
    each = tile // 2
    rows = beams // leaf
    own_leaf, own_turn = lax.axis_index("leaf"), lax.axis_index("turn")

    keep_y, send_y, edge = compress(chirp, None, echoes, high, mids, True, far, high)
    got_y = swapped(send_y, "turn", 0)
    keep_z, send_z, _ = compress(chirp, edge, echoes, high, mids, False, far, 0)
    got_z = swapped(send_z, "turn", far)

    own_sides = [bit(own_leaf, level) for level in range(levels)]
    row = jnp.arange(beams, dtype=jnp.int32)
    part, place = row // rows, row % rows
    group = own_leaf ^ (2 * (part % (leaf // 2)) + part // (leaf // 2))
    orders = [row] * (levels - 1) + [group * rows + place]
    own_taps = [
        lax.dynamic_index_in_dim(taps[n], own_sides[n], 0, False) for n in range(levels)
    ]
    groups = own_taps[-1].reshape(leaf, rows, -1)
    own_taps[-1] = jnp.concatenate(
        [
            lax.dynamic_index_in_dim(groups, own_leaf ^ (2 * g + side), 0, False)
            for side in range(2)
            for g in range(leaf // 2)
        ],
        axis=0,
    )
    matrices = interpolation(jnp.stack(own_taps), beams)
    interp = jnp.concatenate([matrices[1:]] * 2, axis=-1).astype(jnp.bfloat16)
    scale = 1.0 / math.sqrt(2.0 * slots.shape[1] * pulses)
    wanted = own_turn ^ jnp.array([0, 1, 1 << far], jnp.int32)
    picked = jnp.arange(slots.shape[1], dtype=jnp.int32) == wanted[:, None]
    own_slots = jnp.where(picked, slots, 0).sum(axis=1)
    steer = steering(own_slots, matrices[0], own_sides[0], beams, pulses, scale)
    steer_y = steer[:, :2].reshape(2 * beams, 4 * pulses)
    steer_z = jnp.concatenate([steer[:, :1], steer[:, 2:]], axis=1).reshape(2 * beams, 4 * pulses)

    leans = jnp.stack([2 * order + 1 - beams for order in orders])
    bins = jnp.arange(each * half, dtype=jnp.int32) + 1
    slopes = jnp.stack([(2 * own_sides[n] - 1) * (n + 2) for n in range(levels)])[:, None] * leans
    step = jnp.stack(unit(slopes[:, :, None] * bins, PERIOD), axis=1)
    squares = jnp.stack(
        [orders[n] * orders[n] * (own_sides[n] + 1) * (1 if n else 0) for n in range(levels)]
    )

    def bases(tiles):
        parts = (2 * tiles[:, None] + jnp.arange(2, dtype=jnp.int32)).reshape(-1)
        start = (parts * each * half)[:, None, None]
        both = jnp.stack(unit(slopes * start + squares, PERIOD), axis=2)
        return both.reshape(parts.shape[0], 2 * levels, beams)

    index = jnp.arange(turn // 4, dtype=jnp.int32)
    tiles_y = turn // 2 + 2 * (index ^ (own_turn >> 1 & turn // 4 - 1)) + bit(own_turn, 0)
    low_part = (index ^ own_turn) & (1 << far) - 1
    high_part = index >> far ^ (own_turn >> far + 1 & high - 1)
    tiles_z = (high_part * 2 + bit(own_turn, far)) * (1 << far) + low_part

    final = []
    for name, keep, got, steer_own, tiles in (
        ("y", keep_y, got_y, steer_y, tiles_y),
        ("z", keep_z, got_z, steer_z, tiles_z),
    ):
        shape = (turn // 2, each, pulses, width)
        data = jnp.stack([keep.reshape(shape), got.reshape(shape)])
        kept, sent = backproject(data, steer_own, interp, bases(tiles), step, leaf)
        gone = 0 if name == "y" else far
        leading = [("leaf", b) for b in range(levels - 1, 0, -1)]
        leading += [("turn", b) for b in range(top - 1, -1, -1) if b != gone]
        order = [("leaf", b) for b in range(1, levels)]
        rest = [("turn", b) for b in range(top) if b not in (0, far)]
        order = order + [("turn", far)] if name == "y" else [("turn", 0)] + order
        arrived = swapped(sent, "leaf", 0)
        for axis, b in order + rest:
            at = leading.index((axis, b))
            before, after = 1 << at, (1 << len(leading) - at - 1) * tile
            leading.pop(at)
            split = (before, 2, after, rows, width)
            kept, sent = fold(kept.reshape(split), arrived.reshape(split))
            arrived = swapped(sent, axis, b)
        shape = (tile, rows, width)
        final.append(kept.reshape(shape) + arrived.reshape(shape).astype(jnp.float32))
    upper = bit(own_turn, top) == 1
    kept = jnp.where(upper, final[0], final[1])
    sent = jnp.where(upper, final[1], final[0]).astype(jnp.bfloat16)
    return last_sum(kept, swapped(sent, "turn", top))


def solution(mesh):
    placed = (P(("leaf", "turn"), None, None), P(), P(), P("leaf", None))
    return jax.shard_map(
        per_device, mesh=mesh, in_specs=placed, out_specs=P("leaf", "turn", None), check_vma=False
    )
```

```python
import functools
import math

import jax
import jax.numpy as jnp
from jax import lax
from jax.experimental import pallas as pl
from jax.experimental.pallas import tpu as pltpu
from jax.sharding import PartitionSpec as P

WEIGHTS = (-1.0 / 32, 3.0 / 32, -7.0 / 32, 21.0 / 32, 21.0 / 32, -7.0 / 32, 3.0 / 32, -1.0 / 32)
PERIOD = 4096
VMEM_BYTES = 56 * 2**20


def bits_of(count):
    return count.bit_length() - 1


def bit(value, at):
    return value >> at & 1


def swapped(array, axis, bit):
    return lax.ppermute(array, axis, [(i, i ^ 1 << bit) for i in range(lax.axis_size(axis))])


def unit(phase_int, period):
    angle = jnp.remainder(phase_int, period).astype(jnp.float32) * (2.0 * math.pi / period)
    return jnp.cos(angle), jnp.sin(angle)


def compress_kernel(dims, has_edge, chirp_ref, echo_ref, *refs):
    tile, pulses, half, near_chain, far = dims
    edge_ref, refs = (refs[0], refs[1:]) if has_edge else (None, refs)
    keep_ref, send_ref, edge_out, weights, rows_ref, carry = refs
    blocks = 2 * tile
    pitch = blocks + 1
    mids = pl.num_programs(2)
    high = pl.num_programs(0)
    turn = lax.axis_index("turn")
    spot_h = (high - 1 - pl.program_id(0)) ^ (turn >> far + 1 & high - 1)
    spot_m = (mids - 1 - pl.program_id(2)) ^ (turn >> 1 & mids - 1)
    spot_v = (1 - pl.program_id(1)) ^ bit(turn, far)
    own_u = bit(turn, 0)

    @pl.when((pl.program_id(0) == 0) & (pl.program_id(1) == 0) & (pl.program_id(2) == 0))
    def _():
        rows = lax.broadcasted_iota(jnp.int32, (half, half), 0)
        cols = lax.broadcasted_iota(jnp.int32, (half, half), 1)
        taps = chirp_ref[...].astype(jnp.float32)
        tables = []
        for c in range(2):
            wide = jnp.broadcast_to(taps[c : c + 1], (half, half))
            tables.append(pltpu.roll(wide, 0, 1, stride=1, stride_axis=0).T)
        for m, mask in enumerate((rows >= cols, rows < cols)):
            re, im = (jnp.where(mask, t, 0.0) for t in tables)
            top = jnp.concatenate([re, im], axis=1)
            low = jnp.concatenate([-im, re], axis=1)
            full = jnp.concatenate([top, low], axis=0)
            weights[m * 2 * half : (m + 1) * 2 * half, :] = full.astype(jnp.bfloat16)
        carry[...] = edge_ref[...] if has_edge else jnp.zeros_like(carry)

    for p in range(pulses):
        for c in range(2):
            rows_ref[c, p * pitch : p * pitch + blocks, :] = echo_ref[
                p, :, c * half : (c + 1) * half
            ].astype(jnp.float32)
    turned = []
    for b in range(blocks):
        parts = [rows_ref[c, pl.ds(b, pulses, stride=pitch), :] for c in range(2)]
        turned.append(jnp.concatenate(parts, axis=1).astype(jnp.bfloat16))
    turned.append(carry[...])
    current = jnp.concatenate(turned[:-1], axis=0)
    after = jnp.concatenate(turned[1:], axis=0)
    total = jnp.dot(
        jnp.concatenate([current, after], axis=1),
        weights[...],
        preferred_element_type=jnp.float32,
    ).astype(jnp.bfloat16)
    carry[...] = turned[0]
    edge_out[...] = turned[0]

    def block(b):
        return total[b * pulses : (b + 1) * pulses]

    if near_chain:
        for side in range(2):

            @pl.when(own_u == side)
            def _(side=side):
                for b in range(blocks):
                    ref = keep_ref if b // tile == side else send_ref
                    ref[spot_h, spot_v, spot_m, b % tile] = block(b)
    else:
        for ref, mine in ((keep_ref, 0), (send_ref, 1)):

            @pl.when(spot_v == mine)
            def _(ref=ref):
                for b in range(blocks):
                    ref[spot_h, spot_m, b // tile ^ own_u, b % tile] = block(b)


def compress(chirp, edge, echoes, high, mids, near_chain, far, first_high):
    pulses, blocks, width = echoes.shape
    half = width // 2
    tile = blocks // lax.axis_size("turn")
    if near_chain:
        shape = (high, 2, mids, tile, pulses, width)
    else:
        shape = (high, mids, 2, tile, pulses, width)
    spec = pl.BlockSpec(shape, lambda h, v, m: (0, 0, 0, 0, 0, 0))
    edge_spec = pl.BlockSpec((pulses, width), lambda h, v, m: (0, 0))

    def chunk(h, v, m):
        return 0, ((first_high + high - 1 - h) * 2 + 1 - v) * mids + mids - 1 - m, 0

    in_specs = [
        pl.BlockSpec((2, half), lambda h, v, m: (0, 0)),
        pl.BlockSpec((pulses, 2 * tile, width), chunk),
    ]
    operands = [chirp, echoes]
    if edge is not None:
        in_specs.append(edge_spec)
        operands.append(edge)
    dims = (tile, pulses, half, near_chain, far)
    return pl.pallas_call(
        functools.partial(compress_kernel, dims, edge is not None),
        grid=(high, 2, mids),
        in_specs=in_specs,
        out_specs=[spec, spec, edge_spec],
        out_shape=[
            jax.ShapeDtypeStruct(s, jnp.bfloat16) for s in (shape, shape, (pulses, width))
        ],
        scratch_shapes=[
            pltpu.VMEM((2 * width, width), jnp.bfloat16),
            pltpu.VMEM((2, pulses * (2 * tile + 1), half), jnp.float32),
            pltpu.VMEM((pulses, width), jnp.bfloat16),
        ],
        compiler_params=pltpu.CompilerParams(
            vmem_limit_bytes=VMEM_BYTES if near_chain else 20 * 2**20
        ),
        cost_estimate=pl.CostEstimate(
            flops=2 * pulses * blocks * width * width,
            bytes_accessed=2 * pulses * blocks * width,
            transcendentals=0,
        ),
        name="compress",
    )(*operands)


def image_kernel(dims, data_ref, steer_ref, interp_ref, base_ref, step_ref, out_keep, out_send):
    leaf, each, half, beams, levels = dims
    rows = beams // leaf
    pair = 2
    piece = rows

    def turned(phase, re, im):
        c, s = phase
        return c * re - s * im, c * im + s * re

    bases = []
    for n in range(2 * levels):
        bases.append(jnp.broadcast_to(base_ref[0, n : n + 1, :], (half, beams)).T)

    def phased(level, block, first, re, im):
        cut = slice(first, first + piece)
        lanes = slice(block * half, (block + 1) * half)
        phase = turned(
            (bases[2 * level][cut], bases[2 * level + 1][cut]),
            step_ref[level, 0, cut, lanes],
            step_ref[level, 1, cut, lanes],
        )
        return turned(phase, re, im)

    for at in range(0, each, pair):
        parts = []
        for n in range(2):
            for c in range(2):
                cols = slice(c * half, (c + 1) * half)
                parts.append(
                    jnp.concatenate([data_ref[n, 0, at + i, :, cols] for i in range(pair)], axis=1)
                )
        raw = jnp.dot(
            steer_ref[...], jnp.concatenate(parts, axis=0), preferred_element_type=jnp.float32
        )
        re, im = raw[:beams], raw[beams:]
        for level in range(levels):
            columns = []
            for i in range(pair):
                lanes = slice(i * half, (i + 1) * half)
                pieces = []
                for first in range(0, beams, piece):
                    cut = slice(first, first + piece)
                    both = phased(level, at + i, first, re[cut, lanes], im[cut, lanes])
                    if level == levels - 1:
                        both = jnp.concatenate(both, axis=1)
                        g = first // rows
                        if g < leaf // 2:
                            out_keep[g, 0, at + i] = both
                        else:
                            out_send[g - leaf // 2, 0, at + i] = both.astype(jnp.bfloat16)
                        continue
                    both = jnp.concatenate(both, axis=1)
                    big = both.astype(jnp.bfloat16)
                    low = (both - big.astype(jnp.float32)).astype(jnp.bfloat16)
                    pieces.append((big, low))
                if pieces:
                    columns.append(
                        jnp.concatenate([p[0] for p in pieces] + [p[1] for p in pieces], axis=0)
                    )
            if columns:
                moved = jnp.dot(
                    interp_ref[level],
                    jnp.concatenate(columns, axis=1),
                    preferred_element_type=jnp.float32,
                )
                cuts = [moved[:, n * half : (n + 1) * half] for n in range(2 * pair)]
                re = jnp.concatenate(cuts[0::2], axis=1)
                im = jnp.concatenate(cuts[1::2], axis=1)


def backproject(data, steer, interp, base, step, leaf):
    _, count, each, pulses, width = data.shape
    half = width // 2
    beams = steer.shape[0] // 2
    rows = beams // leaf
    shape = (leaf // 2, count, each, rows, width)

    def block(n):
        return n % (count // 2) * 2 + n // (count // 2)

    out_spec = pl.BlockSpec((leaf // 2, 1) + shape[2:], lambda n: (0, n, 0, 0, 0))
    return pl.pallas_call(
        functools.partial(image_kernel, (leaf, each, half, beams, bits_of(leaf))),
        grid=(count,),
        in_specs=[
            pl.BlockSpec((2, 1, each, pulses, width), lambda n: (0, block(n), 0, 0, 0)),
            pl.BlockSpec(steer.shape, lambda n: (0, 0)),
            pl.BlockSpec(interp.shape, lambda n: (0, 0, 0)),
            pl.BlockSpec((1,) + base.shape[1:], lambda n: (block(n), 0, 0)),
            pl.BlockSpec(step.shape, lambda n: (0, 0, 0, 0)),
        ],
        out_specs=[out_spec, out_spec],
        out_shape=[
            jax.ShapeDtypeStruct(shape, jnp.float32),
            jax.ShapeDtypeStruct(shape, jnp.bfloat16),
        ],
        compiler_params=pltpu.CompilerParams(vmem_limit_bytes=10 * 2**20),
        cost_estimate=pl.CostEstimate(
            flops=12 * beams * pulses * count * each * width,
            bytes_accessed=2 * data.size + 6 * count * each * beams * width // 2,
            transcendentals=0,
        ),
        name="image",
    )(data, steer, interp, base, step)


def fold(keep, got):
    stay, gone = (keep[:, n] + got[:, n].astype(jnp.float32) for n in range(2))
    return stay, gone.astype(jnp.bfloat16)


def last_kernel(*refs):
    out_ref, rows_ref = refs[-2:]
    each, rows, width = refs[0].shape
    blocks = 2 * each
    for n in range(2):
        for i in range(each):
            value = refs[2 * n][i] + refs[2 * n + 1][i].astype(jnp.float32)
            for c in range(2):
                cols = slice(c * width // 2, (c + 1) * width // 2)
                rows_ref[c, pl.ds(n * each + i, rows, stride=blocks), :] = value[:, cols]
    both = jnp.concatenate([rows_ref[0], rows_ref[1]], axis=1)
    out_ref[...] = both.reshape(rows, blocks, width).astype(jnp.bfloat16)


def last_sum(*parts):
    each, rows, width = parts[0].shape
    return pl.pallas_call(
        last_kernel,
        out_shape=jax.ShapeDtypeStruct((rows, 2 * each, width), jnp.bfloat16),
        scratch_shapes=[pltpu.VMEM((2, rows * 2 * each, width // 2), jnp.float32)],
        compiler_params=pltpu.CompilerParams(vmem_limit_bytes=8 * 2**20),
        name="last_sum",
    )(*parts)


def interpolation(taps, beams):
    cells = jnp.arange(beams, dtype=jnp.int32)
    weights = jnp.array(WEIGHTS, jnp.float32)
    picks = taps[..., None] == cells
    return jnp.where(picks, weights[:, None], 0.0).sum(axis=-2)


def steering(slots, matrix, side, beams, pulses, scale):
    count = slots.shape[0]
    beam = jnp.arange(beams, dtype=jnp.int32)[:, None, None]
    place = jnp.arange(pulses, dtype=jnp.int32)
    slot = slots[None, :, None]
    cos, sin = unit(
        (2 * beam + 1 - beams) * (2 * place + 1 - pulses)
        + 3 * (beam + 1) * (2 * slot + 1) * (2 * place + 1),
        8 * pulses,
    )
    pair = jnp.concatenate([cos * scale, sin * scale], axis=2).astype(jnp.bfloat16)
    moved = jnp.dot(
        matrix.astype(jnp.bfloat16),
        pair.reshape(beams, count * 2 * pulses),
        preferred_element_type=jnp.float32,
    ).reshape(beams, count, 2 * pulses)
    re, im = moved[:, :, :pulses], moved[:, :, pulses:]
    row = jnp.arange(beams, dtype=jnp.int32)
    c, s = (t[:, None, None] for t in unit(row * row * (side + 1), PERIOD))
    re, im = c * re - s * im, c * im + s * re
    top = jnp.concatenate([re, -im], axis=2)
    low = jnp.concatenate([im, re], axis=2)
    return jnp.concatenate([top, low], axis=0).astype(jnp.bfloat16)


def per_device(echoes, chirp, taps, slots):
    leaf, turn = lax.axis_size("leaf"), lax.axis_size("turn")
    pulses, blocks, width = echoes.shape
    half = width // 2
    beams = taps.shape[2]
    levels = bits_of(leaf)
    far = (bits_of(turn) + 1) // 2 - 1
    top = bits_of(turn) - 1
    mids = 1 << far - 1
    high = turn >> far + 2
    tile = blocks // turn
    each = tile // 2
    rows = beams // leaf
    own_leaf, own_turn = lax.axis_index("leaf"), lax.axis_index("turn")

    keep_y, send_y, edge = compress(chirp, None, echoes, high, mids, True, far, high)
    got_y = swapped(send_y, "turn", 0)
    keep_z, send_z, _ = compress(chirp, edge, echoes, high, mids, False, far, 0)
    got_z = swapped(send_z, "turn", far)

    own_sides = [bit(own_leaf, level) for level in range(levels)]
    row = jnp.arange(beams, dtype=jnp.int32)
    part, place = row // rows, row % rows
    group = own_leaf ^ (2 * (part % (leaf // 2)) + part // (leaf // 2))
    orders = [row] * (levels - 1) + [group * rows + place]
    own_taps = [
        lax.dynamic_index_in_dim(taps[n], own_sides[n], 0, False) for n in range(levels)
    ]
    groups = own_taps[-1].reshape(leaf, rows, -1)
    own_taps[-1] = jnp.concatenate(
        [
            lax.dynamic_index_in_dim(groups, own_leaf ^ (2 * g + side), 0, False)
            for side in range(2)
            for g in range(leaf // 2)
        ],
        axis=0,
    )
    matrices = interpolation(jnp.stack(own_taps), beams)
    interp = jnp.concatenate([matrices[1:]] * 2, axis=-1).astype(jnp.bfloat16)
    scale = 1.0 / math.sqrt(2.0 * slots.shape[1] * pulses)
    wanted = own_turn ^ jnp.array([0, 1, 1 << far], jnp.int32)
    picked = jnp.arange(slots.shape[1], dtype=jnp.int32) == wanted[:, None]
    own_slots = jnp.where(picked, slots, 0).sum(axis=1)
    steer = steering(own_slots, matrices[0], own_sides[0], beams, pulses, scale)
    steer_y = steer[:, :2].reshape(2 * beams, 4 * pulses)
    steer_z = jnp.concatenate([steer[:, :1], steer[:, 2:]], axis=1).reshape(2 * beams, 4 * pulses)

    leans = jnp.stack([2 * order + 1 - beams for order in orders])
    bins = jnp.arange(each * half, dtype=jnp.int32) + 1
    slopes = jnp.stack([(2 * own_sides[n] - 1) * (n + 2) for n in range(levels)])[:, None] * leans
    step = jnp.stack(unit(slopes[:, :, None] * bins, PERIOD), axis=1)
    squares = jnp.stack(
        [orders[n] * orders[n] * (own_sides[n] + 1) * (1 if n else 0) for n in range(levels)]
    )

    def bases(tiles):
        parts = (2 * tiles[:, None] + jnp.arange(2, dtype=jnp.int32)).reshape(-1)
        start = (parts * each * half)[:, None, None]
        both = jnp.stack(unit(slopes * start + squares, PERIOD), axis=2)
        return both.reshape(parts.shape[0], 2 * levels, beams)

    index = jnp.arange(turn // 4, dtype=jnp.int32)
    tiles_y = turn // 2 + 2 * (index ^ (own_turn >> 1 & turn // 4 - 1)) + bit(own_turn, 0)
    low_part = (index ^ own_turn) & (1 << far) - 1
    high_part = index >> far ^ (own_turn >> far + 1 & high - 1)
    tiles_z = (high_part * 2 + bit(own_turn, far)) * (1 << far) + low_part

    pieces = []
    for name, keep, got, steer_own, tiles in (
        ("y", keep_y, got_y, steer_y, tiles_y),
        ("z", keep_z, got_z, steer_z, tiles_z),
    ):
        shape = (turn // 2, each, pulses, width)
        data = jnp.stack([keep.reshape(shape), got.reshape(shape)])
        kept, sent = backproject(data, steer_own, interp, bases(tiles), step, leaf)
        gone = 0 if name == "y" else far
        arrived = swapped(sent, "leaf", 0)
        parts = (leaf // 2, 2, turn // 4, each, rows, width)
        kept, arrived = kept.reshape(parts), arrived.reshape(parts)
        pieces.append([(kept[:, n], arrived[:, n], gone) for n in range(2)])

    final = [[], []]
    for n in range(2):
        for chain in range(2):
            kept, arrived, gone = pieces[chain][n]
            leading = [("leaf", b) for b in range(levels - 1, 0, -1)]
            leading += [("turn", b) for b in range(top - 1, -1, -1) if b != gone]
            order = [("leaf", b) for b in range(1, levels)]
            rest = [("turn", b) for b in range(top) if b not in (0, far)]
            order = [("turn", 0)] + order if gone else order + [("turn", far)]
            for axis, b in order + rest:
                at = leading.index((axis, b))
                before, after = 1 << at, (1 << len(leading) - at - 1) * each
                leading.pop(at)
                split = (before, 2, after, rows, width)
                kept, sent = fold(kept.reshape(split), arrived.reshape(split))
                arrived = swapped(sent, axis, b)
            shape = (each, rows, width)
            total = kept.reshape(shape) + arrived.reshape(shape).astype(jnp.float32)
            final[n].append(total)
    upper = bit(own_turn, top) == 1
    sums = []
    for first, second in final:
        sent = jnp.where(upper, second, first).astype(jnp.bfloat16)
        sums += [jnp.where(upper, first, second), swapped(sent, "turn", top)]
    return last_sum(*sums)


def solution(mesh):
    placed = (P(("leaf", "turn"), None, None), P(), P(), P("leaf", None))
    return jax.shard_map(
        per_device, mesh=mesh, in_specs=placed, out_specs=P("leaf", "turn", None), check_vma=False
    )
```

```python
import functools
import math

import jax
import jax.numpy as jnp
from jax import lax
from jax.experimental import pallas as pl
from jax.experimental.pallas import tpu as pltpu
from jax.sharding import PartitionSpec as P

WEIGHTS = (-1.0 / 32, 3.0 / 32, -7.0 / 32, 21.0 / 32, 21.0 / 32, -7.0 / 32, 3.0 / 32, -1.0 / 32)
PERIOD = 4096
VMEM_BYTES = 52 * 2**20


def bits_of(count):
    return count.bit_length() - 1


def bit(value, at):
    return value >> at & 1


def swapped(array, axis, bit):
    return lax.ppermute(array, axis, [(i, i ^ 1 << bit) for i in range(lax.axis_size(axis))])


def unit(phase_int, period):
    angle = jnp.remainder(phase_int, period).astype(jnp.float32) * (2.0 * math.pi / period)
    return jnp.cos(angle), jnp.sin(angle)


def compress_kernel(dims, has_edge, chirp_ref, echo_ref, *refs):
    tile, pulses, half, near_chain, far = dims
    edge_ref, refs = (refs[0], refs[1:]) if has_edge else (None, refs)
    keep_ref, send_ref, edge_out, weights, rows_ref, carry = refs
    blocks = 2 * tile
    pitch = blocks + 1
    mids = pl.num_programs(2)
    high = pl.num_programs(0)
    turn = lax.axis_index("turn")
    spot_h = (high - 1 - pl.program_id(0)) ^ (turn >> far + 1 & high - 1)
    spot_m = (mids - 1 - pl.program_id(2)) ^ (turn >> 1 & mids - 1)
    spot_v = (1 - pl.program_id(1)) ^ bit(turn, far)
    own_u = bit(turn, 0)

    @pl.when((pl.program_id(0) == 0) & (pl.program_id(1) == 0) & (pl.program_id(2) == 0))
    def _():
        rows = lax.broadcasted_iota(jnp.int32, (half, half), 0)
        cols = lax.broadcasted_iota(jnp.int32, (half, half), 1)
        taps = chirp_ref[...].astype(jnp.float32)
        tables = []
        for c in range(2):
            wide = jnp.broadcast_to(taps[c : c + 1], (half, half))
            tables.append(pltpu.roll(wide, 0, 1, stride=1, stride_axis=0).T)
        for m, mask in enumerate((rows >= cols, rows < cols)):
            re, im = (jnp.where(mask, t, 0.0) for t in tables)
            top = jnp.concatenate([re, im], axis=1)
            low = jnp.concatenate([-im, re], axis=1)
            full = jnp.concatenate([top, low], axis=0)
            weights[m * 2 * half : (m + 1) * 2 * half, :] = full.astype(jnp.bfloat16)
        carry[...] = edge_ref[...] if has_edge else jnp.zeros_like(carry)

    for p in range(pulses):
        for c in range(2):
            rows_ref[c, p * pitch : p * pitch + blocks, :] = echo_ref[
                p, :, c * half : (c + 1) * half
            ].astype(jnp.float32)
    turned = []
    for b in range(blocks):
        parts = [rows_ref[c, pl.ds(b, pulses, stride=pitch), :] for c in range(2)]
        turned.append(jnp.concatenate(parts, axis=1).astype(jnp.bfloat16))
    turned.append(carry[...])
    current = jnp.concatenate(turned[:-1], axis=0)
    after = jnp.concatenate(turned[1:], axis=0)
    total = jnp.dot(
        jnp.concatenate([current, after], axis=1),
        weights[...],
        preferred_element_type=jnp.float32,
    ).astype(jnp.bfloat16)
    carry[...] = turned[0]
    edge_out[...] = turned[0]

    def block(b):
        return total[b * pulses : (b + 1) * pulses]

    if near_chain:
        for side in range(2):

            @pl.when(own_u == side)
            def _(side=side):
                for b in range(blocks):
                    ref = keep_ref if b // tile == side else send_ref
                    ref[spot_h, spot_v, spot_m, b % tile] = block(b)
    else:
        for ref, mine in ((keep_ref, 0), (send_ref, 1)):

            @pl.when(spot_v == mine)
            def _(ref=ref):
                for b in range(blocks):
                    ref[spot_h, spot_m, b // tile ^ own_u, b % tile] = block(b)


def compress(chirp, edge, echoes, high, mids, near_chain, far, first_high):
    pulses, blocks, width = echoes.shape
    half = width // 2
    tile = blocks // lax.axis_size("turn")
    if near_chain:
        shape = (high, 2, mids, tile, pulses, width)
    else:
        shape = (high, mids, 2, tile, pulses, width)
    spec = pl.BlockSpec(shape, lambda h, v, m: (0, 0, 0, 0, 0, 0))
    edge_spec = pl.BlockSpec((pulses, width), lambda h, v, m: (0, 0))

    def chunk(h, v, m):
        return 0, ((first_high + high - 1 - h) * 2 + 1 - v) * mids + mids - 1 - m, 0

    in_specs = [
        pl.BlockSpec((2, half), lambda h, v, m: (0, 0)),
        pl.BlockSpec((pulses, 2 * tile, width), chunk),
    ]
    operands = [chirp, echoes]
    if edge is not None:
        in_specs.append(edge_spec)
        operands.append(edge)
    dims = (tile, pulses, half, near_chain, far)
    return pl.pallas_call(
        functools.partial(compress_kernel, dims, edge is not None),
        grid=(high, 2, mids),
        in_specs=in_specs,
        out_specs=[spec, spec, edge_spec],
        out_shape=[
            jax.ShapeDtypeStruct(s, jnp.bfloat16) for s in (shape, shape, (pulses, width))
        ],
        scratch_shapes=[
            pltpu.VMEM((2 * width, width), jnp.bfloat16),
            pltpu.VMEM((2, pulses * (2 * tile + 1), half), jnp.float32),
            pltpu.VMEM((pulses, width), jnp.bfloat16),
        ],
        compiler_params=pltpu.CompilerParams(
            vmem_limit_bytes=VMEM_BYTES if near_chain else 20 * 2**20
        ),
        cost_estimate=pl.CostEstimate(
            flops=2 * pulses * blocks * width * width,
            bytes_accessed=2 * pulses * blocks * width,
            transcendentals=0,
        ),
        name="compress",
    )(*operands)


def image_kernel(dims, data_ref, steer_ref, interp_ref, base_ref, step_ref, out_keep, out_send):
    leaf, each, half, beams, levels = dims
    rows = beams // leaf
    pair = 2
    piece = rows

    def turned(phase, re, im):
        c, s = phase
        return c * re - s * im, c * im + s * re

    bases = []
    for n in range(2 * levels):
        bases.append(jnp.broadcast_to(base_ref[0, n : n + 1, :], (half, beams)).T)

    def phased(level, block, first, re, im):
        cut = slice(first, first + piece)
        lanes = slice(block * half, (block + 1) * half)
        phase = turned(
            (bases[2 * level][cut], bases[2 * level + 1][cut]),
            step_ref[level, 0, cut, lanes],
            step_ref[level, 1, cut, lanes],
        )
        return turned(phase, re, im)

    for at in range(0, each, pair):
        parts = []
        for n in range(2):
            for c in range(2):
                cols = slice(c * half, (c + 1) * half)
                parts.append(
                    jnp.concatenate([data_ref[n, 0, at + i, :, cols] for i in range(pair)], axis=1)
                )
        raw = jnp.dot(
            steer_ref[...], jnp.concatenate(parts, axis=0), preferred_element_type=jnp.float32
        )
        re, im = raw[:beams], raw[beams:]
        for level in range(levels):
            columns = []
            for i in range(pair):
                lanes = slice(i * half, (i + 1) * half)
                pieces = []
                for first in range(0, beams, piece):
                    cut = slice(first, first + piece)
                    both = phased(level, at + i, first, re[cut, lanes], im[cut, lanes])
                    if level == levels - 1:
                        both = jnp.concatenate(both, axis=1)
                        g = first // rows
                        if g < leaf // 2:
                            out_keep[g, 0, at + i] = both
                        else:
                            out_send[g - leaf // 2, 0, at + i] = both.astype(jnp.bfloat16)
                        continue
                    pieces.append(jnp.concatenate(both, axis=1).astype(jnp.bfloat16))
                if pieces:
                    columns.append(jnp.concatenate(pieces, axis=0))
            if columns:
                moved = jnp.dot(
                    interp_ref[level],
                    jnp.concatenate(columns, axis=1),
                    preferred_element_type=jnp.float32,
                )
                cuts = [moved[:, n * half : (n + 1) * half] for n in range(2 * pair)]
                re = jnp.concatenate(cuts[0::2], axis=1)
                im = jnp.concatenate(cuts[1::2], axis=1)


def backproject(data, steer, interp, base, step, leaf):
    _, count, each, pulses, width = data.shape
    half = width // 2
    beams = steer.shape[0] // 2
    rows = beams // leaf
    shape = (leaf // 2, count, each, rows, width)

    def block(n):
        return n % (count // 2) * 2 + n // (count // 2)

    out_spec = pl.BlockSpec((leaf // 2, 1) + shape[2:], lambda n: (0, n, 0, 0, 0))
    return pl.pallas_call(
        functools.partial(image_kernel, (leaf, each, half, beams, bits_of(leaf))),
        grid=(count,),
        in_specs=[
            pl.BlockSpec((2, 1, each, pulses, width), lambda n: (0, block(n), 0, 0, 0)),
            pl.BlockSpec(steer.shape, lambda n: (0, 0)),
            pl.BlockSpec(interp.shape, lambda n: (0, 0, 0)),
            pl.BlockSpec((1,) + base.shape[1:], lambda n: (block(n), 0, 0)),
            pl.BlockSpec(step.shape, lambda n: (0, 0, 0, 0)),
        ],
        out_specs=[out_spec, out_spec],
        out_shape=[
            jax.ShapeDtypeStruct(shape, jnp.float32),
            jax.ShapeDtypeStruct(shape, jnp.bfloat16),
        ],
        compiler_params=pltpu.CompilerParams(vmem_limit_bytes=10 * 2**20),
        cost_estimate=pl.CostEstimate(
            flops=12 * beams * pulses * count * each * width,
            bytes_accessed=2 * data.size + 6 * count * each * beams * width // 2,
            transcendentals=0,
        ),
        name="image",
    )(data, steer, interp, base, step)


def fold(keep, got):
    stay, gone = (keep[:, n] + got[:, n].astype(jnp.float32) for n in range(2))
    return stay, gone.astype(jnp.bfloat16)


def last_kernel(keep_ref, got_ref, out_ref, rows_ref):
    blocks, rows, width = keep_ref.shape
    for i in range(blocks):
        value = keep_ref[i] + got_ref[i].astype(jnp.float32)
        for c in range(2):
            cols = slice(c * width // 2, (c + 1) * width // 2)
            rows_ref[c, pl.ds(i, rows, stride=blocks), :] = value[:, cols]
    both = jnp.concatenate([rows_ref[0], rows_ref[1]], axis=1)
    out_ref[...] = both.reshape(rows, blocks, width).astype(jnp.bfloat16)


def last_sum(keep, got):
    blocks, rows, width = keep.shape
    return pl.pallas_call(
        last_kernel,
        out_shape=jax.ShapeDtypeStruct((rows, blocks, width), jnp.bfloat16),
        scratch_shapes=[pltpu.VMEM((2, rows * blocks, width // 2), jnp.float32)],
        compiler_params=pltpu.CompilerParams(vmem_limit_bytes=8 * 2**20),
        name="last_sum",
    )(keep, got)


def interpolation(taps, beams):
    cells = jnp.arange(beams, dtype=jnp.int32)
    weights = jnp.array(WEIGHTS, jnp.float32)
    picks = taps[..., None] == cells
    return jnp.where(picks, weights[:, None], 0.0).sum(axis=-2)


def steering(slots, matrix, side, beams, pulses, scale):
    count = slots.shape[0]
    beam = jnp.arange(beams, dtype=jnp.int32)[:, None, None]
    place = jnp.arange(pulses, dtype=jnp.int32)
    slot = slots[None, :, None]
    cos, sin = unit(
        (2 * beam + 1 - beams) * (2 * place + 1 - pulses)
        + 3 * (beam + 1) * (2 * slot + 1) * (2 * place + 1),
        8 * pulses,
    )
    pair = jnp.concatenate([cos * scale, sin * scale], axis=2).astype(jnp.bfloat16)
    moved = jnp.dot(
        matrix.astype(jnp.bfloat16),
        pair.reshape(beams, count * 2 * pulses),
        preferred_element_type=jnp.float32,
    ).reshape(beams, count, 2 * pulses)
    re, im = moved[:, :, :pulses], moved[:, :, pulses:]
    row = jnp.arange(beams, dtype=jnp.int32)
    c, s = (t[:, None, None] for t in unit(row * row * (side + 1), PERIOD))
    re, im = c * re - s * im, c * im + s * re
    top = jnp.concatenate([re, -im], axis=2)
    low = jnp.concatenate([im, re], axis=2)
    return jnp.concatenate([top, low], axis=0).astype(jnp.bfloat16)


def per_device(echoes, chirp, taps, slots):
    leaf, turn = lax.axis_size("leaf"), lax.axis_size("turn")
    pulses, blocks, width = echoes.shape
    half = width // 2
    beams = taps.shape[2]
    levels = bits_of(leaf)
    far = (bits_of(turn) + 1) // 2 - 1
    top = bits_of(turn) - 1
    mids = 1 << far - 1
    high = turn >> far + 2
    tile = blocks // turn
    each = tile // 2
    rows = beams // leaf
    own_leaf, own_turn = lax.axis_index("leaf"), lax.axis_index("turn")

    keep_y, send_y, edge = compress(chirp, None, echoes, high, mids, True, far, high)
    got_y = swapped(send_y, "turn", 0)
    keep_z, send_z, _ = compress(chirp, edge, echoes, high, mids, False, far, 0)
    got_z = swapped(send_z, "turn", far)

    own_sides = [bit(own_leaf, level) for level in range(levels)]
    row = jnp.arange(beams, dtype=jnp.int32)
    part, place = row // rows, row % rows
    group = own_leaf ^ (2 * (part % (leaf // 2)) + part // (leaf // 2))
    orders = [row] * (levels - 1) + [group * rows + place]
    own_taps = [
        lax.dynamic_index_in_dim(taps[n], own_sides[n], 0, False) for n in range(levels)
    ]
    groups = own_taps[-1].reshape(leaf, rows, -1)
    own_taps[-1] = jnp.concatenate(
        [
            lax.dynamic_index_in_dim(groups, own_leaf ^ (2 * g + side), 0, False)
            for side in range(2)
            for g in range(leaf // 2)
        ],
        axis=0,
    )
    matrices = interpolation(jnp.stack(own_taps), beams)
    interp = matrices[1:].astype(jnp.bfloat16)
    scale = 1.0 / math.sqrt(2.0 * slots.shape[1] * pulses)
    wanted = own_turn ^ jnp.array([0, 1, 1 << far], jnp.int32)
    picked = jnp.arange(slots.shape[1], dtype=jnp.int32) == wanted[:, None]
    own_slots = jnp.where(picked, slots, 0).sum(axis=1)
    steer = steering(own_slots, matrices[0], own_sides[0], beams, pulses, scale)
    steer_y = steer[:, :2].reshape(2 * beams, 4 * pulses)
    steer_z = jnp.concatenate([steer[:, :1], steer[:, 2:]], axis=1).reshape(2 * beams, 4 * pulses)

    leans = jnp.stack([2 * order + 1 - beams for order in orders])
    bins = jnp.arange(each * half, dtype=jnp.int32) + 1
    slopes = jnp.stack([(2 * own_sides[n] - 1) * (n + 2) for n in range(levels)])[:, None] * leans
    step = jnp.stack(unit(slopes[:, :, None] * bins, PERIOD), axis=1)
    squares = jnp.stack(
        [orders[n] * orders[n] * (own_sides[n] + 1) * (1 if n else 0) for n in range(levels)]
    )

    def bases(tiles):
        parts = (2 * tiles[:, None] + jnp.arange(2, dtype=jnp.int32)).reshape(-1)
        start = (parts * each * half)[:, None, None]
        both = jnp.stack(unit(slopes * start + squares, PERIOD), axis=2)
        return both.reshape(parts.shape[0], 2 * levels, beams)

    index = jnp.arange(turn // 4, dtype=jnp.int32)
    tiles_y = turn // 2 + 2 * (index ^ (own_turn >> 1 & turn // 4 - 1)) + bit(own_turn, 0)
    low_part = (index ^ own_turn) & (1 << far) - 1
    high_part = index >> far ^ (own_turn >> far + 1 & high - 1)
    tiles_z = (high_part * 2 + bit(own_turn, far)) * (1 << far) + low_part

    pieces = []
    for name, keep, got, steer_own, tiles in (
        ("y", keep_y, got_y, steer_y, tiles_y),
        ("z", keep_z, got_z, steer_z, tiles_z),
    ):
        shape = (turn // 2, each, pulses, width)
        data = jnp.stack([keep.reshape(shape), got.reshape(shape)])
        kept, sent = backproject(data, steer_own, interp, bases(tiles), step, leaf)
        gone = 0 if name == "y" else far
        arrived = swapped(sent, "leaf", 0)
        parts = (leaf // 2, 2, turn // 4, each, rows, width)
        kept, arrived = kept.reshape(parts), arrived.reshape(parts)
        pieces.append([(kept[:, n], arrived[:, n], gone) for n in range(2)])

    final = [[], []]
    for n in range(2):
        for chain in range(2):
            kept, arrived, gone = pieces[chain][n]
            leading = [("leaf", b) for b in range(levels - 1, 0, -1)]
            leading += [("turn", b) for b in range(top - 1, -1, -1) if b != gone]
            order = [("leaf", b) for b in range(1, levels)]
            rest = [("turn", b) for b in range(top) if b not in (0, far)]
            order = [("turn", 0)] + order if gone else order + [("turn", far)]
            for axis, b in order + rest:
                at = leading.index((axis, b))
                before, after = 1 << at, (1 << len(leading) - at - 1) * each
                leading.pop(at)
                split = (before, 2, after, rows, width)
                kept, sent = fold(kept.reshape(split), arrived.reshape(split))
                arrived = swapped(sent, axis, b)
            shape = (each, rows, width)
            total = kept.reshape(shape) + arrived.reshape(shape).astype(jnp.float32)
            final[n].append(total)
    upper = bit(own_turn, top) == 1
    sent = jnp.stack([jnp.where(upper, second, first) for first, second in final])
    kept = jnp.stack([jnp.where(upper, first, second) for first, second in final])
    shape = (tile, rows, width)
    got = swapped(sent.astype(jnp.bfloat16), "turn", top)
    return last_sum(kept.reshape(shape), got.reshape(shape))


def solution(mesh):
    placed = (P(("leaf", "turn"), None, None), P(), P(), P("leaf", None))
    return jax.shard_map(
        per_device, mesh=mesh, in_specs=placed, out_specs=P("leaf", "turn", None), check_vma=False
    )
```

```python
import functools
import math

import jax
import jax.numpy as jnp
from jax import lax
from jax.experimental import pallas as pl
from jax.experimental.pallas import tpu as pltpu
from jax.sharding import PartitionSpec as P

WEIGHTS = (-1.0 / 32, 3.0 / 32, -7.0 / 32, 21.0 / 32, 21.0 / 32, -7.0 / 32, 3.0 / 32, -1.0 / 32)
PERIOD = 4096
VMEM_BYTES = 56 * 2**20


def bits_of(count):
    return count.bit_length() - 1


def bit(value, at):
    return value >> at & 1


def swapped(array, axis, bit):
    return lax.ppermute(array, axis, [(i, i ^ 1 << bit) for i in range(lax.axis_size(axis))])


def unit(phase_int, period):
    angle = jnp.remainder(phase_int, period).astype(jnp.float32) * (2.0 * math.pi / period)
    return jnp.cos(angle), jnp.sin(angle)


def compress_kernel(dims, has_edge, chirp_ref, echo_ref, *refs):
    tile, pulses, half, near_chain, far = dims
    edge_ref, refs = (refs[0], refs[1:]) if has_edge else (None, refs)
    keep_ref, send_ref, weights, rows_ref, carry = refs
    blocks = 2 * tile
    pitch = blocks + 1
    mids = pl.num_programs(2)
    high = pl.num_programs(0)
    turn = lax.axis_index("turn")
    spot_h = (high - 1 - pl.program_id(0)) ^ (turn >> far + 1 & high - 1)
    spot_m = (mids - 1 - pl.program_id(2)) ^ (turn >> 1 & mids - 1)
    spot_v = (1 - pl.program_id(1)) ^ bit(turn, far)
    own_u = bit(turn, 0)

    @pl.when((pl.program_id(0) == 0) & (pl.program_id(1) == 0) & (pl.program_id(2) == 0))
    def _():
        rows = lax.broadcasted_iota(jnp.int32, (half, half), 0)
        cols = lax.broadcasted_iota(jnp.int32, (half, half), 1)
        taps = chirp_ref[...].astype(jnp.float32)
        tables = []
        for c in range(2):
            wide = jnp.broadcast_to(taps[c : c + 1], (half, half))
            tables.append(pltpu.roll(wide, 0, 1, stride=1, stride_axis=0).T)
        for m, mask in enumerate((rows >= cols, rows < cols)):
            re, im = (jnp.where(mask, t, 0.0) for t in tables)
            top = jnp.concatenate([re, im], axis=1)
            low = jnp.concatenate([-im, re], axis=1)
            full = jnp.concatenate([top, low], axis=0)
            weights[m * 2 * half : (m + 1) * 2 * half, :] = full.astype(jnp.bfloat16)
        if has_edge:
            for p in range(pulses):
                for c in range(2):
                    first = edge_ref[p, :, c * half : (c + 1) * half].astype(jnp.float32)
                    rows_ref[c, p : p + 1, :] = first[:1]
            edges = [rows_ref[c, :pulses, :] for c in range(2)]
            carry[...] = jnp.concatenate(edges, axis=1).astype(jnp.bfloat16)
        else:
            carry[...] = jnp.zeros_like(carry)

    for p in range(pulses):
        for c in range(2):
            rows_ref[c, p * pitch : p * pitch + blocks, :] = echo_ref[
                p, :, c * half : (c + 1) * half
            ].astype(jnp.float32)
    turned = []
    for b in range(blocks):
        parts = [rows_ref[c, pl.ds(b, pulses, stride=pitch), :] for c in range(2)]
        turned.append(jnp.concatenate(parts, axis=1).astype(jnp.bfloat16))
    turned.append(carry[...])
    current = jnp.concatenate(turned[:-1], axis=0)
    after = jnp.concatenate(turned[1:], axis=0)
    total = jnp.dot(
        jnp.concatenate([current, after], axis=1),
        weights[...],
        preferred_element_type=jnp.float32,
    ).astype(jnp.bfloat16)
    carry[...] = turned[0]

    def block(b):
        return total[b * pulses : (b + 1) * pulses]

    if near_chain:
        for side in range(2):

            @pl.when(own_u == side)
            def _(side=side):
                for b in range(blocks):
                    ref = keep_ref if b // tile == side else send_ref
                    ref[0, 0, 0, b % tile] = block(b)
    else:
        for ref, mine in ((keep_ref, 0), (send_ref, 1)):

            @pl.when(spot_v == mine)
            def _(ref=ref):
                for b in range(blocks):
                    ref[spot_h, spot_m, b // tile ^ own_u, b % tile] = block(b)


def compress(chirp, echoes, high, mids, near_chain, far, first_high):
    pulses, blocks, width = echoes.shape
    half = width // 2
    tile = blocks // lax.axis_size("turn")
    if near_chain:
        shape = (high, 2, mids, tile, pulses, width)

        def place(h, v, m):
            turn = lax.axis_index("turn")
            spot_h = (high - 1 - h) ^ (turn >> far + 1 & high - 1)
            spot_m = (mids - 1 - m) ^ (turn >> 1 & mids - 1)
            return spot_h, (1 - v) ^ bit(turn, far), spot_m, 0, 0, 0

        spec = pl.BlockSpec((1, 1, 1) + shape[3:], place)
    else:
        shape = (high, mids, 2, tile, pulses, width)
        spec = pl.BlockSpec(shape, lambda h, v, m: (0, 0, 0, 0, 0, 0))
    def chunk(h, v, m):
        return 0, ((first_high + high - 1 - h) * 2 + 1 - v) * mids + mids - 1 - m, 0

    in_specs = [
        pl.BlockSpec((2, half), lambda h, v, m: (0, 0)),
        pl.BlockSpec((pulses, 2 * tile, width), chunk),
    ]
    operands = [chirp, echoes]
    has_edge = not near_chain
    if has_edge:
        after = (first_high + high) * 2 * mids
        in_specs.append(pl.BlockSpec((pulses, 2 * tile, width), lambda h, v, m: (0, after, 0)))
        operands.append(echoes)
    dims = (tile, pulses, half, near_chain, far)
    return pl.pallas_call(
        functools.partial(compress_kernel, dims, has_edge),
        grid=(high, 2, mids),
        in_specs=in_specs,
        out_specs=[spec, spec],
        out_shape=[jax.ShapeDtypeStruct(shape, jnp.bfloat16)] * 2,
        scratch_shapes=[
            pltpu.VMEM((2 * width, width), jnp.bfloat16),
            pltpu.VMEM((2, pulses * (2 * tile + 1), half), jnp.float32),
            pltpu.VMEM((pulses, width), jnp.bfloat16),
        ],
        compiler_params=pltpu.CompilerParams(
            vmem_limit_bytes=VMEM_BYTES if near_chain else 20 * 2**20
        ),
        cost_estimate=pl.CostEstimate(
            flops=2 * pulses * blocks * width * width,
            bytes_accessed=2 * pulses * blocks * width,
            transcendentals=0,
        ),
        name="compress",
    )(*operands)


def image_kernel(dims, data_ref, steer_ref, interp_ref, base_ref, step_ref, out_keep, out_send):
    leaf, each, half, beams, levels = dims
    rows = beams // leaf
    pair = 2
    piece = rows

    def turned(phase, re, im):
        c, s = phase
        return c * re - s * im, c * im + s * re

    bases = []
    for n in range(2 * levels):
        bases.append(jnp.broadcast_to(base_ref[0, n : n + 1, :], (half, beams)).T)

    def phased(level, block, first, re, im):
        cut = slice(first, first + piece)
        lanes = slice(block * half, (block + 1) * half)
        phase = turned(
            (bases[2 * level][cut], bases[2 * level + 1][cut]),
            step_ref[level, 0, cut, lanes],
            step_ref[level, 1, cut, lanes],
        )
        return turned(phase, re, im)

    for at in range(0, each, pair):
        parts = []
        for n in range(2):
            for c in range(2):
                cols = slice(c * half, (c + 1) * half)
                parts.append(
                    jnp.concatenate([data_ref[n, 0, at + i, :, cols] for i in range(pair)], axis=1)
                )
        raw = jnp.dot(
            steer_ref[...], jnp.concatenate(parts, axis=0), preferred_element_type=jnp.float32
        )
        re, im = raw[:beams], raw[beams:]
        for level in range(levels):
            columns = []
            for i in range(pair):
                lanes = slice(i * half, (i + 1) * half)
                pieces = []
                for first in range(0, beams, piece):
                    cut = slice(first, first + piece)
                    both = phased(level, at + i, first, re[cut, lanes], im[cut, lanes])
                    if level == levels - 1:
                        both = jnp.concatenate(both, axis=1)
                        g = first // rows
                        if g < leaf // 2:
                            out_keep[g, 0, at + i] = both
                        else:
                            out_send[g - leaf // 2, 0, at + i] = both.astype(jnp.bfloat16)
                        continue
                    both = jnp.concatenate(both, axis=1)
                    big = both.astype(jnp.bfloat16)
                    low = (both - big.astype(jnp.float32)).astype(jnp.bfloat16)
                    pieces.append((big, low))
                if pieces:
                    columns.append(
                        jnp.concatenate([p[0] for p in pieces] + [p[1] for p in pieces], axis=0)
                    )
            if columns:
                moved = jnp.dot(
                    interp_ref[level],
                    jnp.concatenate(columns, axis=1),
                    preferred_element_type=jnp.float32,
                )
                cuts = [moved[:, n * half : (n + 1) * half] for n in range(2 * pair)]
                re = jnp.concatenate(cuts[0::2], axis=1)
                im = jnp.concatenate(cuts[1::2], axis=1)


def backproject(data, steer, interp, base, step, leaf):
    _, count, each, pulses, width = data.shape
    half = width // 2
    beams = steer.shape[0] // 2
    rows = beams // leaf
    shape = (leaf // 2, count, each, rows, width)

    def block(n):
        return n % (count // 2) * 2 + n // (count // 2)

    out_spec = pl.BlockSpec((leaf // 2, 1) + shape[2:], lambda n: (0, n, 0, 0, 0))
    return pl.pallas_call(
        functools.partial(image_kernel, (leaf, each, half, beams, bits_of(leaf))),
        grid=(count,),
        in_specs=[
            pl.BlockSpec((2, 1, each, pulses, width), lambda n: (0, block(n), 0, 0, 0)),
            pl.BlockSpec(steer.shape, lambda n: (0, 0)),
            pl.BlockSpec(interp.shape, lambda n: (0, 0, 0)),
            pl.BlockSpec((1,) + base.shape[1:], lambda n: (block(n), 0, 0)),
            pl.BlockSpec(step.shape, lambda n: (0, 0, 0, 0)),
        ],
        out_specs=[out_spec, out_spec],
        out_shape=[
            jax.ShapeDtypeStruct(shape, jnp.float32),
            jax.ShapeDtypeStruct(shape, jnp.bfloat16),
        ],
        compiler_params=pltpu.CompilerParams(vmem_limit_bytes=10 * 2**20),
        cost_estimate=pl.CostEstimate(
            flops=12 * beams * pulses * count * each * width,
            bytes_accessed=2 * data.size + 6 * count * each * beams * width // 2,
            transcendentals=0,
        ),
        name="image",
    )(data, steer, interp, base, step)


def fold(keep, got):
    stay, gone = (keep[:, n] + got[:, n].astype(jnp.float32) for n in range(2))
    return stay, gone.astype(jnp.bfloat16)


def last_kernel(keep_ref, got_ref, out_ref, rows_ref):
    blocks, rows, width = keep_ref.shape
    for i in range(blocks):
        value = keep_ref[i] + got_ref[i].astype(jnp.float32)
        for c in range(2):
            cols = slice(c * width // 2, (c + 1) * width // 2)
            rows_ref[c, pl.ds(i, rows, stride=blocks), :] = value[:, cols]
    both = jnp.concatenate([rows_ref[0], rows_ref[1]], axis=1)
    out_ref[...] = both.reshape(rows, blocks, width).astype(jnp.bfloat16)


def last_sum(keep, got):
    blocks, rows, width = keep.shape
    return pl.pallas_call(
        last_kernel,
        out_shape=jax.ShapeDtypeStruct((rows, blocks, width), jnp.bfloat16),
        scratch_shapes=[pltpu.VMEM((2, rows * blocks, width // 2), jnp.float32)],
        compiler_params=pltpu.CompilerParams(vmem_limit_bytes=8 * 2**20),
        name="last_sum",
    )(keep, got)


def interpolation(taps, beams):
    cells = jnp.arange(beams, dtype=jnp.int32)
    weights = jnp.array(WEIGHTS, jnp.float32)
    picks = taps[..., None] == cells
    return jnp.where(picks, weights[:, None], 0.0).sum(axis=-2)


def steering(slots, matrix, side, beams, pulses, scale):
    count = slots.shape[0]
    beam = jnp.arange(beams, dtype=jnp.int32)[:, None, None]
    place = jnp.arange(pulses, dtype=jnp.int32)
    slot = slots[None, :, None]
    cos, sin = unit(
        (2 * beam + 1 - beams) * (2 * place + 1 - pulses)
        + 3 * (beam + 1) * (2 * slot + 1) * (2 * place + 1),
        8 * pulses,
    )
    pair = jnp.concatenate([cos * scale, sin * scale], axis=2).astype(jnp.bfloat16)
    moved = jnp.dot(
        matrix.astype(jnp.bfloat16),
        pair.reshape(beams, count * 2 * pulses),
        preferred_element_type=jnp.float32,
    ).reshape(beams, count, 2 * pulses)
    re, im = moved[:, :, :pulses], moved[:, :, pulses:]
    row = jnp.arange(beams, dtype=jnp.int32)
    c, s = (t[:, None, None] for t in unit(row * row * (side + 1), PERIOD))
    re, im = c * re - s * im, c * im + s * re
    top = jnp.concatenate([re, -im], axis=2)
    low = jnp.concatenate([im, re], axis=2)
    return jnp.concatenate([top, low], axis=0).astype(jnp.bfloat16)


def per_device(echoes, chirp, taps, slots):
    leaf, turn = lax.axis_size("leaf"), lax.axis_size("turn")
    pulses, blocks, width = echoes.shape
    half = width // 2
    beams = taps.shape[2]
    levels = bits_of(leaf)
    far = (bits_of(turn) + 1) // 2 - 1
    top = bits_of(turn) - 1
    mids = 1 << far - 1
    high = turn >> far + 2
    tile = blocks // turn
    each = tile // 2
    rows = beams // leaf
    own_leaf, own_turn = lax.axis_index("leaf"), lax.axis_index("turn")

    keep_y, send_y = compress(chirp, echoes, high, mids, True, far, high)
    got_y = swapped(send_y, "turn", 0)
    keep_z, send_z = compress(chirp, echoes, high, mids, False, far, 0)
    got_z = swapped(send_z, "turn", far)

    own_sides = [bit(own_leaf, level) for level in range(levels)]
    row = jnp.arange(beams, dtype=jnp.int32)
    part, place = row // rows, row % rows
    group = own_leaf ^ (2 * (part % (leaf // 2)) + part // (leaf // 2))
    orders = [row] * (levels - 1) + [group * rows + place]
    own_taps = [
        lax.dynamic_index_in_dim(taps[n], own_sides[n], 0, False) for n in range(levels)
    ]
    groups = own_taps[-1].reshape(leaf, rows, -1)
    own_taps[-1] = jnp.concatenate(
        [
            lax.dynamic_index_in_dim(groups, own_leaf ^ (2 * g + side), 0, False)
            for side in range(2)
            for g in range(leaf // 2)
        ],
        axis=0,
    )
    matrices = interpolation(jnp.stack(own_taps), beams)
    interp = jnp.concatenate([matrices[1:]] * 2, axis=-1).astype(jnp.bfloat16)
    scale = 1.0 / math.sqrt(2.0 * slots.shape[1] * pulses)
    wanted = own_turn ^ jnp.array([0, 1, 1 << far], jnp.int32)
    picked = jnp.arange(slots.shape[1], dtype=jnp.int32) == wanted[:, None]
    own_slots = jnp.where(picked, slots, 0).sum(axis=1)
    steer = steering(own_slots, matrices[0], own_sides[0], beams, pulses, scale)
    steer_y = steer[:, :2].reshape(2 * beams, 4 * pulses)
    steer_z = jnp.concatenate([steer[:, :1], steer[:, 2:]], axis=1).reshape(2 * beams, 4 * pulses)

    leans = jnp.stack([2 * order + 1 - beams for order in orders])
    bins = jnp.arange(each * half, dtype=jnp.int32) + 1
    slopes = jnp.stack([(2 * own_sides[n] - 1) * (n + 2) for n in range(levels)])[:, None] * leans
    step = jnp.stack(unit(slopes[:, :, None] * bins, PERIOD), axis=1)
    squares = jnp.stack(
        [orders[n] * orders[n] * (own_sides[n] + 1) * (1 if n else 0) for n in range(levels)]
    )

    def bases(tiles):
        parts = (2 * tiles[:, None] + jnp.arange(2, dtype=jnp.int32)).reshape(-1)
        start = (parts * each * half)[:, None, None]
        both = jnp.stack(unit(slopes * start + squares, PERIOD), axis=2)
        return both.reshape(parts.shape[0], 2 * levels, beams)

    index = jnp.arange(turn // 4, dtype=jnp.int32)
    tiles_y = turn // 2 + 2 * (index ^ (own_turn >> 1 & turn // 4 - 1)) + bit(own_turn, 0)
    low_part = (index ^ own_turn) & (1 << far) - 1
    high_part = index >> far ^ (own_turn >> far + 1 & high - 1)
    tiles_z = (high_part * 2 + bit(own_turn, far)) * (1 << far) + low_part

    pieces = []
    for name, keep, got, steer_own, tiles in (
        ("y", keep_y, got_y, steer_y, tiles_y),
        ("z", keep_z, got_z, steer_z, tiles_z),
    ):
        shape = (turn // 2, each, pulses, width)
        data = jnp.stack([keep.reshape(shape), got.reshape(shape)])
        kept, sent = backproject(data, steer_own, interp, bases(tiles), step, leaf)
        gone = 0 if name == "y" else far
        arrived = swapped(sent, "leaf", 0)
        parts = (leaf // 2, 2, turn // 4, each, rows, width)
        kept, arrived = kept.reshape(parts), arrived.reshape(parts)
        pieces.append([(kept[:, n], arrived[:, n], gone) for n in range(2)])

    final = [[], []]
    for n in range(2):
        for chain in range(2):
            kept, arrived, gone = pieces[chain][n]
            leading = [("leaf", b) for b in range(levels - 1, 0, -1)]
            leading += [("turn", b) for b in range(top - 1, -1, -1) if b != gone]
            order = [("leaf", b) for b in range(1, levels)]
            rest = [("turn", b) for b in range(top) if b not in (0, far)]
            order = [("turn", 0)] + order if gone else order + [("turn", far)]
            for axis, b in order + rest:
                at = leading.index((axis, b))
                before, after = 1 << at, (1 << len(leading) - at - 1) * each
                leading.pop(at)
                split = (before, 2, after, rows, width)
                kept, sent = fold(kept.reshape(split), arrived.reshape(split))
                arrived = swapped(sent, axis, b)
            shape = (each, rows, width)
            total = kept.reshape(shape) + arrived.reshape(shape).astype(jnp.float32)
            final[n].append(total)
    upper = bit(own_turn, top) == 1
    sent = jnp.stack([jnp.where(upper, second, first) for first, second in final])
    kept = jnp.stack([jnp.where(upper, first, second) for first, second in final])
    shape = (tile, rows, width)
    got = swapped(sent.astype(jnp.bfloat16), "turn", top)
    return last_sum(kept.reshape(shape), got.reshape(shape))


def solution(mesh):
    placed = (P(("leaf", "turn"), None, None), P(), P(), P("leaf", None))
    return jax.shard_map(
        per_device, mesh=mesh, in_specs=placed, out_specs=P("leaf", "turn", None), check_vma=False
    )
```

```python
import functools
import math

import jax
import jax.numpy as jnp
from jax import lax
from jax.experimental import pallas as pl
from jax.experimental.pallas import tpu as pltpu
from jax.sharding import PartitionSpec as P

WEIGHTS = (-1.0 / 32, 3.0 / 32, -7.0 / 32, 21.0 / 32, 21.0 / 32, -7.0 / 32, 3.0 / 32, -1.0 / 32)
PERIOD = 4096
VMEM_BYTES = 20 * 2**20


def bits_of(count):
    return count.bit_length() - 1


def bit(value, at):
    return value >> at & 1


def swapped(array, axis, bit):
    return lax.ppermute(array, axis, [(i, i ^ 1 << bit) for i in range(lax.axis_size(axis))])


def unit(phase_int, period):
    angle = jnp.remainder(phase_int, period).astype(jnp.float32) * (2.0 * math.pi / period)
    return jnp.cos(angle), jnp.sin(angle)


def compress_kernel(dims, has_edge, chirp_ref, echo_ref, *refs):
    tile, pulses, half, near_chain, far = dims
    edge_ref, refs = (refs[0], refs[1:]) if has_edge else (None, refs)
    keep_ref, send_ref, weights, rows_ref, carry = refs
    blocks = 2 * tile
    pitch = blocks + 1
    mids = pl.num_programs(2)
    high = pl.num_programs(0)
    turn = lax.axis_index("turn")
    spot_h = (high - 1 - pl.program_id(0)) ^ (turn >> far + 1 & high - 1)
    spot_m = (mids - 1 - pl.program_id(2)) ^ (turn >> 1 & mids - 1)
    spot_v = (1 - pl.program_id(1)) ^ bit(turn, far)
    own_u = bit(turn, 0)

    @pl.when((pl.program_id(0) == 0) & (pl.program_id(1) == 0) & (pl.program_id(2) == 0))
    def _():
        rows = lax.broadcasted_iota(jnp.int32, (half, half), 0)
        cols = lax.broadcasted_iota(jnp.int32, (half, half), 1)
        taps = chirp_ref[...]
        tables = []
        for c in range(2):
            wide = jnp.broadcast_to(taps[c : c + 1], (half, half))
            tables.append(pltpu.roll(wide, 0, 1, stride=1, stride_axis=0).T)
        for m, mask in enumerate((rows >= cols, rows < cols)):
            re, im = (jnp.where(mask, t, 0.0) for t in tables)
            top = jnp.concatenate([re, im], axis=1)
            low = jnp.concatenate([-im, re], axis=1)
            full = jnp.concatenate([top, low], axis=0)
            weights[m * 2 * half : (m + 1) * 2 * half, :] = full.astype(jnp.bfloat16)
        if has_edge:
            for p in range(pulses):
                for c in range(2):
                    first = edge_ref[p, :, c * half : (c + 1) * half].astype(jnp.float32)
                    rows_ref[c, p : p + 1, :] = first[:1]
            edges = [rows_ref[c, :pulses, :] for c in range(2)]
            carry[...] = jnp.concatenate(edges, axis=1).astype(jnp.bfloat16)
        else:
            carry[...] = jnp.zeros_like(carry)

    for p in range(pulses):
        for c in range(2):
            rows_ref[c, p * pitch : p * pitch + blocks, :] = echo_ref[
                p, :, c * half : (c + 1) * half
            ].astype(jnp.float32)
    turned = []
    for b in range(blocks):
        parts = [rows_ref[c, pl.ds(b, pulses, stride=pitch), :] for c in range(2)]
        turned.append(jnp.concatenate(parts, axis=1).astype(jnp.bfloat16))
    turned.append(carry[...])
    current = jnp.concatenate(turned[:-1], axis=0)
    after = jnp.concatenate(turned[1:], axis=0)
    total = jnp.dot(
        jnp.concatenate([current, after], axis=1),
        weights[...],
        preferred_element_type=jnp.float32,
    ).astype(jnp.bfloat16)
    carry[...] = turned[0]

    def block(b):
        return total[b * pulses : (b + 1) * pulses]

    if near_chain:
        for side in range(2):

            @pl.when(own_u == side)
            def _(side=side):
                for b in range(blocks):
                    ref = keep_ref if b // tile == side else send_ref
                    ref[0, 0, 0, b % tile] = block(b)
    else:
        for ref, mine in ((keep_ref, 0), (send_ref, 1)):

            @pl.when(spot_v == mine)
            def _(ref=ref):
                for b in range(blocks):
                    ref[spot_h, spot_m, b // tile ^ own_u, b % tile] = block(b)


def compress(chirp, echoes, high, mids, near_chain, far, first_high):
    pulses, blocks, width = echoes.shape
    half = width // 2
    tile = blocks // lax.axis_size("turn")
    if near_chain:
        shape = (high, 2, mids, tile, pulses, width)

        def place(h, v, m):
            turn = lax.axis_index("turn")
            spot_h = (high - 1 - h) ^ (turn >> far + 1 & high - 1)
            spot_m = (mids - 1 - m) ^ (turn >> 1 & mids - 1)
            return spot_h, (1 - v) ^ bit(turn, far), spot_m, 0, 0, 0

        spec = pl.BlockSpec((1, 1, 1) + shape[3:], place)
    else:
        shape = (high, mids, 2, tile, pulses, width)
        spec = pl.BlockSpec(shape, lambda h, v, m: (0, 0, 0, 0, 0, 0))
    def chunk(h, v, m):
        return 0, ((first_high + high - 1 - h) * 2 + 1 - v) * mids + mids - 1 - m, 0

    in_specs = [
        pl.BlockSpec((2, half), lambda h, v, m: (0, 0)),
        pl.BlockSpec((pulses, 2 * tile, width), chunk),
    ]
    operands = [chirp, echoes]
    has_edge = not near_chain
    if has_edge:
        after = (first_high + high) * 2 * mids
        in_specs.append(pl.BlockSpec((pulses, 2 * tile, width), lambda h, v, m: (0, after, 0)))
        operands.append(echoes)
    dims = (tile, pulses, half, near_chain, far)
    return pl.pallas_call(
        functools.partial(compress_kernel, dims, has_edge),
        grid=(high, 2, mids),
        in_specs=in_specs,
        out_specs=[spec, spec],
        out_shape=[jax.ShapeDtypeStruct(shape, jnp.bfloat16)] * 2,
        scratch_shapes=[
            pltpu.VMEM((2 * width, width), jnp.bfloat16),
            pltpu.VMEM((2, pulses * (2 * tile + 1), half), jnp.float32),
            pltpu.VMEM((pulses, width), jnp.bfloat16),
        ],
        compiler_params=pltpu.CompilerParams(vmem_limit_bytes=VMEM_BYTES),
        cost_estimate=pl.CostEstimate(
            flops=2 * pulses * blocks * width * width,
            bytes_accessed=2 * pulses * blocks * width,
            transcendentals=0,
        ),
        name="compress",
    )(*operands)


def image_kernel(dims, data_ref, steer_ref, interp_ref, base_ref, step_ref, out_keep, out_send):
    leaf, each, half, beams, levels = dims
    rows = beams // leaf
    pair = 2
    piece = rows

    def turned(phase, re, im):
        c, s = phase
        return c * re - s * im, c * im + s * re

    bases = []
    for n in range(2 * levels):
        bases.append(jnp.broadcast_to(base_ref[0, n : n + 1, :], (half, beams)).T)

    def phased(level, block, first, re, im):
        cut = slice(first, first + piece)
        lanes = slice(block * half, (block + 1) * half)
        phase = turned(
            (bases[2 * level][cut], bases[2 * level + 1][cut]),
            step_ref[level, 0, cut, lanes],
            step_ref[level, 1, cut, lanes],
        )
        return turned(phase, re, im)

    for at in range(0, each, pair):
        parts = []
        for n in range(2):
            for c in range(2):
                cols = slice(c * half, (c + 1) * half)
                parts.append(
                    jnp.concatenate([data_ref[n, 0, at + i, :, cols] for i in range(pair)], axis=1)
                )
        raw = jnp.dot(
            steer_ref[...], jnp.concatenate(parts, axis=0), preferred_element_type=jnp.float32
        )
        re, im = raw[:beams], raw[beams:]
        for level in range(levels):
            columns = []
            for i in range(pair):
                lanes = slice(i * half, (i + 1) * half)
                pieces = []
                for first in range(0, beams, piece):
                    cut = slice(first, first + piece)
                    both = phased(level, at + i, first, re[cut, lanes], im[cut, lanes])
                    if level == levels - 1:
                        both = jnp.concatenate(both, axis=1)
                        g = first // rows
                        if g < leaf // 2:
                            out_keep[g, 0, at + i] = both
                        else:
                            out_send[g - leaf // 2, 0, at + i] = both.astype(jnp.bfloat16)
                        continue
                    both = jnp.concatenate(both, axis=1)
                    big = both.astype(jnp.bfloat16)
                    low = (both - big.astype(jnp.float32)).astype(jnp.bfloat16)
                    pieces.append((big, low))
                if pieces:
                    columns.append(
                        jnp.concatenate([p[0] for p in pieces] + [p[1] for p in pieces], axis=0)
                    )
            if columns:
                moved = jnp.dot(
                    interp_ref[level],
                    jnp.concatenate(columns, axis=1),
                    preferred_element_type=jnp.float32,
                )
                cuts = [moved[:, n * half : (n + 1) * half] for n in range(2 * pair)]
                re = jnp.concatenate(cuts[0::2], axis=1)
                im = jnp.concatenate(cuts[1::2], axis=1)


def backproject(data, steer, interp, base, step, leaf):
    _, count, each, pulses, width = data.shape
    half = width // 2
    beams = steer.shape[0] // 2
    rows = beams // leaf
    shape = (leaf // 2, count, each, rows, width)

    def block(n):
        return n % (count // 2) * 2 + n // (count // 2)

    out_spec = pl.BlockSpec((leaf // 2, 1) + shape[2:], lambda n: (0, n, 0, 0, 0))
    return pl.pallas_call(
        functools.partial(image_kernel, (leaf, each, half, beams, bits_of(leaf))),
        grid=(count,),
        in_specs=[
            pl.BlockSpec((2, 1, each, pulses, width), lambda n: (0, block(n), 0, 0, 0)),
            pl.BlockSpec(steer.shape, lambda n: (0, 0)),
            pl.BlockSpec(interp.shape, lambda n: (0, 0, 0)),
            pl.BlockSpec((1,) + base.shape[1:], lambda n: (block(n), 0, 0)),
            pl.BlockSpec(step.shape, lambda n: (0, 0, 0, 0)),
        ],
        out_specs=[out_spec, out_spec],
        out_shape=[
            jax.ShapeDtypeStruct(shape, jnp.float32),
            jax.ShapeDtypeStruct(shape, jnp.bfloat16),
        ],
        compiler_params=pltpu.CompilerParams(vmem_limit_bytes=10 * 2**20),
        cost_estimate=pl.CostEstimate(
            flops=12 * beams * pulses * count * each * width,
            bytes_accessed=2 * data.size + 6 * count * each * beams * width // 2,
            transcendentals=0,
        ),
        name="image",
    )(data, steer, interp, base, step)


def fold(keep, got):
    stay, gone = (keep[:, n] + got[:, n].astype(jnp.float32) for n in range(2))
    return stay, gone.astype(jnp.bfloat16)


def last_kernel(keep_ref, got_ref, out_ref, rows_ref):
    blocks, rows, width = keep_ref.shape
    for i in range(blocks):
        value = keep_ref[i] + got_ref[i].astype(jnp.float32)
        for c in range(2):
            cols = slice(c * width // 2, (c + 1) * width // 2)
            rows_ref[c, pl.ds(i, rows, stride=blocks), :] = value[:, cols]
    both = jnp.concatenate([rows_ref[0], rows_ref[1]], axis=1)
    out_ref[...] = both.reshape(rows, blocks, width).astype(jnp.bfloat16)


def last_sum(keep, got):
    blocks, rows, width = keep.shape
    return pl.pallas_call(
        last_kernel,
        out_shape=jax.ShapeDtypeStruct((rows, blocks, width), jnp.bfloat16),
        scratch_shapes=[pltpu.VMEM((2, rows * blocks, width // 2), jnp.float32)],
        compiler_params=pltpu.CompilerParams(vmem_limit_bytes=8 * 2**20),
        name="last_sum",
    )(keep, got)


def interpolation(taps, beams):
    cells = jnp.arange(beams, dtype=jnp.int32)
    weights = jnp.array(WEIGHTS, jnp.float32)
    picks = taps[..., None] == cells
    return jnp.where(picks, weights[:, None], 0.0).sum(axis=-2)


def steering(slots, matrix, side, beams, pulses, scale):
    count = slots.shape[0]
    beam = jnp.arange(beams, dtype=jnp.int32)[:, None, None]
    place = jnp.arange(pulses, dtype=jnp.int32)
    slot = slots[None, :, None]
    cos, sin = unit(
        (2 * beam + 1 - beams) * (2 * place + 1 - pulses)
        + 3 * (beam + 1) * (2 * slot + 1) * (2 * place + 1),
        8 * pulses,
    )
    pair = jnp.concatenate([cos * scale, sin * scale], axis=2).astype(jnp.bfloat16)
    moved = jnp.dot(
        matrix.astype(jnp.bfloat16),
        pair.reshape(beams, count * 2 * pulses),
        preferred_element_type=jnp.float32,
    ).reshape(beams, count, 2 * pulses)
    re, im = moved[:, :, :pulses], moved[:, :, pulses:]
    row = jnp.arange(beams, dtype=jnp.int32)
    c, s = (t[:, None, None] for t in unit(row * row * (side + 1), PERIOD))
    re, im = c * re - s * im, c * im + s * re
    top = jnp.concatenate([re, -im], axis=2)
    low = jnp.concatenate([im, re], axis=2)
    return jnp.concatenate([top, low], axis=0).astype(jnp.bfloat16)


def per_device(echoes, chirp, taps, slots):
    leaf, turn = lax.axis_size("leaf"), lax.axis_size("turn")
    pulses, blocks, width = echoes.shape
    half = width // 2
    beams = taps.shape[2]
    levels = bits_of(leaf)
    far = (bits_of(turn) + 1) // 2 - 1
    top = bits_of(turn) - 1
    mids = 1 << far - 1
    high = turn >> far + 2
    tile = blocks // turn
    each = tile // 2
    rows = beams // leaf
    own_leaf, own_turn = lax.axis_index("leaf"), lax.axis_index("turn")

    chirp = chirp.astype(jnp.float32)
    keep_y, send_y = compress(chirp, echoes, high, mids, True, far, high)
    got_y = swapped(send_y, "turn", 0)
    keep_z, send_z = compress(chirp, echoes, high, mids, False, far, 0)
    got_z = swapped(send_z, "turn", far)

    own_sides = [bit(own_leaf, level) for level in range(levels)]
    row = jnp.arange(beams, dtype=jnp.int32)
    part, place = row // rows, row % rows
    group = own_leaf ^ (2 * (part % (leaf // 2)) + part // (leaf // 2))
    orders = [row] * (levels - 1) + [group * rows + place]
    own_taps = [
        lax.dynamic_index_in_dim(taps[n], own_sides[n], 0, False) for n in range(levels)
    ]
    groups = own_taps[-1].reshape(leaf, rows, -1)
    own_taps[-1] = jnp.concatenate(
        [
            lax.dynamic_index_in_dim(groups, own_leaf ^ (2 * g + side), 0, False)
            for side in range(2)
            for g in range(leaf // 2)
        ],
        axis=0,
    )
    matrices = interpolation(jnp.stack(own_taps), beams)
    interp = jnp.concatenate([matrices[1:]] * 2, axis=-1).astype(jnp.bfloat16)
    scale = 1.0 / math.sqrt(2.0 * slots.shape[1] * pulses)
    wanted = own_turn ^ jnp.array([0, 1, 1 << far], jnp.int32)
    picked = jnp.arange(slots.shape[1], dtype=jnp.int32) == wanted[:, None]
    own_slots = jnp.where(picked, slots, 0).sum(axis=1)
    steer = steering(own_slots, matrices[0], own_sides[0], beams, pulses, scale)
    steer_y = steer[:, :2].reshape(2 * beams, 4 * pulses)
    steer_z = jnp.concatenate([steer[:, :1], steer[:, 2:]], axis=1).reshape(2 * beams, 4 * pulses)

    leans = jnp.stack([2 * order + 1 - beams for order in orders])
    bins = jnp.arange(each * half, dtype=jnp.int32) + 1
    slopes = jnp.stack([(2 * own_sides[n] - 1) * (n + 2) for n in range(levels)])[:, None] * leans
    step = jnp.stack(unit(slopes[:, :, None] * bins, PERIOD), axis=1)
    squares = jnp.stack(
        [orders[n] * orders[n] * (own_sides[n] + 1) * (1 if n else 0) for n in range(levels)]
    )

    def bases(tiles):
        parts = (2 * tiles[:, None] + jnp.arange(2, dtype=jnp.int32)).reshape(-1)
        start = (parts * each * half)[:, None, None]
        both = jnp.stack(unit(slopes * start + squares, PERIOD), axis=2)
        return both.reshape(parts.shape[0], 2 * levels, beams)

    index = jnp.arange(turn // 4, dtype=jnp.int32)
    tiles_y = turn // 2 + 2 * (index ^ (own_turn >> 1 & turn // 4 - 1)) + bit(own_turn, 0)
    low_part = (index ^ own_turn) & (1 << far) - 1
    high_part = index >> far ^ (own_turn >> far + 1 & high - 1)
    tiles_z = (high_part * 2 + bit(own_turn, far)) * (1 << far) + low_part

    pieces = []
    for name, keep, got, steer_own, tiles in (
        ("y", keep_y, got_y, steer_y, tiles_y),
        ("z", keep_z, got_z, steer_z, tiles_z),
    ):
        shape = (turn // 2, each, pulses, width)
        data = jnp.stack([keep.reshape(shape), got.reshape(shape)])
        kept, sent = backproject(data, steer_own, interp, bases(tiles), step, leaf)
        gone = 0 if name == "y" else far
        arrived = swapped(sent, "leaf", 0)
        parts = (leaf // 2, 2, turn // 4, each, rows, width)
        kept, arrived = kept.reshape(parts), arrived.reshape(parts)
        pieces.append([(kept[:, n], arrived[:, n], gone) for n in range(2)])

    final = [[], []]
    for n in range(2):
        for chain in range(2):
            kept, arrived, gone = pieces[chain][n]
            leading = [("leaf", b) for b in range(levels - 1, 0, -1)]
            leading += [("turn", b) for b in range(top - 1, -1, -1) if b != gone]
            order = [("leaf", b) for b in range(1, levels)]
            rest = [("turn", b) for b in range(top) if b not in (0, far)]
            order = [("turn", 0)] + order if gone else order + [("turn", far)]
            for axis, b in order + rest:
                at = leading.index((axis, b))
                before, after = 1 << at, (1 << len(leading) - at - 1) * each
                leading.pop(at)
                split = (before, 2, after, rows, width)
                kept, sent = fold(kept.reshape(split), arrived.reshape(split))
                arrived = swapped(sent, axis, b)
            shape = (each, rows, width)
            total = kept.reshape(shape) + arrived.reshape(shape).astype(jnp.float32)
            final[n].append(total)
    upper = bit(own_turn, top) == 1
    sent = jnp.stack([jnp.where(upper, second, first) for first, second in final])
    kept = jnp.stack([jnp.where(upper, first, second) for first, second in final])
    shape = (tile, rows, width)
    got = swapped(sent.astype(jnp.bfloat16), "turn", top)
    return last_sum(kept.reshape(shape), got.reshape(shape))


def solution(mesh):
    placed = (P(("leaf", "turn"), None, None), P(), P(), P("leaf", None))
    return jax.shard_map(
        per_device, mesh=mesh, in_specs=placed, out_specs=P("leaf", "turn", None), check_vma=False
    )
```

```python
import functools
import math

import jax
import jax.numpy as jnp
from jax import lax
from jax.experimental import pallas as pl
from jax.experimental.pallas import tpu as pltpu
from jax.sharding import PartitionSpec as P

WEIGHTS = (-1.0 / 32, 3.0 / 32, -7.0 / 32, 21.0 / 32, 21.0 / 32, -7.0 / 32, 3.0 / 32, -1.0 / 32)
PERIOD = 4096
VMEM_BYTES = 56 * 2**20


def bits_of(count):
    return count.bit_length() - 1


def bit(value, at):
    return value >> at & 1


def swapped(array, axis, bit):
    return lax.ppermute(array, axis, [(i, i ^ 1 << bit) for i in range(lax.axis_size(axis))])


def unit(phase_int, period):
    angle = jnp.remainder(phase_int, period).astype(jnp.float32) * (2.0 * math.pi / period)
    return jnp.cos(angle), jnp.sin(angle)


def compress_kernel(dims, has_edge, chirp_ref, echo_ref, *refs):
    tile, pulses, half, near_chain, far = dims
    edge_ref, refs = (refs[0], refs[1:]) if has_edge else (None, refs)
    keep_ref, send_ref, weights, rows_ref, carry = refs
    blocks = 2 * tile
    pitch = blocks + 1
    mids = pl.num_programs(2)
    high = pl.num_programs(0)
    turn = lax.axis_index("turn")
    spot_h = (high - 1 - pl.program_id(0)) ^ (turn >> far + 1 & high - 1)
    spot_m = (mids - 1 - pl.program_id(2)) ^ (turn >> 1 & mids - 1)
    spot_v = (1 - pl.program_id(1)) ^ bit(turn, far)
    own_u = bit(turn, 0)

    @pl.when((pl.program_id(0) == 0) & (pl.program_id(1) == 0) & (pl.program_id(2) == 0))
    def _():
        rows = lax.broadcasted_iota(jnp.int32, (half, half), 0)
        cols = lax.broadcasted_iota(jnp.int32, (half, half), 1)
        taps = chirp_ref[...].astype(jnp.float32)
        tables = []
        for c in range(2):
            wide = jnp.broadcast_to(taps[c : c + 1], (half, half))
            tables.append(pltpu.roll(wide, 0, 1, stride=1, stride_axis=0).T)
        for m, mask in enumerate((rows >= cols, rows < cols)):
            re, im = (jnp.where(mask, t, 0.0) for t in tables)
            top = jnp.concatenate([re, im], axis=1)
            low = jnp.concatenate([-im, re], axis=1)
            full = jnp.concatenate([top, low], axis=0)
            weights[m * 2 * half : (m + 1) * 2 * half, :] = full.astype(jnp.bfloat16)
        if has_edge:
            for p in range(pulses):
                for c in range(2):
                    first = edge_ref[p, :, c * half : (c + 1) * half].astype(jnp.float32)
                    rows_ref[c, p : p + 1, :] = first[:1]
            edges = [rows_ref[c, :pulses, :] for c in range(2)]
            carry[...] = jnp.concatenate(edges, axis=1).astype(jnp.bfloat16)
        else:
            carry[...] = jnp.zeros_like(carry)

    for p in range(pulses):
        for c in range(2):
            rows_ref[c, p * pitch : p * pitch + blocks, :] = echo_ref[
                p, :, c * half : (c + 1) * half
            ].astype(jnp.float32)
    turned = []
    for b in range(blocks):
        parts = [rows_ref[c, pl.ds(b, pulses, stride=pitch), :] for c in range(2)]
        turned.append(jnp.concatenate(parts, axis=1).astype(jnp.bfloat16))
    turned.append(carry[...])
    current = jnp.concatenate(turned[:-1], axis=0)
    after = jnp.concatenate(turned[1:], axis=0)
    total = jnp.dot(
        jnp.concatenate([current, after], axis=1),
        weights[...],
        preferred_element_type=jnp.float32,
    ).astype(jnp.bfloat16)
    carry[...] = turned[0]

    def block(b):
        return total[b * pulses : (b + 1) * pulses]

    if near_chain:
        for side in range(2):

            @pl.when(own_u == side)
            def _(side=side):
                for b in range(blocks):
                    ref = keep_ref if b // tile == side else send_ref
                    ref[0, 0, 0, b % tile] = block(b)
    else:
        for ref, mine in ((keep_ref, 0), (send_ref, 1)):

            @pl.when(spot_v == mine)
            def _(ref=ref):
                for b in range(blocks):
                    ref[spot_h, spot_m, b // tile ^ own_u, b % tile] = block(b)


def compress(chirp, echoes, high, mids, near_chain, far, first_high):
    pulses, blocks, width = echoes.shape
    half = width // 2
    tile = blocks // lax.axis_size("turn")
    if near_chain:
        shape = (high, 2, mids, tile, pulses, width)

        def place(h, v, m):
            turn = lax.axis_index("turn")
            spot_h = (high - 1 - h) ^ (turn >> far + 1 & high - 1)
            spot_m = (mids - 1 - m) ^ (turn >> 1 & mids - 1)
            return spot_h, (1 - v) ^ bit(turn, far), spot_m, 0, 0, 0

        spec = pl.BlockSpec((1, 1, 1) + shape[3:], place)
    else:
        shape = (high, mids, 2, tile, pulses, width)
        spec = pl.BlockSpec(shape, lambda h, v, m: (0, 0, 0, 0, 0, 0))
    def chunk(h, v, m):
        return 0, ((first_high + high - 1 - h) * 2 + 1 - v) * mids + mids - 1 - m, 0

    in_specs = [
        pl.BlockSpec((2, half), lambda h, v, m: (0, 0)),
        pl.BlockSpec((pulses, 2 * tile, width), chunk),
    ]
    operands = [chirp, echoes]
    has_edge = not near_chain
    if has_edge:
        after = (first_high + high) * 2 * mids
        in_specs.append(pl.BlockSpec((pulses, 2 * tile, width), lambda h, v, m: (0, after, 0)))
        operands.append(echoes)
    dims = (tile, pulses, half, near_chain, far)
    return pl.pallas_call(
        functools.partial(compress_kernel, dims, has_edge),
        grid=(high, 2, mids),
        in_specs=in_specs,
        out_specs=[spec, spec],
        out_shape=[jax.ShapeDtypeStruct(shape, jnp.bfloat16)] * 2,
        scratch_shapes=[
            pltpu.VMEM((2 * width, width), jnp.bfloat16),
            pltpu.VMEM((2, pulses * (2 * tile + 1), half), jnp.float32),
            pltpu.VMEM((pulses, width), jnp.bfloat16),
        ],
        compiler_params=pltpu.CompilerParams(
            vmem_limit_bytes=VMEM_BYTES if near_chain else 20 * 2**20
        ),
        cost_estimate=pl.CostEstimate(
            flops=2 * pulses * blocks * width * width,
            bytes_accessed=2 * pulses * blocks * width,
            transcendentals=0,
        ),
        name="compress",
    )(*operands)


def image_kernel(dims, data_ref, steer_ref, interp_ref, base_ref, step_ref, out_keep, out_send):
    leaf, each, half, beams, levels = dims
    rows = beams // leaf
    pair = 2
    piece = rows

    def turned(phase, re, im):
        c, s = phase
        return c * re - s * im, c * im + s * re

    bases = []
    for n in range(2 * levels):
        bases.append(jnp.broadcast_to(base_ref[0, n : n + 1, :], (half, beams)).T)

    def phased(level, block, first, re, im):
        cut = slice(first, first + piece)
        lanes = slice(block * half, (block + 1) * half)
        phase = turned(
            (bases[2 * level][cut], bases[2 * level + 1][cut]),
            step_ref[level, 0, cut, lanes],
            step_ref[level, 1, cut, lanes],
        )
        return turned(phase, re, im)

    for at in range(0, each, pair):
        parts = []
        for n in range(2):
            for c in range(2):
                cols = slice(c * half, (c + 1) * half)
                parts.append(
                    jnp.concatenate([data_ref[n, 0, at + i, :, cols] for i in range(pair)], axis=1)
                )
        raw = jnp.dot(
            steer_ref[...], jnp.concatenate(parts, axis=0), preferred_element_type=jnp.float32
        )
        re, im = raw[:beams], raw[beams:]
        for level in range(levels):
            columns = []
            for i in range(pair):
                lanes = slice(i * half, (i + 1) * half)
                pieces = []
                for first in range(0, beams, piece):
                    cut = slice(first, first + piece)
                    both = phased(level, at + i, first, re[cut, lanes], im[cut, lanes])
                    if level == levels - 1:
                        both = jnp.concatenate(both, axis=1)
                        g = first // rows
                        if g < leaf // 2:
                            out_keep[g, 0, at + i] = both
                        else:
                            out_send[g - leaf // 2, 0, at + i] = both.astype(jnp.bfloat16)
                        continue
                    both = jnp.concatenate(both, axis=1)
                    big = both.astype(jnp.bfloat16)
                    low = (both - big.astype(jnp.float32)).astype(jnp.bfloat16)
                    pieces.append((big, low))
                if pieces:
                    columns.append(
                        jnp.concatenate([p[0] for p in pieces] + [p[1] for p in pieces], axis=0)
                    )
            if columns:
                moved = jnp.dot(
                    interp_ref[level],
                    jnp.concatenate(columns, axis=1),
                    preferred_element_type=jnp.float32,
                )
                cuts = [moved[:, n * half : (n + 1) * half] for n in range(2 * pair)]
                re = jnp.concatenate(cuts[0::2], axis=1)
                im = jnp.concatenate(cuts[1::2], axis=1)


def backproject(data, steer, interp, base, step, leaf):
    _, count, each, pulses, width = data.shape
    half = width // 2
    beams = steer.shape[0] // 2
    rows = beams // leaf
    shape = (leaf // 2, count, each, rows, width)

    def block(n):
        return n % (count // 2) * 2 + n // (count // 2)

    out_spec = pl.BlockSpec((leaf // 2, 1) + shape[2:], lambda n: (0, n, 0, 0, 0))
    return pl.pallas_call(
        functools.partial(image_kernel, (leaf, each, half, beams, bits_of(leaf))),
        grid=(count,),
        in_specs=[
            pl.BlockSpec((2, 1, each, pulses, width), lambda n: (0, block(n), 0, 0, 0)),
            pl.BlockSpec(steer.shape, lambda n: (0, 0)),
            pl.BlockSpec(interp.shape, lambda n: (0, 0, 0)),
            pl.BlockSpec((1,) + base.shape[1:], lambda n: (block(n), 0, 0)),
            pl.BlockSpec(step.shape, lambda n: (0, 0, 0, 0)),
        ],
        out_specs=[out_spec, out_spec],
        out_shape=[
            jax.ShapeDtypeStruct(shape, jnp.float32),
            jax.ShapeDtypeStruct(shape, jnp.bfloat16),
        ],
        compiler_params=pltpu.CompilerParams(vmem_limit_bytes=10 * 2**20),
        cost_estimate=pl.CostEstimate(
            flops=12 * beams * pulses * count * each * width,
            bytes_accessed=2 * data.size + 6 * count * each * beams * width // 2,
            transcendentals=0,
        ),
        name="image",
    )(data, steer, interp, base, step)


def fold(keep, got):
    stay, gone = (keep[:, n] + got[:, n].astype(jnp.float32) for n in range(2))
    return stay, gone.astype(jnp.bfloat16)


def last_kernel(keep_ref, got_ref, out_ref, rows_ref):
    blocks, rows, width = keep_ref.shape
    for i in range(blocks):
        value = keep_ref[i] + got_ref[i].astype(jnp.float32)
        for c in range(2):
            cols = slice(c * width // 2, (c + 1) * width // 2)
            rows_ref[c, pl.ds(i, rows, stride=blocks), :] = value[:, cols]
    both = jnp.concatenate([rows_ref[0], rows_ref[1]], axis=1)
    out_ref[...] = both.reshape(rows, blocks, width).astype(jnp.bfloat16)


def last_sum(keep, got):
    blocks, rows, width = keep.shape
    return pl.pallas_call(
        last_kernel,
        out_shape=jax.ShapeDtypeStruct((rows, blocks, width), jnp.bfloat16),
        scratch_shapes=[pltpu.VMEM((2, rows * blocks, width // 2), jnp.float32)],
        compiler_params=pltpu.CompilerParams(vmem_limit_bytes=8 * 2**20),
        name="last_sum",
    )(keep, got)


def interpolation(taps, beams):
    cells = jnp.arange(beams, dtype=jnp.int32)
    weights = jnp.array(WEIGHTS, jnp.float32)
    picks = taps[..., None] == cells
    return jnp.where(picks, weights[:, None], 0.0).sum(axis=-2)


def steering(slots, matrix, side, beams, pulses, scale):
    count = slots.shape[0]
    beam = jnp.arange(beams, dtype=jnp.int32)[:, None, None]
    place = jnp.arange(pulses, dtype=jnp.int32)
    slot = slots[None, :, None]
    cos, sin = unit(
        (2 * beam + 1 - beams) * (2 * place + 1 - pulses)
        + 3 * (beam + 1) * (2 * slot + 1) * (2 * place + 1),
        8 * pulses,
    )
    pair = jnp.concatenate([cos * scale, sin * scale], axis=2).astype(jnp.bfloat16)
    moved = jnp.dot(
        matrix.astype(jnp.bfloat16),
        pair.reshape(beams, count * 2 * pulses),
        preferred_element_type=jnp.float32,
    ).reshape(beams, count, 2 * pulses)
    re, im = moved[:, :, :pulses], moved[:, :, pulses:]
    row = jnp.arange(beams, dtype=jnp.int32)
    c, s = (t[:, None, None] for t in unit(row * row * (side + 1), PERIOD))
    re, im = c * re - s * im, c * im + s * re
    top = jnp.concatenate([re, -im], axis=2)
    low = jnp.concatenate([im, re], axis=2)
    return jnp.concatenate([top, low], axis=0).astype(jnp.bfloat16)


def per_device(echoes, chirp, taps, slots):
    leaf, turn = lax.axis_size("leaf"), lax.axis_size("turn")
    pulses, blocks, width = echoes.shape
    half = width // 2
    beams = taps.shape[2]
    levels = bits_of(leaf)
    far = (bits_of(turn) + 1) // 2 - 1
    top = bits_of(turn) - 1
    mids = 1 << far - 1
    high = turn >> far + 2
    tile = blocks // turn
    each = tile // 2
    rows = beams // leaf
    own_leaf, own_turn = lax.axis_index("leaf"), lax.axis_index("turn")

    keep_y, send_y = compress(chirp, echoes, high, mids, True, far, high)
    chirp, send_y = lax.optimization_barrier((chirp, send_y))
    got_y = swapped(send_y, "turn", 0)
    keep_z, send_z = compress(chirp, echoes, high, mids, False, far, 0)
    got_z = swapped(send_z, "turn", far)

    own_sides = [bit(own_leaf, level) for level in range(levels)]
    row = jnp.arange(beams, dtype=jnp.int32)
    part, place = row // rows, row % rows
    group = own_leaf ^ (2 * (part % (leaf // 2)) + part // (leaf // 2))
    orders = [row] * (levels - 1) + [group * rows + place]
    own_taps = [
        lax.dynamic_index_in_dim(taps[n], own_sides[n], 0, False) for n in range(levels)
    ]
    groups = own_taps[-1].reshape(leaf, rows, -1)
    own_taps[-1] = jnp.concatenate(
        [
            lax.dynamic_index_in_dim(groups, own_leaf ^ (2 * g + side), 0, False)
            for side in range(2)
            for g in range(leaf // 2)
        ],
        axis=0,
    )
    matrices = interpolation(jnp.stack(own_taps), beams)
    interp = jnp.concatenate([matrices[1:]] * 2, axis=-1).astype(jnp.bfloat16)
    scale = 1.0 / math.sqrt(2.0 * slots.shape[1] * pulses)
    wanted = own_turn ^ jnp.array([0, 1, 1 << far], jnp.int32)
    picked = jnp.arange(slots.shape[1], dtype=jnp.int32) == wanted[:, None]
    own_slots = jnp.where(picked, slots, 0).sum(axis=1)
    steer = steering(own_slots, matrices[0], own_sides[0], beams, pulses, scale)
    steer_y = steer[:, :2].reshape(2 * beams, 4 * pulses)
    steer_z = jnp.concatenate([steer[:, :1], steer[:, 2:]], axis=1).reshape(2 * beams, 4 * pulses)

    leans = jnp.stack([2 * order + 1 - beams for order in orders])
    bins = jnp.arange(each * half, dtype=jnp.int32) + 1
    slopes = jnp.stack([(2 * own_sides[n] - 1) * (n + 2) for n in range(levels)])[:, None] * leans
    step = jnp.stack(unit(slopes[:, :, None] * bins, PERIOD), axis=1)
    squares = jnp.stack(
        [orders[n] * orders[n] * (own_sides[n] + 1) * (1 if n else 0) for n in range(levels)]
    )

    def bases(tiles):
        parts = (2 * tiles[:, None] + jnp.arange(2, dtype=jnp.int32)).reshape(-1)
        start = (parts * each * half)[:, None, None]
        both = jnp.stack(unit(slopes * start + squares, PERIOD), axis=2)
        return both.reshape(parts.shape[0], 2 * levels, beams)

    index = jnp.arange(turn // 4, dtype=jnp.int32)
    tiles_y = turn // 2 + 2 * (index ^ (own_turn >> 1 & turn // 4 - 1)) + bit(own_turn, 0)
    low_part = (index ^ own_turn) & (1 << far) - 1
    high_part = index >> far ^ (own_turn >> far + 1 & high - 1)
    tiles_z = (high_part * 2 + bit(own_turn, far)) * (1 << far) + low_part

    pieces = []
    for name, keep, got, steer_own, tiles in (
        ("y", keep_y, got_y, steer_y, tiles_y),
        ("z", keep_z, got_z, steer_z, tiles_z),
    ):
        shape = (turn // 2, each, pulses, width)
        data = jnp.stack([keep.reshape(shape), got.reshape(shape)])
        kept, sent = backproject(data, steer_own, interp, bases(tiles), step, leaf)
        gone = 0 if name == "y" else far
        arrived = swapped(sent, "leaf", 0)
        parts = (leaf // 2, 2, turn // 4, each, rows, width)
        kept, arrived = kept.reshape(parts), arrived.reshape(parts)
        pieces.append([(kept[:, n], arrived[:, n], gone) for n in range(2)])

    final = [[], []]
    for n in range(2):
        for chain in range(2):
            kept, arrived, gone = pieces[chain][n]
            leading = [("leaf", b) for b in range(levels - 1, 0, -1)]
            leading += [("turn", b) for b in range(top - 1, -1, -1) if b != gone]
            order = [("leaf", b) for b in range(1, levels)]
            rest = [("turn", b) for b in range(top) if b not in (0, far)]
            order = [("turn", 0)] + order if gone else order + [("turn", far)]
            for axis, b in order + rest:
                at = leading.index((axis, b))
                before, after = 1 << at, (1 << len(leading) - at - 1) * each
                leading.pop(at)
                split = (before, 2, after, rows, width)
                kept, sent = fold(kept.reshape(split), arrived.reshape(split))
                arrived = swapped(sent, axis, b)
            shape = (each, rows, width)
            total = kept.reshape(shape) + arrived.reshape(shape).astype(jnp.float32)
            final[n].append(total)
    upper = bit(own_turn, top) == 1
    sent = jnp.stack([jnp.where(upper, second, first) for first, second in final])
    kept = jnp.stack([jnp.where(upper, first, second) for first, second in final])
    shape = (tile, rows, width)
    got = swapped(sent.astype(jnp.bfloat16), "turn", top)
    return last_sum(kept.reshape(shape), got.reshape(shape))


def solution(mesh):
    placed = (P(("leaf", "turn"), None, None), P(), P(), P("leaf", None))
    return jax.shard_map(
        per_device, mesh=mesh, in_specs=placed, out_specs=P("leaf", "turn", None), check_vma=False
    )
```

```python
import functools
import math

import jax
import jax.numpy as jnp
from jax import lax
from jax.experimental import pallas as pl
from jax.experimental.pallas import tpu as pltpu
from jax.sharding import PartitionSpec as P

WEIGHTS = (-1.0 / 32, 3.0 / 32, -7.0 / 32, 21.0 / 32, 21.0 / 32, -7.0 / 32, 3.0 / 32, -1.0 / 32)
PERIOD = 4096
VMEM_BYTES = 56 * 2**20


def bits_of(count):
    return count.bit_length() - 1


def bit(value, at):
    return value >> at & 1


def swapped(array, axis, bit):
    return lax.ppermute(array, axis, [(i, i ^ 1 << bit) for i in range(lax.axis_size(axis))])


def unit(phase_int, period):
    angle = jnp.remainder(phase_int, period).astype(jnp.float32) * (2.0 * math.pi / period)
    return jnp.cos(angle), jnp.sin(angle)


def compress_kernel(dims, has_edge, chirp_ref, echo_ref, *refs):
    tile, pulses, half, near_chain, far = dims
    edge_ref, refs = (refs[0], refs[1:]) if has_edge else (None, refs)
    keeps, sends, (weights, rows_ref, carry) = refs[:2], refs[2:4], refs[4:]
    blocks = 2 * tile
    pitch = blocks + 1
    mids = pl.num_programs(2)
    turn = lax.axis_index("turn")
    spot_m = (mids - 1 - pl.program_id(2)) ^ (turn >> 1 & mids - 1)
    spot_v = (1 - pl.program_id(1)) ^ bit(turn, far)
    own_u = bit(turn, 0)

    @pl.when((pl.program_id(0) == 0) & (pl.program_id(1) == 0) & (pl.program_id(2) == 0))
    def _():
        rows = lax.broadcasted_iota(jnp.int32, (half, half), 0)
        cols = lax.broadcasted_iota(jnp.int32, (half, half), 1)
        taps = chirp_ref[...].astype(jnp.float32)
        tables = []
        for c in range(2):
            wide = jnp.broadcast_to(taps[c : c + 1], (half, half))
            tables.append(pltpu.roll(wide, 0, 1, stride=1, stride_axis=0).T)
        for m, mask in enumerate((rows >= cols, rows < cols)):
            re, im = (jnp.where(mask, t, 0.0) for t in tables)
            top = jnp.concatenate([re, im], axis=1)
            low = jnp.concatenate([-im, re], axis=1)
            full = jnp.concatenate([top, low], axis=0)
            weights[m * 2 * half : (m + 1) * 2 * half, :] = full.astype(jnp.bfloat16)
        if has_edge:
            for p in range(pulses):
                for c in range(2):
                    first = edge_ref[p, :, c * half : (c + 1) * half].astype(jnp.float32)
                    rows_ref[c, p : p + 1, :] = first[:1]
            edges = [rows_ref[c, :pulses, :] for c in range(2)]
            carry[...] = jnp.concatenate(edges, axis=1).astype(jnp.bfloat16)
        else:
            carry[...] = jnp.zeros_like(carry)

    for p in range(pulses):
        for c in range(2):
            rows_ref[c, p * pitch : p * pitch + blocks, :] = echo_ref[
                p, :, c * half : (c + 1) * half
            ].astype(jnp.float32)
    turned = []
    for b in range(blocks):
        parts = [rows_ref[c, pl.ds(b, pulses, stride=pitch), :] for c in range(2)]
        turned.append(jnp.concatenate(parts, axis=1).astype(jnp.bfloat16))
    turned.append(carry[...])
    current = jnp.concatenate(turned[:-1], axis=0)
    after = jnp.concatenate(turned[1:], axis=0)
    total = jnp.dot(
        jnp.concatenate([current, after], axis=1),
        weights[...],
        preferred_element_type=jnp.float32,
    ).astype(jnp.bfloat16)
    carry[...] = turned[0]

    def block(b):
        return total[b * pulses : (b + 1) * pulses]

    for spot, side in ((0, 0), (0, 1), (1, 0), (1, 1)):

        @pl.when((spot_v == spot) & (own_u == side))
        def _(spot=spot, side=side):
            for b in range(blocks):
                other = b // tile ^ side
                swaps, part = (other, spot) if near_chain else (spot, other)
                (sends if swaps else keeps)[part][0, spot_m, b % tile] = block(b)


def compress(chirp, echoes, high, mids, near_chain, far, first_high):
    pulses, blocks, width = echoes.shape
    half = width // 2
    tile = blocks // lax.axis_size("turn")
    shape = (high, mids, tile, pulses, width)

    def place(h, v, m):
        turn = lax.axis_index("turn")
        return (high - 1 - h) ^ (turn >> far + 1 & high - 1), 0, 0, 0, 0

    spec = pl.BlockSpec((1,) + shape[1:], place)

    def chunk(h, v, m):
        return 0, ((first_high + high - 1 - h) * 2 + 1 - v) * mids + mids - 1 - m, 0

    in_specs = [
        pl.BlockSpec((2, half), lambda h, v, m: (0, 0)),
        pl.BlockSpec((pulses, 2 * tile, width), chunk),
    ]
    operands = [chirp, echoes]
    has_edge = not near_chain
    if has_edge:
        after = (first_high + high) * 2 * mids
        in_specs.append(pl.BlockSpec((pulses, 2 * tile, width), lambda h, v, m: (0, after, 0)))
        operands.append(echoes)
    dims = (tile, pulses, half, near_chain, far)
    return pl.pallas_call(
        functools.partial(compress_kernel, dims, has_edge),
        grid=(high, 2, mids),
        in_specs=in_specs,
        out_specs=[spec] * 4,
        out_shape=[jax.ShapeDtypeStruct(shape, jnp.bfloat16)] * 4,
        scratch_shapes=[
            pltpu.VMEM((2 * width, width), jnp.bfloat16),
            pltpu.VMEM((2, pulses * (2 * tile + 1), half), jnp.float32),
            pltpu.VMEM((pulses, width), jnp.bfloat16),
        ],
        compiler_params=pltpu.CompilerParams(
            vmem_limit_bytes=VMEM_BYTES if near_chain else 20 * 2**20
        ),
        cost_estimate=pl.CostEstimate(
            flops=2 * pulses * blocks * width * width,
            bytes_accessed=2 * pulses * blocks * width,
            transcendentals=0,
        ),
        name="compress",
    )(*operands)


def image_kernel(dims, data_ref, steer_ref, interp_ref, base_ref, step_ref, *refs):
    leaf, each, half, beams, levels = dims
    out_keep, out_send = refs[-2:]
    rows = beams // leaf
    pair = 2
    piece = rows

    def turned(phase, re, im):
        c, s = phase
        return c * re - s * im, c * im + s * re

    bases = []
    for n in range(2 * levels):
        bases.append(jnp.broadcast_to(base_ref[0, 0, 0, n : n + 1, :], (half, beams)).T)

    def phased(level, block, first, re, im):
        cut = slice(first, first + piece)
        lanes = slice(block * half, (block + 1) * half)
        phase = turned(
            (bases[2 * level][cut], bases[2 * level + 1][cut]),
            step_ref[level, 0, cut, lanes],
            step_ref[level, 1, cut, lanes],
        )
        return turned(phase, re, im)

    for at in range(0, each, pair):
        parts = []
        for n in range(2):
            for c in range(2):
                cols = slice(c * half, (c + 1) * half)
                parts.append(
                    jnp.concatenate([data_ref[n, 0, 0, 0, at + i, :, cols] for i in range(pair)], axis=1)
                )
        raw = jnp.dot(
            steer_ref[...], jnp.concatenate(parts, axis=0), preferred_element_type=jnp.float32
        )
        re, im = raw[:beams], raw[beams:]
        for level in range(levels):
            columns = []
            for i in range(pair):
                lanes = slice(i * half, (i + 1) * half)
                pieces = []
                for first in range(0, beams, piece):
                    cut = slice(first, first + piece)
                    both = phased(level, at + i, first, re[cut, lanes], im[cut, lanes])
                    if level == levels - 1:
                        both = jnp.concatenate(both, axis=1)
                        g = first // rows
                        if g < leaf // 2:
                            out_keep[g, 0, 0, 0, 0, at + i] = both
                        else:
                            out_send[g - leaf // 2, 0, 0, 0, 0, at + i] = both.astype(jnp.bfloat16)
                        continue
                    both = jnp.concatenate(both, axis=1)
                    big = both.astype(jnp.bfloat16)
                    low = (both - big.astype(jnp.float32)).astype(jnp.bfloat16)
                    pieces.append((big, low))
                if pieces:
                    columns.append(
                        jnp.concatenate([p[0] for p in pieces] + [p[1] for p in pieces], axis=0)
                    )
            if columns:
                moved = jnp.dot(
                    interp_ref[level],
                    jnp.concatenate(columns, axis=1),
                    preferred_element_type=jnp.float32,
                )
                cuts = [moved[:, n * half : (n + 1) * half] for n in range(2 * pair)]
                re = jnp.concatenate(cuts[0::2], axis=1)
                im = jnp.concatenate(cuts[1::2], axis=1)


def backproject(data, steer, interp, base, step, leaf, near_chain, part, earlier):
    _, high, mids, _, each, pulses, width = data.shape
    half = width // 2
    beams = steer.shape[0] // 2
    rows = beams // leaf
    middle = (high, 2, mids) if near_chain else (high, mids, 2)
    shape = (leaf // 2, 2) + middle + (each, rows, width)

    def place(n, h, m):
        return (0, n) + ((h, part, m) if near_chain else (h, m, part)) + (0, 0, 0)

    out_spec = pl.BlockSpec((leaf // 2, 1, 1, 1, 1, each, rows, width), place)
    return pl.pallas_call(
        functools.partial(image_kernel, (leaf, each, half, beams, bits_of(leaf))),
        grid=(2, high, mids),
        in_specs=[
            pl.BlockSpec(
                (2, 1, 1, 1, each, pulses, width), lambda n, h, m: (0, h, m, n, 0, 0, 0)
            ),
            pl.BlockSpec(steer.shape, lambda n, h, m: (0, 0)),
            pl.BlockSpec(interp.shape, lambda n, h, m: (0, 0, 0)),
            pl.BlockSpec((1, 1, 1) + base.shape[3:], lambda n, h, m: (h, m, n, 0, 0)),
            pl.BlockSpec(step.shape, lambda n, h, m: (0, 0, 0, 0)),
        ]
        + [pl.BlockSpec(memory_space=pl.ANY)] * len(earlier),
        out_specs=[out_spec, out_spec],
        out_shape=[
            jax.ShapeDtypeStruct(shape, jnp.float32),
            jax.ShapeDtypeStruct(shape, jnp.bfloat16),
        ],
        input_output_aliases={5 + n: n for n in range(len(earlier))},
        compiler_params=pltpu.CompilerParams(vmem_limit_bytes=10 * 2**20),
        cost_estimate=pl.CostEstimate(
            flops=6 * beams * data.size,
            bytes_accessed=2 * data.size + 3 * beams * 2 * high * mids * each * width,
            transcendentals=0,
        ),
        name="image",
    )(data, steer, interp, base, step, *earlier)


def fold(keep, got):
    stay, gone = (keep[:, n] + got[:, n].astype(jnp.float32) for n in range(2))
    return stay, gone.astype(jnp.bfloat16)


def last_kernel(keep_ref, got_ref, out_ref, rows_ref):
    blocks, rows, width = keep_ref.shape
    for i in range(blocks):
        value = keep_ref[i] + got_ref[i].astype(jnp.float32)
        for c in range(2):
            cols = slice(c * width // 2, (c + 1) * width // 2)
            rows_ref[c, pl.ds(i, rows, stride=blocks), :] = value[:, cols]
    both = jnp.concatenate([rows_ref[0], rows_ref[1]], axis=1)
    out_ref[...] = both.reshape(rows, blocks, width).astype(jnp.bfloat16)


def last_sum(keep, got):
    blocks, rows, width = keep.shape
    return pl.pallas_call(
        last_kernel,
        out_shape=jax.ShapeDtypeStruct((rows, blocks, width), jnp.bfloat16),
        scratch_shapes=[pltpu.VMEM((2, rows * blocks, width // 2), jnp.float32)],
        compiler_params=pltpu.CompilerParams(vmem_limit_bytes=8 * 2**20),
        name="last_sum",
    )(keep, got)


def interpolation(taps, beams):
    cells = jnp.arange(beams, dtype=jnp.int32)
    weights = jnp.array(WEIGHTS, jnp.float32)
    picks = taps[..., None] == cells
    return jnp.where(picks, weights[:, None], 0.0).sum(axis=-2)


def steering(slots, matrix, side, beams, pulses, scale):
    count = slots.shape[0]
    beam = jnp.arange(beams, dtype=jnp.int32)[:, None, None]
    place = jnp.arange(pulses, dtype=jnp.int32)
    slot = slots[None, :, None]
    cos, sin = unit(
        (2 * beam + 1 - beams) * (2 * place + 1 - pulses)
        + 3 * (beam + 1) * (2 * slot + 1) * (2 * place + 1),
        8 * pulses,
    )
    pair = jnp.concatenate([cos * scale, sin * scale], axis=2).astype(jnp.bfloat16)
    moved = jnp.dot(
        matrix.astype(jnp.bfloat16),
        pair.reshape(beams, count * 2 * pulses),
        preferred_element_type=jnp.float32,
    ).reshape(beams, count, 2 * pulses)
    re, im = moved[:, :, :pulses], moved[:, :, pulses:]
    row = jnp.arange(beams, dtype=jnp.int32)
    c, s = (t[:, None, None] for t in unit(row * row * (side + 1), PERIOD))
    re, im = c * re - s * im, c * im + s * re
    top = jnp.concatenate([re, -im], axis=2)
    low = jnp.concatenate([im, re], axis=2)
    return jnp.concatenate([top, low], axis=0).astype(jnp.bfloat16)


def per_device(echoes, chirp, taps, slots):
    leaf, turn = lax.axis_size("leaf"), lax.axis_size("turn")
    pulses, blocks, width = echoes.shape
    half = width // 2
    beams = taps.shape[2]
    levels = bits_of(leaf)
    far = (bits_of(turn) + 1) // 2 - 1
    top = bits_of(turn) - 1
    mids = 1 << far - 1
    high = turn >> far + 2
    tile = blocks // turn
    each = tile // 2
    rows = beams // leaf
    own_leaf, own_turn = lax.axis_index("leaf"), lax.axis_index("turn")

    swaps = ((True, 0, high), (False, far, 0))
    keeps, gots = [], []
    for near_chain, swap_bit, first_high in swaps:
        *arrays, = compress(chirp, echoes, high, mids, near_chain, far, first_high)
        chirp, *arrays = lax.optimization_barrier((chirp, *arrays))
        keeps.append(arrays[:2])
        gots.append([swapped(a, "turn", swap_bit) for a in arrays[2:]])

    own_sides = [bit(own_leaf, level) for level in range(levels)]
    row = jnp.arange(beams, dtype=jnp.int32)
    part, place = row // rows, row % rows
    group = own_leaf ^ (2 * (part % (leaf // 2)) + part // (leaf // 2))
    orders = [row] * (levels - 1) + [group * rows + place]
    own_taps = [
        lax.dynamic_index_in_dim(taps[n], own_sides[n], 0, False) for n in range(levels)
    ]
    groups = own_taps[-1].reshape(leaf, rows, -1)
    own_taps[-1] = jnp.concatenate(
        [
            lax.dynamic_index_in_dim(groups, own_leaf ^ (2 * g + side), 0, False)
            for side in range(2)
            for g in range(leaf // 2)
        ],
        axis=0,
    )
    matrices = interpolation(jnp.stack(own_taps), beams)
    interp = jnp.concatenate([matrices[1:]] * 2, axis=-1).astype(jnp.bfloat16)
    scale = 1.0 / math.sqrt(2.0 * slots.shape[1] * pulses)
    wanted = own_turn ^ jnp.array([0, 1, 1 << far], jnp.int32)
    picked = jnp.arange(slots.shape[1], dtype=jnp.int32) == wanted[:, None]
    own_slots = jnp.where(picked, slots, 0).sum(axis=1)
    steer = steering(own_slots, matrices[0], own_sides[0], beams, pulses, scale)
    steer_y = steer[:, :2].reshape(2 * beams, 4 * pulses)
    steer_z = jnp.concatenate([steer[:, :1], steer[:, 2:]], axis=1).reshape(2 * beams, 4 * pulses)

    leans = jnp.stack([2 * order + 1 - beams for order in orders])
    bins = jnp.arange(each * half, dtype=jnp.int32) + 1
    slopes = jnp.stack([(2 * own_sides[n] - 1) * (n + 2) for n in range(levels)])[:, None] * leans
    step = jnp.stack(unit(slopes[:, :, None] * bins, PERIOD), axis=1)
    squares = jnp.stack(
        [orders[n] * orders[n] * (own_sides[n] + 1) * (1 if n else 0) for n in range(levels)]
    )

    own_high, own_mid = own_turn >> far + 1 & high - 1, own_turn >> 1 & mids - 1
    own_near, own_far = bit(own_turn, 0), bit(own_turn, far)

    def bases(near_chain, part):
        h = (jnp.arange(high, dtype=jnp.int32) ^ own_high)[:, None]
        m = (jnp.arange(mids, dtype=jnp.int32) ^ own_mid)[None, :]
        if near_chain:
            h, u, v = h + high, own_near, own_far ^ part
        else:
            u, v = own_near ^ part, own_far
        tiles = ((h * 2 + v) * mids + m) * 2 + u
        parts = (2 * tiles[..., None] + jnp.arange(2, dtype=jnp.int32)).reshape(-1)
        start = (parts * each * half)[:, None, None]
        both = jnp.stack(unit(slopes * start + squares, PERIOD), axis=2)
        return both.reshape(high, mids, 2, 2 * levels, beams)

    pieces = []
    results = [(), ()]
    for part in range(2):
        for n, steer_own in enumerate((steer_y, steer_z)):
            shape = (high, mids, 2, each, pulses, width)
            data = jnp.stack([keeps[n][part].reshape(shape), gots[n][part].reshape(shape)])
            base = bases(n == 0, part)
            results[n] = backproject(
                data, steer_own, interp, base, step, leaf, n == 0, part, results[n]
            )
    for n in range(2):
        kept, sent = results[n]
        gone = swaps[n][1]
        arrived = swapped(sent, "leaf", 0)
        parts = (leaf // 2, 2, turn // 4, each, rows, width)
        kept, arrived = kept.reshape(parts), arrived.reshape(parts)
        pieces.append([(kept[:, k], arrived[:, k], gone) for k in range(2)])

    final = [[], []]
    for n in range(2):
        for chain in range(2):
            kept, arrived, gone = pieces[chain][n]
            leading = [("leaf", b) for b in range(levels - 1, 0, -1)]
            leading += [("turn", b) for b in range(top - 1, -1, -1) if b != gone]
            order = [("leaf", b) for b in range(1, levels)]
            rest = [("turn", b) for b in range(top) if b not in (0, far)]
            order = [("turn", 0)] + order if gone else order + [("turn", far)]
            for axis, b in order + rest:
                at = leading.index((axis, b))
                before, after = 1 << at, (1 << len(leading) - at - 1) * each
                leading.pop(at)
                split = (before, 2, after, rows, width)
                kept, sent = fold(kept.reshape(split), arrived.reshape(split))
                arrived = swapped(sent, axis, b)
            shape = (each, rows, width)
            total = kept.reshape(shape) + arrived.reshape(shape).astype(jnp.float32)
            final[n].append(total)
    upper = bit(own_turn, top) == 1
    sent = jnp.stack([jnp.where(upper, second, first) for first, second in final])
    kept = jnp.stack([jnp.where(upper, first, second) for first, second in final])
    shape = (tile, rows, width)
    got = swapped(sent.astype(jnp.bfloat16), "turn", top)
    return last_sum(kept.reshape(shape), got.reshape(shape))


def solution(mesh):
    placed = (P(("leaf", "turn"), None, None), P(), P(), P("leaf", None))
    return jax.shard_map(
        per_device, mesh=mesh, in_specs=placed, out_specs=P("leaf", "turn", None), check_vma=False
    )
```

```python
import functools
import math

import jax
import jax.numpy as jnp
from jax import lax
from jax.experimental import pallas as pl
from jax.experimental.pallas import tpu as pltpu
from jax.sharding import PartitionSpec as P

WEIGHTS = (-1.0 / 32, 3.0 / 32, -7.0 / 32, 21.0 / 32, 21.0 / 32, -7.0 / 32, 3.0 / 32, -1.0 / 32)
PERIOD = 4096
VMEM_BYTES = 56 * 2**20


def bits_of(count):
    return count.bit_length() - 1


def bit(value, at):
    return value >> at & 1


def swapped(array, axis, bit):
    return lax.ppermute(array, axis, [(i, i ^ 1 << bit) for i in range(lax.axis_size(axis))])


def unit(phase_int, period):
    angle = jnp.remainder(phase_int, period).astype(jnp.float32) * (2.0 * math.pi / period)
    return jnp.cos(angle), jnp.sin(angle)


def compress_kernel(dims, has_edge, chirp_ref, echo_ref, *refs):
    tile, pulses, half, near_chain, far = dims
    edge_ref, refs = (refs[0], refs[1:]) if has_edge else (None, refs)
    keep_ref, send_ref, weights, rows_ref, carry = refs
    blocks = 2 * tile
    pitch = blocks + 1
    mids = pl.num_programs(2)
    high = pl.num_programs(0)
    turn = lax.axis_index("turn")
    spot_h = (high - 1 - pl.program_id(0)) ^ (turn >> far + 1 & high - 1)
    spot_m = (mids - 1 - pl.program_id(2)) ^ (turn >> 1 & mids - 1)
    spot_v = (1 - pl.program_id(1)) ^ bit(turn, far)
    own_u = bit(turn, 0)

    @pl.when((pl.program_id(0) == 0) & (pl.program_id(1) == 0) & (pl.program_id(2) == 0))
    def _():
        rows = lax.broadcasted_iota(jnp.int32, (half, half), 0)
        cols = lax.broadcasted_iota(jnp.int32, (half, half), 1)
        taps = chirp_ref[...].astype(jnp.float32)
        tables = []
        for c in range(2):
            wide = jnp.broadcast_to(taps[c : c + 1], (half, half))
            tables.append(pltpu.roll(wide, 0, 1, stride=1, stride_axis=0).T)
        for m, mask in enumerate((rows >= cols, rows < cols)):
            re, im = (jnp.where(mask, t, 0.0) for t in tables)
            top = jnp.concatenate([re, im], axis=1)
            low = jnp.concatenate([-im, re], axis=1)
            full = jnp.concatenate([top, low], axis=0)
            weights[m * 2 * half : (m + 1) * 2 * half, :] = full.astype(jnp.bfloat16)
        if has_edge:
            for p in range(pulses):
                for c in range(2):
                    first = edge_ref[p, :, c * half : (c + 1) * half].astype(jnp.float32)
                    rows_ref[c, p : p + 1, :] = first[:1]
            edges = [rows_ref[c, :pulses, :] for c in range(2)]
            carry[...] = jnp.concatenate(edges, axis=1).astype(jnp.bfloat16)
        else:
            carry[...] = jnp.zeros_like(carry)

    for p in range(pulses):
        for c in range(2):
            rows_ref[c, p * pitch : p * pitch + blocks, :] = echo_ref[
                p, :, c * half : (c + 1) * half
            ].astype(jnp.float32)
    turned = []
    for b in range(blocks):
        parts = [rows_ref[c, pl.ds(b, pulses, stride=pitch), :] for c in range(2)]
        turned.append(jnp.concatenate(parts, axis=1).astype(jnp.bfloat16))
    turned.append(carry[...])
    current = jnp.concatenate(turned[:-1], axis=0)
    after = jnp.concatenate(turned[1:], axis=0)
    total = jnp.dot(
        jnp.concatenate([current, after], axis=1),
        weights[...],
        preferred_element_type=jnp.float32,
    ).astype(jnp.bfloat16)
    carry[...] = turned[0]

    def block(b):
        return total[b * pulses : (b + 1) * pulses]

    if near_chain:
        for side in range(2):

            @pl.when(own_u == side)
            def _(side=side):
                for b in range(blocks):
                    ref = keep_ref if b // tile == side else send_ref
                    ref[0, 0, 0, b % tile] = block(b)
    else:
        for ref, mine in ((keep_ref, 0), (send_ref, 1)):

            @pl.when(spot_v == mine)
            def _(ref=ref):
                for b in range(blocks):
                    ref[spot_h, spot_m, b // tile ^ own_u, b % tile] = block(b)


def compress(chirp, echoes, high, mids, near_chain, far, first_high):
    pulses, blocks, width = echoes.shape
    half = width // 2
    tile = blocks // lax.axis_size("turn")
    if near_chain:
        shape = (high, 2, mids, tile, pulses, width)

        def place(h, v, m):
            turn = lax.axis_index("turn")
            spot_h = (high - 1 - h) ^ (turn >> far + 1 & high - 1)
            spot_m = (mids - 1 - m) ^ (turn >> 1 & mids - 1)
            return spot_h, (1 - v) ^ bit(turn, far), spot_m, 0, 0, 0

        spec = pl.BlockSpec((1, 1, 1) + shape[3:], place)
    else:
        shape = (high, mids, 2, tile, pulses, width)
        spec = pl.BlockSpec(shape, lambda h, v, m: (0, 0, 0, 0, 0, 0))
    def chunk(h, v, m):
        return 0, ((first_high + high - 1 - h) * 2 + 1 - v) * mids + mids - 1 - m, 0

    in_specs = [
        pl.BlockSpec((2, half), lambda h, v, m: (0, 0)),
        pl.BlockSpec((pulses, 2 * tile, width), chunk),
    ]
    operands = [chirp, echoes]
    has_edge = not near_chain
    if has_edge:
        after = (first_high + high) * 2 * mids
        in_specs.append(pl.BlockSpec((pulses, 2 * tile, width), lambda h, v, m: (0, after, 0)))
        operands.append(echoes)
    dims = (tile, pulses, half, near_chain, far)
    return pl.pallas_call(
        functools.partial(compress_kernel, dims, has_edge),
        grid=(high, 2, mids),
        in_specs=in_specs,
        out_specs=[spec, spec],
        out_shape=[jax.ShapeDtypeStruct(shape, jnp.bfloat16)] * 2,
        scratch_shapes=[
            pltpu.VMEM((2 * width, width), jnp.bfloat16),
            pltpu.VMEM((2, pulses * (2 * tile + 1), half), jnp.float32),
            pltpu.VMEM((pulses, width), jnp.bfloat16),
        ],
        compiler_params=pltpu.CompilerParams(
            vmem_limit_bytes=VMEM_BYTES if near_chain else 20 * 2**20
        ),
        cost_estimate=pl.CostEstimate(
            flops=2 * pulses * blocks * width * width,
            bytes_accessed=2 * pulses * blocks * width,
            transcendentals=0,
        ),
        name="compress",
    )(*operands)


def image_kernel(dims, data_ref, steer_ref, interp_ref, base_ref, step_ref, out_keep, out_send):
    leaf, each, half, beams, levels = dims
    rows = beams // leaf
    pair = each
    piece = rows

    def turned(phase, re, im):
        c, s = phase
        return c * re - s * im, c * im + s * re

    bases = []
    for n in range(2 * levels):
        bases.append(jnp.broadcast_to(base_ref[0, n : n + 1, :], (half, beams)).T)

    def phased(level, block, first, re, im):
        cut = slice(first, first + piece)
        lanes = slice(block * half, (block + 1) * half)
        phase = turned(
            (bases[2 * level][cut], bases[2 * level + 1][cut]),
            step_ref[level, 0, cut, lanes],
            step_ref[level, 1, cut, lanes],
        )
        return turned(phase, re, im)

    for at in range(0, each, pair):
        parts = []
        for n in range(2):
            for c in range(2):
                cols = slice(c * half, (c + 1) * half)
                parts.append(
                    jnp.concatenate([data_ref[n, 0, at + i, :, cols] for i in range(pair)], axis=1)
                )
        raw = jnp.dot(
            steer_ref[...], jnp.concatenate(parts, axis=0), preferred_element_type=jnp.float32
        )
        re, im = raw[:beams], raw[beams:]
        for level in range(levels):
            columns = []
            for i in range(pair):
                lanes = slice(i * half, (i + 1) * half)
                pieces = []
                for first in range(0, beams, piece):
                    cut = slice(first, first + piece)
                    both = phased(level, at + i, first, re[cut, lanes], im[cut, lanes])
                    if level == levels - 1:
                        both = jnp.concatenate(both, axis=1)
                        g = first // rows
                        if g < leaf // 2:
                            out_keep[g, 0, at + i] = both
                        else:
                            out_send[g - leaf // 2, 0, at + i] = both.astype(jnp.bfloat16)
                        continue
                    both = jnp.concatenate(both, axis=1)
                    big = both.astype(jnp.bfloat16)
                    low = (both - big.astype(jnp.float32)).astype(jnp.bfloat16)
                    pieces.append((big, low))
                if pieces:
                    columns.append(
                        jnp.concatenate([p[0] for p in pieces] + [p[1] for p in pieces], axis=0)
                    )
            if columns:
                moved = jnp.dot(
                    interp_ref[level],
                    jnp.concatenate(columns, axis=1),
                    preferred_element_type=jnp.float32,
                )
                cuts = [moved[:, n * half : (n + 1) * half] for n in range(2 * pair)]
                re = jnp.concatenate(cuts[0::2], axis=1)
                im = jnp.concatenate(cuts[1::2], axis=1)


def backproject(data, steer, interp, base, step, leaf):
    _, count, each, pulses, width = data.shape
    half = width // 2
    beams = steer.shape[0] // 2
    rows = beams // leaf
    shape = (leaf // 2, count, each, rows, width)

    def block(n):
        return n % (count // 2) * 2 + n // (count // 2)

    out_spec = pl.BlockSpec((leaf // 2, 1) + shape[2:], lambda n: (0, n, 0, 0, 0))
    return pl.pallas_call(
        functools.partial(image_kernel, (leaf, each, half, beams, bits_of(leaf))),
        grid=(count,),
        in_specs=[
            pl.BlockSpec((2, 1, each, pulses, width), lambda n: (0, block(n), 0, 0, 0)),
            pl.BlockSpec(steer.shape, lambda n: (0, 0)),
            pl.BlockSpec(interp.shape, lambda n: (0, 0, 0)),
            pl.BlockSpec((1,) + base.shape[1:], lambda n: (block(n), 0, 0)),
            pl.BlockSpec(step.shape, lambda n: (0, 0, 0, 0)),
        ],
        out_specs=[out_spec, out_spec],
        out_shape=[
            jax.ShapeDtypeStruct(shape, jnp.float32),
            jax.ShapeDtypeStruct(shape, jnp.bfloat16),
        ],
        compiler_params=pltpu.CompilerParams(vmem_limit_bytes=10 * 2**20),
        cost_estimate=pl.CostEstimate(
            flops=12 * beams * pulses * count * each * width,
            bytes_accessed=2 * data.size + 6 * count * each * beams * width // 2,
            transcendentals=0,
        ),
        name="image",
    )(data, steer, interp, base, step)


def fold(keep, got):
    stay, gone = (keep[:, n] + got[:, n].astype(jnp.float32) for n in range(2))
    return stay, gone.astype(jnp.bfloat16)


def last_kernel(keep_ref, got_ref, out_ref, rows_ref):
    blocks, rows, width = keep_ref.shape
    for i in range(blocks):
        value = keep_ref[i] + got_ref[i].astype(jnp.float32)
        for c in range(2):
            cols = slice(c * width // 2, (c + 1) * width // 2)
            rows_ref[c, pl.ds(i, rows, stride=blocks), :] = value[:, cols]
    both = jnp.concatenate([rows_ref[0], rows_ref[1]], axis=1)
    out_ref[...] = both.reshape(rows, blocks, width).astype(jnp.bfloat16)


def last_sum(keep, got):
    blocks, rows, width = keep.shape
    return pl.pallas_call(
        last_kernel,
        out_shape=jax.ShapeDtypeStruct((rows, blocks, width), jnp.bfloat16),
        scratch_shapes=[pltpu.VMEM((2, rows * blocks, width // 2), jnp.float32)],
        compiler_params=pltpu.CompilerParams(vmem_limit_bytes=8 * 2**20),
        name="last_sum",
    )(keep, got)


def interpolation(taps, beams):
    cells = jnp.arange(beams, dtype=jnp.int32)
    weights = jnp.array(WEIGHTS, jnp.float32)
    picks = taps[..., None] == cells
    return jnp.where(picks, weights[:, None], 0.0).sum(axis=-2)


def steering(slots, matrix, side, beams, pulses, scale):
    count = slots.shape[0]
    beam = jnp.arange(beams, dtype=jnp.int32)[:, None, None]
    place = jnp.arange(pulses, dtype=jnp.int32)
    slot = slots[None, :, None]
    cos, sin = unit(
        (2 * beam + 1 - beams) * (2 * place + 1 - pulses)
        + 3 * (beam + 1) * (2 * slot + 1) * (2 * place + 1),
        8 * pulses,
    )
    pair = jnp.concatenate([cos * scale, sin * scale], axis=2).astype(jnp.bfloat16)
    moved = jnp.dot(
        matrix.astype(jnp.bfloat16),
        pair.reshape(beams, count * 2 * pulses),
        preferred_element_type=jnp.float32,
    ).reshape(beams, count, 2 * pulses)
    re, im = moved[:, :, :pulses], moved[:, :, pulses:]
    row = jnp.arange(beams, dtype=jnp.int32)
    c, s = (t[:, None, None] for t in unit(row * row * (side + 1), PERIOD))
    re, im = c * re - s * im, c * im + s * re
    top = jnp.concatenate([re, -im], axis=2)
    low = jnp.concatenate([im, re], axis=2)
    return jnp.concatenate([top, low], axis=0).astype(jnp.bfloat16)


def per_device(echoes, chirp, taps, slots):
    leaf, turn = lax.axis_size("leaf"), lax.axis_size("turn")
    pulses, blocks, width = echoes.shape
    half = width // 2
    beams = taps.shape[2]
    levels = bits_of(leaf)
    far = (bits_of(turn) + 1) // 2 - 1
    top = bits_of(turn) - 1
    mids = 1 << far - 1
    high = turn >> far + 2
    tile = blocks // turn
    each = tile // 2
    rows = beams // leaf
    own_leaf, own_turn = lax.axis_index("leaf"), lax.axis_index("turn")

    keep_y, send_y = compress(chirp, echoes, high, mids, True, far, high)
    chirp, send_y = lax.optimization_barrier((chirp, send_y))
    got_y = swapped(send_y, "turn", 0)
    keep_z, send_z = compress(chirp, echoes, high, mids, False, far, 0)
    got_z = swapped(send_z, "turn", far)

    own_sides = [bit(own_leaf, level) for level in range(levels)]
    row = jnp.arange(beams, dtype=jnp.int32)
    part, place = row // rows, row % rows
    group = own_leaf ^ (2 * (part % (leaf // 2)) + part // (leaf // 2))
    orders = [row] * (levels - 1) + [group * rows + place]
    own_taps = [
        lax.dynamic_index_in_dim(taps[n], own_sides[n], 0, False) for n in range(levels)
    ]
    groups = own_taps[-1].reshape(leaf, rows, -1)
    own_taps[-1] = jnp.concatenate(
        [
            lax.dynamic_index_in_dim(groups, own_leaf ^ (2 * g + side), 0, False)
            for side in range(2)
            for g in range(leaf // 2)
        ],
        axis=0,
    )
    matrices = interpolation(jnp.stack(own_taps), beams)
    interp = jnp.concatenate([matrices[1:]] * 2, axis=-1).astype(jnp.bfloat16)
    scale = 1.0 / math.sqrt(2.0 * slots.shape[1] * pulses)
    wanted = own_turn ^ jnp.array([0, 1, 1 << far], jnp.int32)
    picked = jnp.arange(slots.shape[1], dtype=jnp.int32) == wanted[:, None]
    own_slots = jnp.where(picked, slots, 0).sum(axis=1)
    steer = steering(own_slots, matrices[0], own_sides[0], beams, pulses, scale)
    steer_y = steer[:, :2].reshape(2 * beams, 4 * pulses)
    steer_z = jnp.concatenate([steer[:, :1], steer[:, 2:]], axis=1).reshape(2 * beams, 4 * pulses)

    leans = jnp.stack([2 * order + 1 - beams for order in orders])
    bins = jnp.arange(each * half, dtype=jnp.int32) + 1
    slopes = jnp.stack([(2 * own_sides[n] - 1) * (n + 2) for n in range(levels)])[:, None] * leans
    step = jnp.stack(unit(slopes[:, :, None] * bins, PERIOD), axis=1)
    squares = jnp.stack(
        [orders[n] * orders[n] * (own_sides[n] + 1) * (1 if n else 0) for n in range(levels)]
    )

    def bases(tiles):
        parts = (2 * tiles[:, None] + jnp.arange(2, dtype=jnp.int32)).reshape(-1)
        start = (parts * each * half)[:, None, None]
        both = jnp.stack(unit(slopes * start + squares, PERIOD), axis=2)
        return both.reshape(parts.shape[0], 2 * levels, beams)

    index = jnp.arange(turn // 4, dtype=jnp.int32)
    tiles_y = turn // 2 + 2 * (index ^ (own_turn >> 1 & turn // 4 - 1)) + bit(own_turn, 0)
    low_part = (index ^ own_turn) & (1 << far) - 1
    high_part = index >> far ^ (own_turn >> far + 1 & high - 1)
    tiles_z = (high_part * 2 + bit(own_turn, far)) * (1 << far) + low_part

    pieces = []
    for name, keep, got, steer_own, tiles in (
        ("y", keep_y, got_y, steer_y, tiles_y),
        ("z", keep_z, got_z, steer_z, tiles_z),
    ):
        shape = (turn // 2, each, pulses, width)
        data = jnp.stack([keep.reshape(shape), got.reshape(shape)])
        kept, sent = backproject(data, steer_own, interp, bases(tiles), step, leaf)
        gone = 0 if name == "y" else far
        arrived = swapped(sent, "leaf", 0)
        parts = (leaf // 2, 2, turn // 4, each, rows, width)
        kept, arrived = kept.reshape(parts), arrived.reshape(parts)
        pieces.append([(kept[:, n], arrived[:, n], gone) for n in range(2)])

    final = [[], []]
    for n in range(2):
        for chain in range(2):
            kept, arrived, gone = pieces[chain][n]
            leading = [("leaf", b) for b in range(levels - 1, 0, -1)]
            leading += [("turn", b) for b in range(top - 1, -1, -1) if b != gone]
            order = [("leaf", b) for b in range(1, levels)]
            rest = [("turn", b) for b in range(top) if b not in (0, far)]
            order = [("turn", 0)] + order if gone else order + [("turn", far)]
            for axis, b in order + rest:
                at = leading.index((axis, b))
                before, after = 1 << at, (1 << len(leading) - at - 1) * each
                leading.pop(at)
                split = (before, 2, after, rows, width)
                kept, sent = fold(kept.reshape(split), arrived.reshape(split))
                arrived = swapped(sent, axis, b)
            shape = (each, rows, width)
            total = kept.reshape(shape) + arrived.reshape(shape).astype(jnp.float32)
            final[n].append(total)
    upper = bit(own_turn, top) == 1
    sent = jnp.stack([jnp.where(upper, second, first) for first, second in final])
    kept = jnp.stack([jnp.where(upper, first, second) for first, second in final])
    shape = (tile, rows, width)
    got = swapped(sent.astype(jnp.bfloat16), "turn", top)
    return last_sum(kept.reshape(shape), got.reshape(shape))


def solution(mesh):
    placed = (P(("leaf", "turn"), None, None), P(), P(), P("leaf", None))
    return jax.shard_map(
        per_device, mesh=mesh, in_specs=placed, out_specs=P("leaf", "turn", None), check_vma=False
    )
```

```python
import functools
import math

import jax
import jax.numpy as jnp
from jax import lax
from jax.experimental import pallas as pl
from jax.experimental.pallas import tpu as pltpu
from jax.sharding import PartitionSpec as P

WEIGHTS = (-1.0 / 32, 3.0 / 32, -7.0 / 32, 21.0 / 32, 21.0 / 32, -7.0 / 32, 3.0 / 32, -1.0 / 32)
PERIOD = 4096
VMEM_BYTES = 56 * 2**20


def bits_of(count):
    return count.bit_length() - 1


def bit(value, at):
    return value >> at & 1


def swapped(array, axis, bit):
    return lax.ppermute(array, axis, [(i, i ^ 1 << bit) for i in range(lax.axis_size(axis))])


def unit(phase_int, period):
    angle = jnp.remainder(phase_int, period).astype(jnp.float32) * (2.0 * math.pi / period)
    return jnp.cos(angle), jnp.sin(angle)


def compress_kernel(dims, has_edge, chirp_ref, echo_ref, *refs):
    tile, pulses, half, near_chain, far = dims
    edge_ref, refs = (refs[0], refs[1:]) if has_edge else (None, refs)
    keep_ref, send_ref, weights, rows_ref, carry = refs
    blocks = 2 * tile
    pitch = blocks + 1
    mids = pl.num_programs(2)
    high = pl.num_programs(0)
    turn = lax.axis_index("turn")
    spot_h = (high - 1 - pl.program_id(0)) ^ (turn >> far + 1 & high - 1)
    spot_m = (mids - 1 - pl.program_id(2)) ^ (turn >> 1 & mids - 1)
    spot_v = (1 - pl.program_id(1)) ^ bit(turn, far)
    own_u = bit(turn, 0)

    @pl.when((pl.program_id(0) == 0) & (pl.program_id(1) == 0) & (pl.program_id(2) == 0))
    def _():
        rows = lax.broadcasted_iota(jnp.int32, (half, half), 0)
        cols = lax.broadcasted_iota(jnp.int32, (half, half), 1)
        taps = chirp_ref[...].astype(jnp.float32)
        tables = []
        for c in range(2):
            wide = jnp.broadcast_to(taps[c : c + 1], (half, half))
            tables.append(pltpu.roll(wide, 0, 1, stride=1, stride_axis=0).T)
        for m, mask in enumerate((rows >= cols, rows < cols)):
            re, im = (jnp.where(mask, t, 0.0) for t in tables)
            top = jnp.concatenate([re, im], axis=1)
            low = jnp.concatenate([-im, re], axis=1)
            full = jnp.concatenate([top, low], axis=0)
            weights[m * 2 * half : (m + 1) * 2 * half, :] = full.astype(jnp.bfloat16)
        if has_edge:
            for p in range(pulses):
                for c in range(2):
                    first = edge_ref[p, :, c * half : (c + 1) * half].astype(jnp.float32)
                    rows_ref[c, p : p + 1, :] = first[:1]
            edges = [rows_ref[c, :pulses, :] for c in range(2)]
            carry[...] = jnp.concatenate(edges, axis=1).astype(jnp.bfloat16)
        else:
            carry[...] = jnp.zeros_like(carry)

    for p in range(pulses):
        for c in range(2):
            rows_ref[c, p * pitch : p * pitch + blocks, :] = echo_ref[
                p, :, c * half : (c + 1) * half
            ].astype(jnp.float32)
    turned = []
    for b in range(blocks):
        parts = [rows_ref[c, pl.ds(b, pulses, stride=pitch), :] for c in range(2)]
        turned.append(jnp.concatenate(parts, axis=1).astype(jnp.bfloat16))
    turned.append(carry[...])
    current = jnp.concatenate(turned[:-1], axis=0)
    after = jnp.concatenate(turned[1:], axis=0)
    total = jnp.dot(
        jnp.concatenate([current, after], axis=1),
        weights[...],
        preferred_element_type=jnp.float32,
    ).astype(jnp.bfloat16)
    carry[...] = turned[0]

    def block(b):
        return total[b * pulses : (b + 1) * pulses]

    if near_chain:
        for side in range(2):

            @pl.when(own_u == side)
            def _(side=side):
                for b in range(blocks):
                    ref = keep_ref if b // tile == side else send_ref
                    ref[0, 0, 0, b % tile] = block(b)
    else:
        for ref, mine in ((keep_ref, 0), (send_ref, 1)):

            @pl.when(spot_v == mine)
            def _(ref=ref):
                for b in range(blocks):
                    ref[spot_h, spot_m, b // tile ^ own_u, b % tile] = block(b)


def compress(chirp, echoes, high, mids, near_chain, far, first_high):
    pulses, blocks, width = echoes.shape
    half = width // 2
    tile = blocks // lax.axis_size("turn")
    if near_chain:
        shape = (high, 2, mids, tile, pulses, width)

        def place(h, v, m):
            turn = lax.axis_index("turn")
            spot_h = (high - 1 - h) ^ (turn >> far + 1 & high - 1)
            spot_m = (mids - 1 - m) ^ (turn >> 1 & mids - 1)
            return spot_h, (1 - v) ^ bit(turn, far), spot_m, 0, 0, 0

        spec = pl.BlockSpec((1, 1, 1) + shape[3:], place)
    else:
        shape = (high, mids, 2, tile, pulses, width)
        spec = pl.BlockSpec(shape, lambda h, v, m: (0, 0, 0, 0, 0, 0))
    def chunk(h, v, m):
        return 0, ((first_high + high - 1 - h) * 2 + 1 - v) * mids + mids - 1 - m, 0

    in_specs = [
        pl.BlockSpec((2, half), lambda h, v, m: (0, 0)),
        pl.BlockSpec((pulses, 2 * tile, width), chunk),
    ]
    operands = [chirp, echoes]
    has_edge = not near_chain
    if has_edge:
        after = (first_high + high) * 2 * mids
        in_specs.append(pl.BlockSpec((pulses, 2 * tile, width), lambda h, v, m: (0, after, 0)))
        operands.append(echoes)
    dims = (tile, pulses, half, near_chain, far)
    return pl.pallas_call(
        functools.partial(compress_kernel, dims, has_edge),
        grid=(high, 2, mids),
        in_specs=in_specs,
        out_specs=[spec, spec],
        out_shape=[jax.ShapeDtypeStruct(shape, jnp.bfloat16)] * 2,
        scratch_shapes=[
            pltpu.VMEM((2 * width, width), jnp.bfloat16),
            pltpu.VMEM((2, pulses * (2 * tile + 1), half), jnp.float32),
            pltpu.VMEM((pulses, width), jnp.bfloat16),
        ],
        compiler_params=pltpu.CompilerParams(
            vmem_limit_bytes=VMEM_BYTES if near_chain else 20 * 2**20
        ),
        cost_estimate=pl.CostEstimate(
            flops=2 * pulses * blocks * width * width,
            bytes_accessed=2 * pulses * blocks * width,
            transcendentals=0,
        ),
        name="compress",
    )(*operands)


def image_kernel(dims, data_ref, steer_ref, interp_ref, base_ref, step_ref, out_keep, out_send):
    leaf, each, half, beams, levels = dims
    rows = beams // leaf
    pair = 2
    piece = rows

    def turned(phase, re, im):
        c, s = phase
        return c * re - s * im, c * im + s * re

    bases = []
    for n in range(2 * levels):
        bases.append(jnp.broadcast_to(base_ref[0, n : n + 1, :], (half, beams)).T)

    def phased(level, block, first, re, im):
        cut = slice(first, first + piece)
        lanes = slice(block * half, (block + 1) * half)
        phase = turned(
            (bases[2 * level][cut], bases[2 * level + 1][cut]),
            step_ref[level, 0, cut, lanes],
            step_ref[level, 1, cut, lanes],
        )
        return turned(phase, re, im)

    for at in range(0, each, pair):
        parts = []
        for n in range(2):
            for c in range(2):
                cols = slice(c * half, (c + 1) * half)
                parts.append(
                    jnp.concatenate([data_ref[n, 0, at + i, :, cols] for i in range(pair)], axis=1)
                )
        raw = jnp.dot(
            steer_ref[...], jnp.concatenate(parts, axis=0), preferred_element_type=jnp.float32
        )
        re, im = raw[:beams], raw[beams:]
        for level in range(levels):
            columns = []
            for i in range(pair):
                lanes = slice(i * half, (i + 1) * half)
                pieces = []
                for first in range(0, beams, piece):
                    cut = slice(first, first + piece)
                    both = phased(level, at + i, first, re[cut, lanes], im[cut, lanes])
                    if level == levels - 1:
                        both = jnp.concatenate(both, axis=1)
                        g = first // rows
                        if g < leaf // 2:
                            out_keep[g, 0, at + i] = both
                        else:
                            out_send[g - leaf // 2, 0, at + i] = both.astype(jnp.bfloat16)
                        continue
                    both = jnp.concatenate(both, axis=1)
                    big = both.astype(jnp.bfloat16)
                    low = (both - big.astype(jnp.float32)).astype(jnp.bfloat16)
                    pieces.append((big, low))
                if pieces:
                    columns.append(
                        jnp.concatenate([p[0] for p in pieces] + [p[1] for p in pieces], axis=0)
                    )
            if columns:
                moved = jnp.dot(
                    interp_ref[level],
                    jnp.concatenate(columns, axis=1),
                    preferred_element_type=jnp.float32,
                )
                cuts = [moved[:, n * half : (n + 1) * half] for n in range(2 * pair)]
                re = jnp.concatenate(cuts[0::2], axis=1)
                im = jnp.concatenate(cuts[1::2], axis=1)


def backproject(data, steer, interp, base, step, leaf):
    _, count, each, pulses, width = data.shape
    half = width // 2
    beams = steer.shape[0] // 2
    rows = beams // leaf
    shape = (leaf // 2, count, each, rows, width)

    def block(n):
        return n % (count // 2) * 2 + n // (count // 2)

    out_spec = pl.BlockSpec((leaf // 2, 1) + shape[2:], lambda n: (0, n, 0, 0, 0))
    return pl.pallas_call(
        functools.partial(image_kernel, (leaf, each, half, beams, bits_of(leaf))),
        grid=(count,),
        in_specs=[
            pl.BlockSpec((2, 1, each, pulses, width), lambda n: (0, block(n), 0, 0, 0)),
            pl.BlockSpec(steer.shape, lambda n: (0, 0)),
            pl.BlockSpec(interp.shape, lambda n: (0, 0, 0)),
            pl.BlockSpec((1,) + base.shape[1:], lambda n: (block(n), 0, 0)),
            pl.BlockSpec(step.shape, lambda n: (0, 0, 0, 0)),
        ],
        out_specs=[out_spec, out_spec],
        out_shape=[
            jax.ShapeDtypeStruct(shape, jnp.float32),
            jax.ShapeDtypeStruct(shape, jnp.bfloat16),
        ],
        compiler_params=pltpu.CompilerParams(vmem_limit_bytes=10 * 2**20),
        cost_estimate=pl.CostEstimate(
            flops=12 * beams * pulses * count * each * width,
            bytes_accessed=2 * data.size + 6 * count * each * beams * width // 2,
            transcendentals=0,
        ),
        name="image",
    )(data, steer, interp, base, step)


def fold(keep, got):
    stay, gone = (keep[:, n] + got[:, n].astype(jnp.float32) for n in range(2))
    return stay, gone.astype(jnp.bfloat16)


def last_kernel(keep_ref, got_ref, out_ref, rows_ref):
    blocks, rows, width = keep_ref.shape
    for i in range(blocks):
        value = keep_ref[i] + got_ref[i].astype(jnp.float32)
        for c in range(2):
            cols = slice(c * width // 2, (c + 1) * width // 2)
            rows_ref[c, pl.ds(i, rows, stride=blocks), :] = value[:, cols]
    both = jnp.concatenate([rows_ref[0], rows_ref[1]], axis=1)
    out_ref[...] = both.reshape(rows, blocks, width).astype(jnp.bfloat16)


def last_sum(keep, got):
    blocks, rows, width = keep.shape
    return pl.pallas_call(
        last_kernel,
        out_shape=jax.ShapeDtypeStruct((rows, blocks, width), jnp.bfloat16),
        scratch_shapes=[pltpu.VMEM((2, rows * blocks, width // 2), jnp.float32)],
        compiler_params=pltpu.CompilerParams(vmem_limit_bytes=8 * 2**20),
        name="last_sum",
    )(keep, got)


def interpolation(taps, beams):
    cells = jnp.arange(beams, dtype=jnp.int32)
    weights = jnp.array(WEIGHTS, jnp.float32)
    picks = taps[..., None] == cells
    return jnp.where(picks, weights[:, None], 0.0).sum(axis=-2)


def steering(slots, matrix, side, beams, pulses, scale):
    count = slots.shape[0]
    beam = jnp.arange(beams, dtype=jnp.int32)[:, None, None]
    place = jnp.arange(pulses, dtype=jnp.int32)
    slot = slots[None, :, None]
    cos, sin = unit(
        (2 * beam + 1 - beams) * (2 * place + 1 - pulses)
        + 3 * (beam + 1) * (2 * slot + 1) * (2 * place + 1),
        8 * pulses,
    )
    pair = jnp.concatenate([cos * scale, sin * scale], axis=2).astype(jnp.bfloat16)
    moved = jnp.dot(
        matrix.astype(jnp.bfloat16),
        pair.reshape(beams, count * 2 * pulses),
        preferred_element_type=jnp.float32,
    ).reshape(beams, count, 2 * pulses)
    re, im = moved[:, :, :pulses], moved[:, :, pulses:]
    row = jnp.arange(beams, dtype=jnp.int32)
    c, s = (t[:, None, None] for t in unit(row * row * (side + 1), PERIOD))
    re, im = c * re - s * im, c * im + s * re
    top = jnp.concatenate([re, -im], axis=2)
    low = jnp.concatenate([im, re], axis=2)
    return jnp.concatenate([top, low], axis=0).astype(jnp.bfloat16)


def per_device(echoes, chirp, taps, slots):
    leaf, turn = lax.axis_size("leaf"), lax.axis_size("turn")
    pulses, blocks, width = echoes.shape
    half = width // 2
    beams = taps.shape[2]
    levels = bits_of(leaf)
    far = (bits_of(turn) + 1) // 2 - 1
    top = bits_of(turn) - 1
    mids = 1 << far - 1
    high = turn >> far + 2
    tile = blocks // turn
    each = tile // 2
    rows = beams // leaf
    own_leaf, own_turn = lax.axis_index("leaf"), lax.axis_index("turn")

    keep_y, send_y = compress(chirp, echoes, high, mids, True, far, high)
    chirp, send_y = lax.optimization_barrier((chirp, send_y))
    got_y = swapped(send_y, "turn", 0)
    keep_z, send_z = compress(chirp, echoes, high, mids, False, far, 0)
    got_z = swapped(send_z, "turn", far)

    own_sides = [bit(own_leaf, level) for level in range(levels)]
    row = jnp.arange(beams, dtype=jnp.int32)
    part, place = row // rows, row % rows
    group = own_leaf ^ (2 * (part % (leaf // 2)) + part // (leaf // 2))
    orders = [row] * (levels - 1) + [group * rows + place]
    own_taps = [
        lax.dynamic_index_in_dim(taps[n], own_sides[n], 0, False) for n in range(levels)
    ]
    groups = own_taps[-1].reshape(leaf, rows, -1)
    own_taps[-1] = jnp.concatenate(
        [
            lax.dynamic_index_in_dim(groups, own_leaf ^ (2 * g + side), 0, False)
            for side in range(2)
            for g in range(leaf // 2)
        ],
        axis=0,
    )
    matrices = interpolation(jnp.stack(own_taps), beams)
    interp = jnp.concatenate([matrices[1:]] * 2, axis=-1).astype(jnp.bfloat16)
    scale = 1.0 / math.sqrt(2.0 * slots.shape[1] * pulses)
    wanted = own_turn ^ jnp.array([0, 1, 1 << far], jnp.int32)
    picked = jnp.arange(slots.shape[1], dtype=jnp.int32) == wanted[:, None]
    own_slots = jnp.where(picked, slots, 0).sum(axis=1)
    steer = steering(own_slots, matrices[0], own_sides[0], beams, pulses, scale)
    steer_y = steer[:, :2].reshape(2 * beams, 4 * pulses)
    steer_z = jnp.concatenate([steer[:, :1], steer[:, 2:]], axis=1).reshape(2 * beams, 4 * pulses)

    leans = jnp.stack([2 * order + 1 - beams for order in orders])
    bins = jnp.arange(each * half, dtype=jnp.int32) + 1
    slopes = jnp.stack([(2 * own_sides[n] - 1) * (n + 2) for n in range(levels)])[:, None] * leans
    step = jnp.stack(unit(slopes[:, :, None] * bins, PERIOD), axis=1)
    squares = jnp.stack(
        [orders[n] * orders[n] * (own_sides[n] + 1) * (1 if n else 0) for n in range(levels)]
    )

    def bases(tiles):
        parts = (2 * tiles[:, None] + jnp.arange(2, dtype=jnp.int32)).reshape(-1)
        start = (parts * each * half)[:, None, None]
        both = jnp.stack(unit(slopes * start + squares, PERIOD), axis=2)
        return both.reshape(parts.shape[0], 2 * levels, beams)

    index = jnp.arange(turn // 4, dtype=jnp.int32)
    tiles_y = turn // 2 + 2 * (index ^ (own_turn >> 1 & turn // 4 - 1)) + bit(own_turn, 0)
    low_part = (index ^ own_turn) & (1 << far) - 1
    high_part = index >> far ^ (own_turn >> far + 1 & high - 1)
    tiles_z = (high_part * 2 + bit(own_turn, far)) * (1 << far) + low_part

    pieces = []
    for name, keep, got, steer_own, tiles in (
        ("y", keep_y, got_y, steer_y, tiles_y),
        ("z", keep_z, got_z, steer_z, tiles_z),
    ):
        shape = (turn // 2, each, pulses, width)
        data = jnp.stack([keep.reshape(shape), got.reshape(shape)])
        kept, sent = backproject(data, steer_own, interp, bases(tiles), step, leaf)
        gone = 0 if name == "y" else far
        arrived = swapped(sent, "leaf", 0)
        parts = (leaf // 2, 2, turn // 4, each, rows, width)
        kept, arrived = kept.reshape(parts), arrived.reshape(parts)
        pieces.append([(kept[:, n], arrived[:, n], gone) for n in range(2)])

    states = {}
    for n in range(2):
        for chain in range(2):
            kept, arrived, gone = pieces[chain][n]
            leading = [("leaf", b) for b in range(levels - 1, 0, -1)]
            leading += [("turn", b) for b in range(top - 1, -1, -1) if b != gone]
            order = [("leaf", b) for b in range(1, levels)]
            rest = [("turn", b) for b in range(top) if b not in (0, far)]
            order = [("turn", 0)] + order if gone else order + [("turn", far)]
            states[n, chain] = [kept, arrived, leading, order + rest]
    for stage in range(len(states[0, 0][3])):
        ahead = states[0, 1][1]
        for (n, chain), state in states.items():
            kept, arrived, leading, order = state
            axis, b = order[stage]
            at = leading.index((axis, b))
            before, after = 1 << at, (1 << len(leading) - at - 1) * each
            leading.pop(at)
            split = (before, 2, after, rows, width)
            kept, sent = fold(kept.reshape(split), arrived.reshape(split))
            if stage and (n, chain) == (1, 0):
                sent, ahead = lax.optimization_barrier((sent, ahead))
            state[:2] = kept, swapped(sent, axis, b)
    shape = (each, rows, width)
    final = [
        [
            states[n, chain][0].reshape(shape)
            + states[n, chain][1].reshape(shape).astype(jnp.float32)
            for chain in range(2)
        ]
        for n in range(2)
    ]
    upper = bit(own_turn, top) == 1
    sent = jnp.stack([jnp.where(upper, second, first) for first, second in final])
    kept = jnp.stack([jnp.where(upper, first, second) for first, second in final])
    shape = (tile, rows, width)
    got = swapped(sent.astype(jnp.bfloat16), "turn", top)
    return last_sum(kept.reshape(shape), got.reshape(shape))


def solution(mesh):
    placed = (P(("leaf", "turn"), None, None), P(), P(), P("leaf", None))
    return jax.shard_map(
        per_device, mesh=mesh, in_specs=placed, out_specs=P("leaf", "turn", None), check_vma=False
    )
```

```python
import functools
import math

import jax
import jax.numpy as jnp
from jax import lax
from jax.experimental import pallas as pl
from jax.experimental.pallas import tpu as pltpu
from jax.sharding import PartitionSpec as P

WEIGHTS = (-1.0 / 32, 3.0 / 32, -7.0 / 32, 21.0 / 32, 21.0 / 32, -7.0 / 32, 3.0 / 32, -1.0 / 32)
PERIOD = 4096
VMEM_BYTES = 56 * 2**20


def bits_of(count):
    return count.bit_length() - 1


def bit(value, at):
    return value >> at & 1


def swapped(array, axis, bit):
    return lax.ppermute(array, axis, [(i, i ^ 1 << bit) for i in range(lax.axis_size(axis))])


def unit(phase_int, period):
    angle = jnp.remainder(phase_int, period).astype(jnp.float32) * (2.0 * math.pi / period)
    return jnp.cos(angle), jnp.sin(angle)


def compress_kernel(dims, has_edge, chirp_ref, echo_ref, *refs):
    tile, pulses, half, near_chain, far = dims
    edge_ref, refs = (refs[0], refs[1:]) if has_edge else (None, refs)
    keep_ref, send_ref, weights, rows_ref, carry = refs
    blocks = 2 * tile
    pitch = blocks + 1
    mids = pl.num_programs(2)
    high = pl.num_programs(0)
    turn = lax.axis_index("turn")
    spot_h = (high - 1 - pl.program_id(0)) ^ (turn >> far + 1 & high - 1)
    spot_m = (mids - 1 - pl.program_id(2)) ^ (turn >> 1 & mids - 1)
    spot_v = (1 - pl.program_id(1)) ^ bit(turn, far)
    own_u = bit(turn, 0)

    @pl.when((pl.program_id(0) == 0) & (pl.program_id(1) == 0) & (pl.program_id(2) == 0))
    def _():
        rows = lax.broadcasted_iota(jnp.int32, (half, half), 0)
        cols = lax.broadcasted_iota(jnp.int32, (half, half), 1)
        taps = chirp_ref[...].astype(jnp.float32)
        tables = []
        for c in range(2):
            wide = jnp.broadcast_to(taps[c : c + 1], (half, half))
            tables.append(pltpu.roll(wide, 0, 1, stride=1, stride_axis=0).T)
        for m, mask in enumerate((rows >= cols, rows < cols)):
            re, im = (jnp.where(mask, t, 0.0) for t in tables)
            top = jnp.concatenate([re, im], axis=1)
            low = jnp.concatenate([-im, re], axis=1)
            full = jnp.concatenate([top, low], axis=0)
            weights[m * 2 * half : (m + 1) * 2 * half, :] = full.astype(jnp.bfloat16)
        if has_edge:
            for p in range(pulses):
                for c in range(2):
                    first = edge_ref[p, :, c * half : (c + 1) * half].astype(jnp.float32)
                    rows_ref[c, p : p + 1, :] = first[:1]
            edges = [rows_ref[c, :pulses, :] for c in range(2)]
            carry[...] = jnp.concatenate(edges, axis=1).astype(jnp.bfloat16)
        else:
            carry[...] = jnp.zeros_like(carry)

    for p in range(pulses):
        for c in range(2):
            rows_ref[c, p * pitch : p * pitch + blocks, :] = echo_ref[
                p, :, c * half : (c + 1) * half
            ].astype(jnp.float32)
    turned = []
    for b in range(blocks):
        parts = [rows_ref[c, pl.ds(b, pulses, stride=pitch), :] for c in range(2)]
        turned.append(jnp.concatenate(parts, axis=1).astype(jnp.bfloat16))
    turned.append(carry[...])
    current = jnp.concatenate(turned[:-1], axis=0)
    after = jnp.concatenate(turned[1:], axis=0)
    total = jnp.dot(
        jnp.concatenate([current, after], axis=1),
        weights[...],
        preferred_element_type=jnp.float32,
    ).astype(jnp.bfloat16)
    carry[...] = turned[0]

    def block(b):
        return total[b * pulses : (b + 1) * pulses]

    if near_chain:
        for side in range(2):

            @pl.when(own_u == side)
            def _(side=side):
                for b in range(blocks):
                    ref = keep_ref if b // tile == side else send_ref
                    ref[0, 0, 0, b % tile] = block(b)
    else:
        for ref, mine in ((keep_ref, 0), (send_ref, 1)):

            @pl.when(spot_v == mine)
            def _(ref=ref):
                for b in range(blocks):
                    ref[spot_h, spot_m, b // tile ^ own_u, b % tile] = block(b)


def compress(chirp, echoes, high, mids, near_chain, far, first_high):
    pulses, blocks, width = echoes.shape
    half = width // 2
    tile = blocks // lax.axis_size("turn")
    if near_chain:
        shape = (high, 2, mids, tile, pulses, width)

        def place(h, v, m):
            turn = lax.axis_index("turn")
            spot_h = (high - 1 - h) ^ (turn >> far + 1 & high - 1)
            spot_m = (mids - 1 - m) ^ (turn >> 1 & mids - 1)
            return spot_h, (1 - v) ^ bit(turn, far), spot_m, 0, 0, 0

        spec = pl.BlockSpec((1, 1, 1) + shape[3:], place)
    else:
        shape = (high, mids, 2, tile, pulses, width)
        spec = pl.BlockSpec(shape, lambda h, v, m: (0, 0, 0, 0, 0, 0))
    def chunk(h, v, m):
        return 0, ((first_high + high - 1 - h) * 2 + 1 - v) * mids + mids - 1 - m, 0

    in_specs = [
        pl.BlockSpec((2, half), lambda h, v, m: (0, 0)),
        pl.BlockSpec((pulses, 2 * tile, width), chunk),
    ]
    operands = [chirp, echoes]
    has_edge = not near_chain
    if has_edge:
        after = (first_high + high) * 2 * mids
        in_specs.append(pl.BlockSpec((pulses, 2 * tile, width), lambda h, v, m: (0, after, 0)))
        operands.append(echoes)
    dims = (tile, pulses, half, near_chain, far)
    return pl.pallas_call(
        functools.partial(compress_kernel, dims, has_edge),
        grid=(high, 2, mids),
        in_specs=in_specs,
        out_specs=[spec, spec],
        out_shape=[jax.ShapeDtypeStruct(shape, jnp.bfloat16)] * 2,
        scratch_shapes=[
            pltpu.VMEM((2 * width, width), jnp.bfloat16),
            pltpu.VMEM((2, pulses * (2 * tile + 1), half), jnp.float32),
            pltpu.VMEM((pulses, width), jnp.bfloat16),
        ],
        compiler_params=pltpu.CompilerParams(
            vmem_limit_bytes=VMEM_BYTES if near_chain else 20 * 2**20
        ),
        cost_estimate=pl.CostEstimate(
            flops=2 * pulses * blocks * width * width,
            bytes_accessed=2 * pulses * blocks * width,
            transcendentals=0,
        ),
        name="compress",
    )(*operands)


def image_kernel(dims, data_ref, steer_ref, interp_ref, base_ref, step_ref, out_keep, out_send):
    leaf, each, half, beams, levels = dims
    rows = beams // leaf
    pair = 2
    piece = rows

    def turned(phase, re, im):
        c, s = phase
        return c * re - s * im, c * im + s * re

    bases = []
    for n in range(2 * levels):
        bases.append(jnp.broadcast_to(base_ref[0, n : n + 1, :], (half, beams)).T)

    def phased(level, block, first, re, im):
        cut = slice(first, first + piece)
        lanes = slice(block * half, (block + 1) * half)
        phase = turned(
            (bases[2 * level][cut], bases[2 * level + 1][cut]),
            step_ref[level, 0, cut, lanes],
            step_ref[level, 1, cut, lanes],
        )
        return turned(phase, re, im)

    for at in range(0, each, pair):
        parts = []
        for n in range(2):
            for c in range(2):
                cols = slice(c * half, (c + 1) * half)
                parts.append(
                    jnp.concatenate([data_ref[n, 0, at + i, :, cols] for i in range(pair)], axis=1)
                )
        raw = jnp.dot(
            steer_ref[...], jnp.concatenate(parts, axis=0), preferred_element_type=jnp.float32
        )
        re, im = raw[:beams], raw[beams:]
        for level in range(levels):
            columns = []
            for i in range(pair):
                lanes = slice(i * half, (i + 1) * half)
                pieces = []
                for first in range(0, beams, piece):
                    cut = slice(first, first + piece)
                    both = phased(level, at + i, first, re[cut, lanes], im[cut, lanes])
                    if level == levels - 1:
                        both = jnp.concatenate(both, axis=1)
                        g = first // rows
                        if g < leaf // 2:
                            out_keep[g, 0, at + i] = both
                        else:
                            out_send[g - leaf // 2, 0, at + i] = both.astype(jnp.bfloat16)
                        continue
                    both = jnp.concatenate(both, axis=1)
                    big = both.astype(jnp.bfloat16)
                    low = (both - big.astype(jnp.float32)).astype(jnp.bfloat16)
                    pieces.append((big, low))
                if pieces:
                    columns.append(
                        jnp.concatenate([p[0] for p in pieces] + [p[1] for p in pieces], axis=0)
                    )
            if columns:
                moved = jnp.dot(
                    interp_ref[level],
                    jnp.concatenate(columns, axis=1),
                    preferred_element_type=jnp.float32,
                )
                cuts = [moved[:, n * half : (n + 1) * half] for n in range(2 * pair)]
                re = jnp.concatenate(cuts[0::2], axis=1)
                im = jnp.concatenate(cuts[1::2], axis=1)


def backproject(data, steer, interp, base, step, leaf):
    _, count, each, pulses, width = data.shape
    half = width // 2
    beams = steer.shape[0] // 2
    rows = beams // leaf
    shape = (leaf // 2, count, each, rows, width)

    def block(n):
        return n % (count // 2) * 2 + n // (count // 2)

    out_spec = pl.BlockSpec((leaf // 2, 1) + shape[2:], lambda n: (0, n, 0, 0, 0))
    return pl.pallas_call(
        functools.partial(image_kernel, (leaf, each, half, beams, bits_of(leaf))),
        grid=(count,),
        in_specs=[
            pl.BlockSpec((2, 1, each, pulses, width), lambda n: (0, block(n), 0, 0, 0)),
            pl.BlockSpec(steer.shape, lambda n: (0, 0)),
            pl.BlockSpec(interp.shape, lambda n: (0, 0, 0)),
            pl.BlockSpec((1,) + base.shape[1:], lambda n: (block(n), 0, 0)),
            pl.BlockSpec(step.shape, lambda n: (0, 0, 0, 0)),
        ],
        out_specs=[out_spec, out_spec],
        out_shape=[
            jax.ShapeDtypeStruct(shape, jnp.float32),
            jax.ShapeDtypeStruct(shape, jnp.bfloat16),
        ],
        compiler_params=pltpu.CompilerParams(vmem_limit_bytes=10 * 2**20),
        cost_estimate=pl.CostEstimate(
            flops=12 * beams * pulses * count * each * width,
            bytes_accessed=2 * data.size + 6 * count * each * beams * width // 2,
            transcendentals=0,
        ),
        name="image",
    )(data, steer, interp, base, step)


def fold(keep, got):
    stay, gone = (keep[:, n] + got[:, n].astype(jnp.float32) for n in range(2))
    return stay, gone.astype(jnp.bfloat16)


def last_kernel(keep_ref, got_ref, out_ref, rows_ref):
    blocks, rows, width = keep_ref.shape
    for i in range(blocks):
        value = keep_ref[i] + got_ref[i].astype(jnp.float32)
        for c in range(2):
            cols = slice(c * width // 2, (c + 1) * width // 2)
            rows_ref[c, pl.ds(i, rows, stride=blocks), :] = value[:, cols]
    both = jnp.concatenate([rows_ref[0], rows_ref[1]], axis=1)
    out_ref[...] = both.reshape(rows, blocks, width).astype(jnp.bfloat16)


def last_sum(keep, got):
    blocks, rows, width = keep.shape
    return pl.pallas_call(
        last_kernel,
        out_shape=jax.ShapeDtypeStruct((rows, blocks, width), jnp.bfloat16),
        scratch_shapes=[pltpu.VMEM((2, rows * blocks, width // 2), jnp.float32)],
        compiler_params=pltpu.CompilerParams(vmem_limit_bytes=8 * 2**20),
        name="last_sum",
    )(keep, got)


def interpolation(taps, beams):
    cells = jnp.arange(beams, dtype=jnp.int32)
    weights = jnp.array(WEIGHTS, jnp.float32)
    picks = taps[..., None] == cells
    return jnp.where(picks, weights[:, None], 0.0).sum(axis=-2)


def steering(slots, matrix, side, beams, pulses, scale):
    count = slots.shape[0]
    beam = jnp.arange(beams, dtype=jnp.int32)[:, None, None]
    place = jnp.arange(pulses, dtype=jnp.int32)
    slot = slots[None, :, None]
    cos, sin = unit(
        (2 * beam + 1 - beams) * (2 * place + 1 - pulses)
        + 3 * (beam + 1) * (2 * slot + 1) * (2 * place + 1),
        8 * pulses,
    )
    pair = jnp.concatenate([cos * scale, sin * scale], axis=2).astype(jnp.bfloat16)
    moved = jnp.dot(
        matrix.astype(jnp.bfloat16),
        pair.reshape(beams, count * 2 * pulses),
        preferred_element_type=jnp.float32,
    ).reshape(beams, count, 2 * pulses)
    re, im = moved[:, :, :pulses], moved[:, :, pulses:]
    row = jnp.arange(beams, dtype=jnp.int32)
    c, s = (t[:, None, None] for t in unit(row * row * (side + 1), PERIOD))
    re, im = c * re - s * im, c * im + s * re
    top = jnp.concatenate([re, -im], axis=2)
    low = jnp.concatenate([im, re], axis=2)
    return jnp.concatenate([top, low], axis=0).astype(jnp.bfloat16)


def per_device(echoes, chirp, taps, slots):
    leaf, turn = lax.axis_size("leaf"), lax.axis_size("turn")
    pulses, blocks, width = echoes.shape
    half = width // 2
    beams = taps.shape[2]
    levels = bits_of(leaf)
    far = (bits_of(turn) + 1) // 2 - 1
    top = bits_of(turn) - 1
    mids = 1 << far - 1
    high = turn >> far + 2
    tile = blocks // turn
    each = tile // 2
    rows = beams // leaf
    own_leaf, own_turn = lax.axis_index("leaf"), lax.axis_index("turn")

    keep_y, send_y = compress(chirp, echoes, high, mids, True, far, high)
    chirp, send_y = lax.optimization_barrier((chirp, send_y))
    got_y = swapped(send_y, "turn", 0)
    keep_z, send_z = compress(chirp, echoes, high, mids, False, far, 0)
    got_z = swapped(send_z, "turn", far)

    own_sides = [bit(own_leaf, level) for level in range(levels)]
    row = jnp.arange(beams, dtype=jnp.int32)
    part, place = row // rows, row % rows
    group = own_leaf ^ (2 * (part % (leaf // 2)) + part // (leaf // 2))
    orders = [row] * (levels - 1) + [group * rows + place]
    own_taps = [
        lax.dynamic_index_in_dim(taps[n], own_sides[n], 0, False) for n in range(levels)
    ]
    groups = own_taps[-1].reshape(leaf, rows, -1)
    own_taps[-1] = jnp.concatenate(
        [
            lax.dynamic_index_in_dim(groups, own_leaf ^ (2 * g + side), 0, False)
            for side in range(2)
            for g in range(leaf // 2)
        ],
        axis=0,
    )
    matrices = interpolation(jnp.stack(own_taps), beams)
    interp = jnp.concatenate([matrices[1:]] * 2, axis=-1).astype(jnp.bfloat16)
    scale = 1.0 / math.sqrt(2.0 * slots.shape[1] * pulses)
    wanted = own_turn ^ jnp.array([0, 1, 1 << far], jnp.int32)
    picked = jnp.arange(slots.shape[1], dtype=jnp.int32) == wanted[:, None]
    own_slots = jnp.where(picked, slots, 0).sum(axis=1)
    steer = steering(own_slots, matrices[0], own_sides[0], beams, pulses, scale)
    steer_y = steer[:, :2].reshape(2 * beams, 4 * pulses)
    steer_z = jnp.concatenate([steer[:, :1], steer[:, 2:]], axis=1).reshape(2 * beams, 4 * pulses)

    leans = jnp.stack([2 * order + 1 - beams for order in orders])
    bins = jnp.arange(each * half, dtype=jnp.int32) + 1
    slopes = jnp.stack([(2 * own_sides[n] - 1) * (n + 2) for n in range(levels)])[:, None] * leans
    step = jnp.stack(unit(slopes[:, :, None] * bins, PERIOD), axis=1)
    squares = jnp.stack(
        [orders[n] * orders[n] * (own_sides[n] + 1) * (1 if n else 0) for n in range(levels)]
    )

    def bases(tiles):
        parts = (2 * tiles[:, None] + jnp.arange(2, dtype=jnp.int32)).reshape(-1)
        start = (parts * each * half)[:, None, None]
        both = jnp.stack(unit(slopes * start + squares, PERIOD), axis=2)
        return both.reshape(parts.shape[0], 2 * levels, beams)

    index = jnp.arange(turn // 4, dtype=jnp.int32)
    tiles_y = turn // 2 + 2 * (index ^ (own_turn >> 1 & turn // 4 - 1)) + bit(own_turn, 0)
    low_part = (index ^ own_turn) & (1 << far) - 1
    high_part = index >> far ^ (own_turn >> far + 1 & high - 1)
    tiles_z = (high_part * 2 + bit(own_turn, far)) * (1 << far) + low_part

    pieces = []
    for name, keep, got, steer_own, tiles in (
        ("y", keep_y, got_y, steer_y, tiles_y),
        ("z", keep_z, got_z, steer_z, tiles_z),
    ):
        shape = (turn // 2, each, pulses, width)
        data = jnp.stack([keep.reshape(shape), got.reshape(shape)])
        kept, sent = backproject(data, steer_own, interp, bases(tiles), step, leaf)
        gone = 0 if name == "y" else far
        arrived = swapped(sent, "leaf", 0)
        parts = (leaf // 2, 2, turn // 4, each, rows, width)
        kept, arrived = kept.reshape(parts), arrived.reshape(parts)
        pieces.append([(kept[:, n], arrived[:, n], gone) for n in range(2)])

    states = {}
    for n in range(2):
        for chain in range(2):
            kept, arrived, gone = pieces[chain][n]
            leading = [("leaf", b) for b in range(levels - 1, 0, -1)]
            leading += [("turn", b) for b in range(top - 1, -1, -1) if b != gone]
            order = [("leaf", b) for b in range(1, levels)]
            rest = [("turn", b) for b in range(top) if b not in (0, far)]
            order = [("turn", 0)] + order if gone else order + [("turn", far)]
            states[n, chain] = [kept, arrived, leading, order + rest]
    for stage in range(len(states[0, 0][3])):
        ahead = states[1, 1][1]
        for (n, chain), state in states.items():
            kept, arrived, leading, order = state
            axis, b = order[stage]
            at = leading.index((axis, b))
            before, after = 1 << at, (1 << len(leading) - at - 1) * each
            leading.pop(at)
            split = (before, 2, after, rows, width)
            kept, sent = fold(kept.reshape(split), arrived.reshape(split))
            if stage and (n, chain) == (0, 0):
                sent, ahead = lax.optimization_barrier((sent, ahead))
            state[:2] = kept, swapped(sent, axis, b)
    shape = (each, rows, width)
    final = [
        [
            states[n, chain][0].reshape(shape)
            + states[n, chain][1].reshape(shape).astype(jnp.float32)
            for chain in range(2)
        ]
        for n in range(2)
    ]
    upper = bit(own_turn, top) == 1
    sent = jnp.stack([jnp.where(upper, second, first) for first, second in final])
    kept = jnp.stack([jnp.where(upper, first, second) for first, second in final])
    shape = (tile, rows, width)
    got = swapped(sent.astype(jnp.bfloat16), "turn", top)
    return last_sum(kept.reshape(shape), got.reshape(shape))


def solution(mesh):
    placed = (P(("leaf", "turn"), None, None), P(), P(), P("leaf", None))
    return jax.shard_map(
        per_device, mesh=mesh, in_specs=placed, out_specs=P("leaf", "turn", None), check_vma=False
    )
```

```python
import functools
import math

import jax
import jax.numpy as jnp
from jax import lax
from jax.experimental import pallas as pl
from jax.experimental.pallas import tpu as pltpu
from jax.sharding import PartitionSpec as P

WEIGHTS = (-1.0 / 32, 3.0 / 32, -7.0 / 32, 21.0 / 32, 21.0 / 32, -7.0 / 32, 3.0 / 32, -1.0 / 32)
PERIOD = 4096
VMEM_BYTES = 56 * 2**20


def bits_of(count):
    return count.bit_length() - 1


def bit(value, at):
    return value >> at & 1


def swapped(array, axis, bit):
    return lax.ppermute(array, axis, [(i, i ^ 1 << bit) for i in range(lax.axis_size(axis))])


def unit(phase_int, period):
    angle = jnp.remainder(phase_int, period).astype(jnp.float32) * (2.0 * math.pi / period)
    return jnp.cos(angle), jnp.sin(angle)


def compress_kernel(dims, has_edge, chirp_ref, echo_ref, *refs):
    tile, pulses, half, near_chain, far = dims
    edge_ref, refs = (refs[0], refs[1:]) if has_edge else (None, refs)
    keep_ref, send_ref, weights, rows_ref, carry = refs
    blocks = 2 * tile
    pitch = blocks + 1
    mids = pl.num_programs(2)
    high = pl.num_programs(0)
    turn = lax.axis_index("turn")
    spot_h = (high - 1 - pl.program_id(0)) ^ (turn >> far + 1 & high - 1)
    spot_m = (mids - 1 - pl.program_id(2)) ^ (turn >> 1 & mids - 1)
    spot_v = (1 - pl.program_id(1)) ^ bit(turn, far)
    own_u = bit(turn, 0)

    @pl.when((pl.program_id(0) == 0) & (pl.program_id(1) == 0) & (pl.program_id(2) == 0))
    def _():
        rows = lax.broadcasted_iota(jnp.int32, (half, half), 0)
        cols = lax.broadcasted_iota(jnp.int32, (half, half), 1)
        taps = chirp_ref[...].astype(jnp.float32)
        tables = []
        for c in range(2):
            wide = jnp.broadcast_to(taps[c : c + 1], (half, half))
            tables.append(pltpu.roll(wide, 0, 1, stride=1, stride_axis=0).T)
        for m, mask in enumerate((rows >= cols, rows < cols)):
            re, im = (jnp.where(mask, t, 0.0) for t in tables)
            top = jnp.concatenate([re, im], axis=1)
            low = jnp.concatenate([-im, re], axis=1)
            full = jnp.concatenate([top, low], axis=0)
            weights[m * 2 * half : (m + 1) * 2 * half, :] = full.astype(jnp.bfloat16)
        if has_edge:
            for p in range(pulses):
                for c in range(2):
                    first = edge_ref[p, :, c * half : (c + 1) * half].astype(jnp.float32)
                    rows_ref[c, p : p + 1, :] = first[:1]
            edges = [rows_ref[c, :pulses, :] for c in range(2)]
            carry[...] = jnp.concatenate(edges, axis=1).astype(jnp.bfloat16)
        else:
            carry[...] = jnp.zeros_like(carry)

    for p in range(pulses):
        for c in range(2):
            rows_ref[c, p * pitch : p * pitch + blocks, :] = echo_ref[
                p, :, c * half : (c + 1) * half
            ].astype(jnp.float32)
    turned = []
    for b in range(blocks):
        parts = [rows_ref[c, pl.ds(b, pulses, stride=pitch), :] for c in range(2)]
        turned.append(jnp.concatenate(parts, axis=1).astype(jnp.bfloat16))
    turned.append(carry[...])
    current = jnp.concatenate(turned[:-1], axis=0)
    after = jnp.concatenate(turned[1:], axis=0)
    total = jnp.dot(
        jnp.concatenate([current, after], axis=1),
        weights[...],
        preferred_element_type=jnp.float32,
    ).astype(jnp.bfloat16)
    carry[...] = turned[0]

    def block(b):
        return total[b * pulses : (b + 1) * pulses]

    if near_chain:
        for side in range(2):

            @pl.when(own_u == side)
            def _(side=side):
                for b in range(blocks):
                    ref = keep_ref if b // tile == side else send_ref
                    ref[0, 0, 0, b % tile] = block(b)
    else:
        for ref, mine in ((keep_ref, 0), (send_ref, 1)):

            @pl.when(spot_v == mine)
            def _(ref=ref):
                for b in range(blocks):
                    ref[spot_h, spot_m, b // tile ^ own_u, b % tile] = block(b)


def compress(chirp, echoes, high, mids, near_chain, far, first_high):
    pulses, blocks, width = echoes.shape
    half = width // 2
    tile = blocks // lax.axis_size("turn")
    if near_chain:
        shape = (high, 2, mids, tile, pulses, width)

        def place(h, v, m):
            turn = lax.axis_index("turn")
            spot_h = (high - 1 - h) ^ (turn >> far + 1 & high - 1)
            spot_m = (mids - 1 - m) ^ (turn >> 1 & mids - 1)
            return spot_h, (1 - v) ^ bit(turn, far), spot_m, 0, 0, 0

        spec = pl.BlockSpec((1, 1, 1) + shape[3:], place)
    else:
        shape = (high, mids, 2, tile, pulses, width)
        spec = pl.BlockSpec(shape, lambda h, v, m: (0, 0, 0, 0, 0, 0))
    def chunk(h, v, m):
        return 0, ((first_high + high - 1 - h) * 2 + 1 - v) * mids + mids - 1 - m, 0

    in_specs = [
        pl.BlockSpec((2, half), lambda h, v, m: (0, 0)),
        pl.BlockSpec((pulses, 2 * tile, width), chunk),
    ]
    operands = [chirp, echoes]
    has_edge = not near_chain
    if has_edge:
        after = (first_high + high) * 2 * mids
        in_specs.append(pl.BlockSpec((pulses, 2 * tile, width), lambda h, v, m: (0, after, 0)))
        operands.append(echoes)
    dims = (tile, pulses, half, near_chain, far)
    return pl.pallas_call(
        functools.partial(compress_kernel, dims, has_edge),
        grid=(high, 2, mids),
        in_specs=in_specs,
        out_specs=[spec, spec],
        out_shape=[jax.ShapeDtypeStruct(shape, jnp.bfloat16)] * 2,
        scratch_shapes=[
            pltpu.VMEM((2 * width, width), jnp.bfloat16),
            pltpu.VMEM((2, pulses * (2 * tile + 1), half), jnp.float32),
            pltpu.VMEM((pulses, width), jnp.bfloat16),
        ],
        compiler_params=pltpu.CompilerParams(
            vmem_limit_bytes=VMEM_BYTES if near_chain else 20 * 2**20
        ),
        cost_estimate=pl.CostEstimate(
            flops=2 * pulses * blocks * width * width,
            bytes_accessed=2 * pulses * blocks * width,
            transcendentals=0,
        ),
        name="compress",
    )(*operands)


def image_kernel(dims, data_ref, steer_ref, interp_ref, base_ref, step_ref, out_keep, out_send):
    leaf, each, half, beams, levels = dims
    rows = beams // leaf
    pair = 2
    piece = rows

    def turned(phase, re, im):
        c, s = phase
        return c * re - s * im, c * im + s * re

    bases = []
    for n in range(2 * levels):
        bases.append(jnp.broadcast_to(base_ref[0, n : n + 1, :], (half, beams)).T)

    def phased(level, block, first, re, im):
        cut = slice(first, first + piece)
        lanes = slice(block * half, (block + 1) * half)
        phase = turned(
            (bases[2 * level][cut], bases[2 * level + 1][cut]),
            step_ref[level, 0, cut, lanes],
            step_ref[level, 1, cut, lanes],
        )
        return turned(phase, re, im)

    for at in range(0, each, pair):
        parts = []
        for n in range(2):
            for c in range(2):
                cols = slice(c * half, (c + 1) * half)
                parts.append(
                    jnp.concatenate([data_ref[n, 0, at + i, :, cols] for i in range(pair)], axis=1)
                )
        raw = jnp.dot(
            steer_ref[...], jnp.concatenate(parts, axis=0), preferred_element_type=jnp.float32
        )
        re, im = raw[:beams], raw[beams:]
        for level in range(levels):
            columns = []
            for i in range(pair):
                lanes = slice(i * half, (i + 1) * half)
                pieces = []
                for first in range(0, beams, piece):
                    cut = slice(first, first + piece)
                    both = phased(level, at + i, first, re[cut, lanes], im[cut, lanes])
                    if level == levels - 1:
                        both = jnp.concatenate(both, axis=1)
                        g = first // rows
                        if g < leaf // 2:
                            out_keep[g, 0, at + i] = both.astype(jnp.bfloat16)
                        else:
                            out_send[g - leaf // 2, 0, at + i] = both.astype(jnp.bfloat16)
                        continue
                    both = jnp.concatenate(both, axis=1)
                    big = both.astype(jnp.bfloat16)
                    low = (both - big.astype(jnp.float32)).astype(jnp.bfloat16)
                    pieces.append((big, low))
                if pieces:
                    columns.append(
                        jnp.concatenate([p[0] for p in pieces] + [p[1] for p in pieces], axis=0)
                    )
            if columns:
                moved = jnp.dot(
                    interp_ref[level],
                    jnp.concatenate(columns, axis=1),
                    preferred_element_type=jnp.float32,
                )
                cuts = [moved[:, n * half : (n + 1) * half] for n in range(2 * pair)]
                re = jnp.concatenate(cuts[0::2], axis=1)
                im = jnp.concatenate(cuts[1::2], axis=1)


def backproject(data, steer, interp, base, step, leaf):
    _, count, each, pulses, width = data.shape
    half = width // 2
    beams = steer.shape[0] // 2
    rows = beams // leaf
    shape = (leaf // 2, count, each, rows, width)

    def block(n):
        return n % (count // 2) * 2 + n // (count // 2)

    out_spec = pl.BlockSpec((leaf // 2, 1) + shape[2:], lambda n: (0, n, 0, 0, 0))
    return pl.pallas_call(
        functools.partial(image_kernel, (leaf, each, half, beams, bits_of(leaf))),
        grid=(count,),
        in_specs=[
            pl.BlockSpec((2, 1, each, pulses, width), lambda n: (0, block(n), 0, 0, 0)),
            pl.BlockSpec(steer.shape, lambda n: (0, 0)),
            pl.BlockSpec(interp.shape, lambda n: (0, 0, 0)),
            pl.BlockSpec((1,) + base.shape[1:], lambda n: (block(n), 0, 0)),
            pl.BlockSpec(step.shape, lambda n: (0, 0, 0, 0)),
        ],
        out_specs=[out_spec, out_spec],
        out_shape=[
            jax.ShapeDtypeStruct(shape, jnp.bfloat16),
            jax.ShapeDtypeStruct(shape, jnp.bfloat16),
        ],
        compiler_params=pltpu.CompilerParams(vmem_limit_bytes=10 * 2**20),
        cost_estimate=pl.CostEstimate(
            flops=12 * beams * pulses * count * each * width,
            bytes_accessed=2 * data.size + 6 * count * each * beams * width // 2,
            transcendentals=0,
        ),
        name="image",
    )(data, steer, interp, base, step)


def fold(keep, got):
    stay, gone = (keep[:, n] + got[:, n].astype(jnp.float32) for n in range(2))
    return stay, gone.astype(jnp.bfloat16)


def last_kernel(keep_ref, got_ref, out_ref, rows_ref):
    blocks, rows, width = keep_ref.shape
    for i in range(blocks):
        value = keep_ref[i] + got_ref[i].astype(jnp.float32)
        for c in range(2):
            cols = slice(c * width // 2, (c + 1) * width // 2)
            rows_ref[c, pl.ds(i, rows, stride=blocks), :] = value[:, cols]
    both = jnp.concatenate([rows_ref[0], rows_ref[1]], axis=1)
    out_ref[...] = both.reshape(rows, blocks, width).astype(jnp.bfloat16)


def last_sum(keep, got):
    blocks, rows, width = keep.shape
    return pl.pallas_call(
        last_kernel,
        out_shape=jax.ShapeDtypeStruct((rows, blocks, width), jnp.bfloat16),
        scratch_shapes=[pltpu.VMEM((2, rows * blocks, width // 2), jnp.float32)],
        compiler_params=pltpu.CompilerParams(vmem_limit_bytes=8 * 2**20),
        name="last_sum",
    )(keep, got)


def interpolation(taps, beams):
    cells = jnp.arange(beams, dtype=jnp.int32)
    weights = jnp.array(WEIGHTS, jnp.float32)
    picks = taps[..., None] == cells
    return jnp.where(picks, weights[:, None], 0.0).sum(axis=-2)


def steering(slots, matrix, side, beams, pulses, scale):
    count = slots.shape[0]
    beam = jnp.arange(beams, dtype=jnp.int32)[:, None, None]
    place = jnp.arange(pulses, dtype=jnp.int32)
    slot = slots[None, :, None]
    cos, sin = unit(
        (2 * beam + 1 - beams) * (2 * place + 1 - pulses)
        + 3 * (beam + 1) * (2 * slot + 1) * (2 * place + 1),
        8 * pulses,
    )
    pair = jnp.concatenate([cos * scale, sin * scale], axis=2).astype(jnp.bfloat16)
    moved = jnp.dot(
        matrix.astype(jnp.bfloat16),
        pair.reshape(beams, count * 2 * pulses),
        preferred_element_type=jnp.float32,
    ).reshape(beams, count, 2 * pulses)
    re, im = moved[:, :, :pulses], moved[:, :, pulses:]
    row = jnp.arange(beams, dtype=jnp.int32)
    c, s = (t[:, None, None] for t in unit(row * row * (side + 1), PERIOD))
    re, im = c * re - s * im, c * im + s * re
    top = jnp.concatenate([re, -im], axis=2)
    low = jnp.concatenate([im, re], axis=2)
    return jnp.concatenate([top, low], axis=0).astype(jnp.bfloat16)


def per_device(echoes, chirp, taps, slots):
    leaf, turn = lax.axis_size("leaf"), lax.axis_size("turn")
    pulses, blocks, width = echoes.shape
    half = width // 2
    beams = taps.shape[2]
    levels = bits_of(leaf)
    far = (bits_of(turn) + 1) // 2 - 1
    top = bits_of(turn) - 1
    mids = 1 << far - 1
    high = turn >> far + 2
    tile = blocks // turn
    each = tile // 2
    rows = beams // leaf
    own_leaf, own_turn = lax.axis_index("leaf"), lax.axis_index("turn")

    keep_y, send_y = compress(chirp, echoes, high, mids, True, far, high)
    chirp, send_y = lax.optimization_barrier((chirp, send_y))
    got_y = swapped(send_y, "turn", 0)
    keep_z, send_z = compress(chirp, echoes, high, mids, False, far, 0)
    got_z = swapped(send_z, "turn", far)

    own_sides = [bit(own_leaf, level) for level in range(levels)]
    row = jnp.arange(beams, dtype=jnp.int32)
    part, place = row // rows, row % rows
    group = own_leaf ^ (2 * (part % (leaf // 2)) + part // (leaf // 2))
    orders = [row] * (levels - 1) + [group * rows + place]
    own_taps = [
        lax.dynamic_index_in_dim(taps[n], own_sides[n], 0, False) for n in range(levels)
    ]
    groups = own_taps[-1].reshape(leaf, rows, -1)
    own_taps[-1] = jnp.concatenate(
        [
            lax.dynamic_index_in_dim(groups, own_leaf ^ (2 * g + side), 0, False)
            for side in range(2)
            for g in range(leaf // 2)
        ],
        axis=0,
    )
    matrices = interpolation(jnp.stack(own_taps), beams)
    interp = jnp.concatenate([matrices[1:]] * 2, axis=-1).astype(jnp.bfloat16)
    scale = 1.0 / math.sqrt(2.0 * slots.shape[1] * pulses)
    wanted = own_turn ^ jnp.array([0, 1, 1 << far], jnp.int32)
    picked = jnp.arange(slots.shape[1], dtype=jnp.int32) == wanted[:, None]
    own_slots = jnp.where(picked, slots, 0).sum(axis=1)
    steer = steering(own_slots, matrices[0], own_sides[0], beams, pulses, scale)
    steer_y = steer[:, :2].reshape(2 * beams, 4 * pulses)
    steer_z = jnp.concatenate([steer[:, :1], steer[:, 2:]], axis=1).reshape(2 * beams, 4 * pulses)

    leans = jnp.stack([2 * order + 1 - beams for order in orders])
    bins = jnp.arange(each * half, dtype=jnp.int32) + 1
    slopes = jnp.stack([(2 * own_sides[n] - 1) * (n + 2) for n in range(levels)])[:, None] * leans
    step = jnp.stack(unit(slopes[:, :, None] * bins, PERIOD), axis=1)
    squares = jnp.stack(
        [orders[n] * orders[n] * (own_sides[n] + 1) * (1 if n else 0) for n in range(levels)]
    )

    def bases(tiles):
        parts = (2 * tiles[:, None] + jnp.arange(2, dtype=jnp.int32)).reshape(-1)
        start = (parts * each * half)[:, None, None]
        both = jnp.stack(unit(slopes * start + squares, PERIOD), axis=2)
        return both.reshape(parts.shape[0], 2 * levels, beams)

    index = jnp.arange(turn // 4, dtype=jnp.int32)
    tiles_y = turn // 2 + 2 * (index ^ (own_turn >> 1 & turn // 4 - 1)) + bit(own_turn, 0)
    low_part = (index ^ own_turn) & (1 << far) - 1
    high_part = index >> far ^ (own_turn >> far + 1 & high - 1)
    tiles_z = (high_part * 2 + bit(own_turn, far)) * (1 << far) + low_part

    pieces = []
    for name, keep, got, steer_own, tiles in (
        ("y", keep_y, got_y, steer_y, tiles_y),
        ("z", keep_z, got_z, steer_z, tiles_z),
    ):
        shape = (turn // 2, each, pulses, width)
        data = jnp.stack([keep.reshape(shape), got.reshape(shape)])
        kept, sent = backproject(data, steer_own, interp, bases(tiles), step, leaf)
        gone = 0 if name == "y" else far
        arrived = swapped(sent, "leaf", 0)
        parts = (leaf // 2, 2, turn // 4, each, rows, width)
        kept, arrived = kept.reshape(parts), arrived.reshape(parts)
        pieces.append([(kept[:, n], arrived[:, n], gone) for n in range(2)])

    final = [[], []]
    for n in range(2):
        for chain in range(2):
            kept, arrived, gone = pieces[chain][n]
            leading = [("leaf", b) for b in range(levels - 1, 0, -1)]
            leading += [("turn", b) for b in range(top - 1, -1, -1) if b != gone]
            order = [("leaf", b) for b in range(1, levels)]
            rest = [("turn", b) for b in range(top) if b not in (0, far)]
            order = [("turn", 0)] + order if gone else order + [("turn", far)]
            for axis, b in order + rest:
                at = leading.index((axis, b))
                before, after = 1 << at, (1 << len(leading) - at - 1) * each
                leading.pop(at)
                split = (before, 2, after, rows, width)
                kept, sent = fold(kept.reshape(split), arrived.reshape(split))
                arrived = swapped(sent, axis, b)
            shape = (each, rows, width)
            total = kept.reshape(shape) + arrived.reshape(shape).astype(jnp.float32)
            final[n].append(total)
    upper = bit(own_turn, top) == 1
    sent = jnp.stack([jnp.where(upper, second, first) for first, second in final])
    kept = jnp.stack([jnp.where(upper, first, second) for first, second in final])
    shape = (tile, rows, width)
    got = swapped(sent.astype(jnp.bfloat16), "turn", top)
    return last_sum(kept.reshape(shape), got.reshape(shape))


def solution(mesh):
    placed = (P(("leaf", "turn"), None, None), P(), P(), P("leaf", None))
    return jax.shard_map(
        per_device, mesh=mesh, in_specs=placed, out_specs=P("leaf", "turn", None), check_vma=False
    )
```

```python
import functools
import math

import jax
import jax.numpy as jnp
from jax import lax
from jax.experimental import pallas as pl
from jax.experimental.pallas import tpu as pltpu
from jax.sharding import PartitionSpec as P

WEIGHTS = (-1.0 / 32, 3.0 / 32, -7.0 / 32, 21.0 / 32, 21.0 / 32, -7.0 / 32, 3.0 / 32, -1.0 / 32)
PERIOD = 4096
VMEM_BYTES = 56 * 2**20


def bits_of(count):
    return count.bit_length() - 1


def bit(value, at):
    return value >> at & 1


def swapped(array, axis, bit):
    return lax.ppermute(array, axis, [(i, i ^ 1 << bit) for i in range(lax.axis_size(axis))])


def unit(phase_int, period):
    angle = jnp.remainder(phase_int, period).astype(jnp.float32) * (2.0 * math.pi / period)
    return jnp.cos(angle), jnp.sin(angle)


def compress_kernel(dims, has_edge, chirp_ref, echo_ref, *refs):
    tile, pulses, half, near_chain, far = dims
    edge_ref, refs = (refs[0], refs[1:]) if has_edge else (None, refs)
    keep_ref, send_ref, weights, rows_ref, carry = refs
    blocks = 2 * tile
    pitch = blocks + 1
    mids = pl.num_programs(2)
    high = pl.num_programs(0)
    turn = lax.axis_index("turn")
    spot_h = (high - 1 - pl.program_id(0)) ^ (turn >> far + 1 & high - 1)
    spot_m = (mids - 1 - pl.program_id(2)) ^ (turn >> 1 & mids - 1)
    spot_v = (1 - pl.program_id(1)) ^ bit(turn, far)
    own_u = bit(turn, 0)

    @pl.when((pl.program_id(0) == 0) & (pl.program_id(1) == 0) & (pl.program_id(2) == 0))
    def _():
        rows = lax.broadcasted_iota(jnp.int32, (half, half), 0)
        cols = lax.broadcasted_iota(jnp.int32, (half, half), 1)
        taps = chirp_ref[...].astype(jnp.float32)
        tables = []
        for c in range(2):
            wide = jnp.broadcast_to(taps[c : c + 1], (half, half))
            tables.append(pltpu.roll(wide, 0, 1, stride=1, stride_axis=0).T)
        for m, mask in enumerate((rows >= cols, rows < cols)):
            re, im = (jnp.where(mask, t, 0.0) for t in tables)
            top = jnp.concatenate([re, im], axis=1)
            low = jnp.concatenate([-im, re], axis=1)
            full = jnp.concatenate([top, low], axis=0)
            weights[m * 2 * half : (m + 1) * 2 * half, :] = full.astype(jnp.bfloat16)
        if has_edge:
            for p in range(pulses):
                for c in range(2):
                    first = edge_ref[p, :, c * half : (c + 1) * half].astype(jnp.float32)
                    rows_ref[c, p : p + 1, :] = first[:1]
            edges = [rows_ref[c, :pulses, :] for c in range(2)]
            carry[...] = jnp.concatenate(edges, axis=1).astype(jnp.bfloat16)
        else:
            carry[...] = jnp.zeros_like(carry)

    for p in range(pulses):
        for c in range(2):
            rows_ref[c, p * pitch : p * pitch + blocks, :] = echo_ref[
                p, :, c * half : (c + 1) * half
            ].astype(jnp.float32)
    turned = []
    for b in range(blocks):
        parts = [rows_ref[c, pl.ds(b, pulses, stride=pitch), :] for c in range(2)]
        turned.append(jnp.concatenate(parts, axis=1).astype(jnp.bfloat16))
    turned.append(carry[...])
    current = jnp.concatenate(turned[:-1], axis=0)
    after = jnp.concatenate(turned[1:], axis=0)
    total = jnp.dot(
        jnp.concatenate([current, after], axis=1),
        weights[...],
        preferred_element_type=jnp.float32,
    ).astype(jnp.bfloat16)
    carry[...] = turned[0]

    def block(b):
        return total[b * pulses : (b + 1) * pulses]

    if near_chain:
        for side in range(2):

            @pl.when(own_u == side)
            def _(side=side):
                for b in range(blocks):
                    ref = keep_ref if b // tile == side else send_ref
                    ref[0, 0, 0, b % tile] = block(b)
    else:
        for ref, mine in ((keep_ref, 0), (send_ref, 1)):

            @pl.when(spot_v == mine)
            def _(ref=ref):
                for b in range(blocks):
                    ref[spot_h, spot_m, b // tile ^ own_u, b % tile] = block(b)


def compress(chirp, echoes, high, mids, near_chain, far, first_high):
    pulses, blocks, width = echoes.shape
    half = width // 2
    tile = blocks // lax.axis_size("turn")
    if near_chain:
        shape = (high, 2, mids, tile, pulses, width)

        def place(h, v, m):
            turn = lax.axis_index("turn")
            spot_h = (high - 1 - h) ^ (turn >> far + 1 & high - 1)
            spot_m = (mids - 1 - m) ^ (turn >> 1 & mids - 1)
            return spot_h, (1 - v) ^ bit(turn, far), spot_m, 0, 0, 0

        spec = pl.BlockSpec((1, 1, 1) + shape[3:], place)
    else:
        shape = (high, mids, 2, tile, pulses, width)
        spec = pl.BlockSpec(shape, lambda h, v, m: (0, 0, 0, 0, 0, 0))
    def chunk(h, v, m):
        return 0, ((first_high + high - 1 - h) * 2 + 1 - v) * mids + mids - 1 - m, 0

    in_specs = [
        pl.BlockSpec((2, half), lambda h, v, m: (0, 0)),
        pl.BlockSpec((pulses, 2 * tile, width), chunk),
    ]
    operands = [chirp, echoes]
    has_edge = not near_chain
    if has_edge:
        after = (first_high + high) * 2 * mids
        in_specs.append(pl.BlockSpec((pulses, 2 * tile, width), lambda h, v, m: (0, after, 0)))
        operands.append(echoes)
    dims = (tile, pulses, half, near_chain, far)
    return pl.pallas_call(
        functools.partial(compress_kernel, dims, has_edge),
        grid=(high, 2, mids),
        in_specs=in_specs,
        out_specs=[spec, spec],
        out_shape=[jax.ShapeDtypeStruct(shape, jnp.bfloat16)] * 2,
        scratch_shapes=[
            pltpu.VMEM((2 * width, width), jnp.bfloat16),
            pltpu.VMEM((2, pulses * (2 * tile + 1), half), jnp.float32),
            pltpu.VMEM((pulses, width), jnp.bfloat16),
        ],
        compiler_params=pltpu.CompilerParams(
            vmem_limit_bytes=20 * 2**20 if near_chain else VMEM_BYTES
        ),
        cost_estimate=pl.CostEstimate(
            flops=2 * pulses * blocks * width * width,
            bytes_accessed=2 * pulses * blocks * width,
            transcendentals=0,
        ),
        name="compress",
    )(*operands)


def image_kernel(dims, data_ref, steer_ref, interp_ref, base_ref, step_ref, out_keep, out_send):
    leaf, each, half, beams, levels = dims
    rows = beams // leaf
    pair = 2
    piece = rows

    def turned(phase, re, im):
        c, s = phase
        return c * re - s * im, c * im + s * re

    bases = []
    for n in range(2 * levels):
        bases.append(jnp.broadcast_to(base_ref[0, n : n + 1, :], (half, beams)).T)

    def phased(level, block, first, re, im):
        cut = slice(first, first + piece)
        lanes = slice(block * half, (block + 1) * half)
        phase = turned(
            (bases[2 * level][cut], bases[2 * level + 1][cut]),
            step_ref[level, 0, cut, lanes],
            step_ref[level, 1, cut, lanes],
        )
        return turned(phase, re, im)

    for at in range(0, each, pair):
        parts = []
        for n in range(2):
            for c in range(2):
                cols = slice(c * half, (c + 1) * half)
                parts.append(
                    jnp.concatenate([data_ref[n, 0, at + i, :, cols] for i in range(pair)], axis=1)
                )
        raw = jnp.dot(
            steer_ref[...], jnp.concatenate(parts, axis=0), preferred_element_type=jnp.float32
        )
        re, im = raw[:beams], raw[beams:]
        for level in range(levels):
            columns = []
            for i in range(pair):
                lanes = slice(i * half, (i + 1) * half)
                pieces = []
                for first in range(0, beams, piece):
                    cut = slice(first, first + piece)
                    both = phased(level, at + i, first, re[cut, lanes], im[cut, lanes])
                    if level == levels - 1:
                        both = jnp.concatenate(both, axis=1)
                        g = first // rows
                        if g < leaf // 2:
                            out_keep[g, 0, at + i] = both.astype(jnp.bfloat16)
                        else:
                            out_send[g - leaf // 2, 0, at + i] = both.astype(jnp.bfloat16)
                        continue
                    both = jnp.concatenate(both, axis=1)
                    big = both.astype(jnp.bfloat16)
                    low = (both - big.astype(jnp.float32)).astype(jnp.bfloat16)
                    pieces.append((big, low))
                if pieces:
                    columns.append(
                        jnp.concatenate([p[0] for p in pieces] + [p[1] for p in pieces], axis=0)
                    )
            if columns:
                moved = jnp.dot(
                    interp_ref[level],
                    jnp.concatenate(columns, axis=1),
                    preferred_element_type=jnp.float32,
                )
                cuts = [moved[:, n * half : (n + 1) * half] for n in range(2 * pair)]
                re = jnp.concatenate(cuts[0::2], axis=1)
                im = jnp.concatenate(cuts[1::2], axis=1)


def backproject(data, steer, interp, base, step, leaf):
    _, count, each, pulses, width = data.shape
    half = width // 2
    beams = steer.shape[0] // 2
    rows = beams // leaf
    shape = (leaf // 2, count, each, rows, width)

    def block(n):
        return n % (count // 2) * 2 + n // (count // 2)

    out_spec = pl.BlockSpec((leaf // 2, 1) + shape[2:], lambda n: (0, n, 0, 0, 0))
    return pl.pallas_call(
        functools.partial(image_kernel, (leaf, each, half, beams, bits_of(leaf))),
        grid=(count,),
        in_specs=[
            pl.BlockSpec((2, 1, each, pulses, width), lambda n: (0, block(n), 0, 0, 0)),
            pl.BlockSpec(steer.shape, lambda n: (0, 0)),
            pl.BlockSpec(interp.shape, lambda n: (0, 0, 0)),
            pl.BlockSpec((1,) + base.shape[1:], lambda n: (block(n), 0, 0)),
            pl.BlockSpec(step.shape, lambda n: (0, 0, 0, 0)),
        ],
        out_specs=[out_spec, out_spec],
        out_shape=[
            jax.ShapeDtypeStruct(shape, jnp.bfloat16),
            jax.ShapeDtypeStruct(shape, jnp.bfloat16),
        ],
        compiler_params=pltpu.CompilerParams(vmem_limit_bytes=10 * 2**20),
        cost_estimate=pl.CostEstimate(
            flops=12 * beams * pulses * count * each * width,
            bytes_accessed=2 * data.size + 6 * count * each * beams * width // 2,
            transcendentals=0,
        ),
        name="image",
    )(data, steer, interp, base, step)


def fold(keep, got):
    stay, gone = (keep[:, n] + got[:, n].astype(jnp.float32) for n in range(2))
    return stay, gone.astype(jnp.bfloat16)


def last_kernel(keep_ref, got_ref, out_ref, rows_ref):
    blocks, rows, width = keep_ref.shape
    for i in range(blocks):
        value = keep_ref[i] + got_ref[i].astype(jnp.float32)
        for c in range(2):
            cols = slice(c * width // 2, (c + 1) * width // 2)
            rows_ref[c, pl.ds(i, rows, stride=blocks), :] = value[:, cols]
    both = jnp.concatenate([rows_ref[0], rows_ref[1]], axis=1)
    out_ref[...] = both.reshape(rows, blocks, width).astype(jnp.bfloat16)


def last_sum(keep, got):
    blocks, rows, width = keep.shape
    return pl.pallas_call(
        last_kernel,
        out_shape=jax.ShapeDtypeStruct((rows, blocks, width), jnp.bfloat16),
        scratch_shapes=[pltpu.VMEM((2, rows * blocks, width // 2), jnp.float32)],
        compiler_params=pltpu.CompilerParams(vmem_limit_bytes=8 * 2**20),
        name="last_sum",
    )(keep, got)


def interpolation(taps, beams):
    cells = jnp.arange(beams, dtype=jnp.int32)
    weights = jnp.array(WEIGHTS, jnp.float32)
    picks = taps[..., None] == cells
    return jnp.where(picks, weights[:, None], 0.0).sum(axis=-2)


def steering(slots, matrix, side, beams, pulses, scale):
    count = slots.shape[0]
    beam = jnp.arange(beams, dtype=jnp.int32)[:, None, None]
    place = jnp.arange(pulses, dtype=jnp.int32)
    slot = slots[None, :, None]
    cos, sin = unit(
        (2 * beam + 1 - beams) * (2 * place + 1 - pulses)
        + 3 * (beam + 1) * (2 * slot + 1) * (2 * place + 1),
        8 * pulses,
    )
    pair = jnp.concatenate([cos * scale, sin * scale], axis=2).astype(jnp.bfloat16)
    moved = jnp.dot(
        matrix.astype(jnp.bfloat16),
        pair.reshape(beams, count * 2 * pulses),
        preferred_element_type=jnp.float32,
    ).reshape(beams, count, 2 * pulses)
    re, im = moved[:, :, :pulses], moved[:, :, pulses:]
    row = jnp.arange(beams, dtype=jnp.int32)
    c, s = (t[:, None, None] for t in unit(row * row * (side + 1), PERIOD))
    re, im = c * re - s * im, c * im + s * re
    top = jnp.concatenate([re, -im], axis=2)
    low = jnp.concatenate([im, re], axis=2)
    return jnp.concatenate([top, low], axis=0).astype(jnp.bfloat16)


def per_device(echoes, chirp, taps, slots):
    leaf, turn = lax.axis_size("leaf"), lax.axis_size("turn")
    pulses, blocks, width = echoes.shape
    half = width // 2
    beams = taps.shape[2]
    levels = bits_of(leaf)
    far = (bits_of(turn) + 1) // 2 - 1
    top = bits_of(turn) - 1
    mids = 1 << far - 1
    high = turn >> far + 2
    tile = blocks // turn
    each = tile // 2
    rows = beams // leaf
    own_leaf, own_turn = lax.axis_index("leaf"), lax.axis_index("turn")

    keep_z, send_z = compress(chirp, echoes, high, mids, False, far, 0)
    chirp, send_z = lax.optimization_barrier((chirp, send_z))
    got_z = swapped(send_z, "turn", far)
    keep_y, send_y = compress(chirp, echoes, high, mids, True, far, high)
    got_y = swapped(send_y, "turn", 0)

    own_sides = [bit(own_leaf, level) for level in range(levels)]
    row = jnp.arange(beams, dtype=jnp.int32)
    part, place = row // rows, row % rows
    group = own_leaf ^ (2 * (part % (leaf // 2)) + part // (leaf // 2))
    orders = [row] * (levels - 1) + [group * rows + place]
    own_taps = [
        lax.dynamic_index_in_dim(taps[n], own_sides[n], 0, False) for n in range(levels)
    ]
    groups = own_taps[-1].reshape(leaf, rows, -1)
    own_taps[-1] = jnp.concatenate(
        [
            lax.dynamic_index_in_dim(groups, own_leaf ^ (2 * g + side), 0, False)
            for side in range(2)
            for g in range(leaf // 2)
        ],
        axis=0,
    )
    matrices = interpolation(jnp.stack(own_taps), beams)
    interp = jnp.concatenate([matrices[1:]] * 2, axis=-1).astype(jnp.bfloat16)
    scale = 1.0 / math.sqrt(2.0 * slots.shape[1] * pulses)
    wanted = own_turn ^ jnp.array([0, 1, 1 << far], jnp.int32)
    picked = jnp.arange(slots.shape[1], dtype=jnp.int32) == wanted[:, None]
    own_slots = jnp.where(picked, slots, 0).sum(axis=1)
    steer = steering(own_slots, matrices[0], own_sides[0], beams, pulses, scale)
    steer_y = steer[:, :2].reshape(2 * beams, 4 * pulses)
    steer_z = jnp.concatenate([steer[:, :1], steer[:, 2:]], axis=1).reshape(2 * beams, 4 * pulses)

    leans = jnp.stack([2 * order + 1 - beams for order in orders])
    bins = jnp.arange(each * half, dtype=jnp.int32) + 1
    slopes = jnp.stack([(2 * own_sides[n] - 1) * (n + 2) for n in range(levels)])[:, None] * leans
    step = jnp.stack(unit(slopes[:, :, None] * bins, PERIOD), axis=1)
    squares = jnp.stack(
        [orders[n] * orders[n] * (own_sides[n] + 1) * (1 if n else 0) for n in range(levels)]
    )

    def bases(tiles):
        parts = (2 * tiles[:, None] + jnp.arange(2, dtype=jnp.int32)).reshape(-1)
        start = (parts * each * half)[:, None, None]
        both = jnp.stack(unit(slopes * start + squares, PERIOD), axis=2)
        return both.reshape(parts.shape[0], 2 * levels, beams)

    index = jnp.arange(turn // 4, dtype=jnp.int32)
    tiles_y = turn // 2 + 2 * (index ^ (own_turn >> 1 & turn // 4 - 1)) + bit(own_turn, 0)
    low_part = (index ^ own_turn) & (1 << far) - 1
    high_part = index >> far ^ (own_turn >> far + 1 & high - 1)
    tiles_z = (high_part * 2 + bit(own_turn, far)) * (1 << far) + low_part

    pieces = []
    for name, keep, got, steer_own, tiles in (
        ("y", keep_y, got_y, steer_y, tiles_y),
        ("z", keep_z, got_z, steer_z, tiles_z),
    ):
        shape = (turn // 2, each, pulses, width)
        data = jnp.stack([keep.reshape(shape), got.reshape(shape)])
        kept, sent = backproject(data, steer_own, interp, bases(tiles), step, leaf)
        gone = 0 if name == "y" else far
        arrived = swapped(sent, "leaf", 0)
        parts = (leaf // 2, 2, turn // 4, each, rows, width)
        kept, arrived = kept.reshape(parts), arrived.reshape(parts)
        pieces.append([(kept[:, n], arrived[:, n], gone) for n in range(2)])

    final = [[], []]
    for n in range(2):
        for chain in range(2):
            kept, arrived, gone = pieces[chain][n]
            leading = [("leaf", b) for b in range(levels - 1, 0, -1)]
            leading += [("turn", b) for b in range(top - 1, -1, -1) if b != gone]
            order = [("leaf", b) for b in range(1, levels)]
            rest = [("turn", b) for b in range(top) if b not in (0, far)]
            order = [("turn", 0)] + order if gone else order + [("turn", far)]
            for axis, b in order + rest:
                at = leading.index((axis, b))
                before, after = 1 << at, (1 << len(leading) - at - 1) * each
                leading.pop(at)
                split = (before, 2, after, rows, width)
                kept, sent = fold(kept.reshape(split), arrived.reshape(split))
                arrived = swapped(sent, axis, b)
            shape = (each, rows, width)
            total = kept.reshape(shape) + arrived.reshape(shape).astype(jnp.float32)
            final[n].append(total)
    upper = bit(own_turn, top) == 1
    sent = jnp.stack([jnp.where(upper, second, first) for first, second in final])
    kept = jnp.stack([jnp.where(upper, first, second) for first, second in final])
    shape = (tile, rows, width)
    got = swapped(sent.astype(jnp.bfloat16), "turn", top)
    return last_sum(kept.reshape(shape), got.reshape(shape))


def solution(mesh):
    placed = (P(("leaf", "turn"), None, None), P(), P(), P("leaf", None))
    return jax.shard_map(
        per_device, mesh=mesh, in_specs=placed, out_specs=P("leaf", "turn", None), check_vma=False
    )
```

```python
import functools
import math

import jax
import jax.numpy as jnp
from jax import lax
from jax.experimental import pallas as pl
from jax.experimental.pallas import tpu as pltpu
from jax.sharding import PartitionSpec as P

WEIGHTS = (-1.0 / 32, 3.0 / 32, -7.0 / 32, 21.0 / 32, 21.0 / 32, -7.0 / 32, 3.0 / 32, -1.0 / 32)
PERIOD = 4096
VMEM_BYTES = 56 * 2**20


def bits_of(count):
    return count.bit_length() - 1


def bit(value, at):
    return value >> at & 1


def swapped(array, axis, bit):
    return lax.ppermute(array, axis, [(i, i ^ 1 << bit) for i in range(lax.axis_size(axis))])


def unit(phase_int, period):
    angle = jnp.remainder(phase_int, period).astype(jnp.float32) * (2.0 * math.pi / period)
    return jnp.cos(angle), jnp.sin(angle)


def compress_kernel(dims, has_edge, chirp_ref, echo_ref, *refs):
    tile, pulses, half, near_chain, far = dims
    edge_ref, refs = (refs[0], refs[1:]) if has_edge else (None, refs)
    keep_ref, send_ref, weights, rows_ref, carry = refs
    blocks = 2 * tile
    pitch = blocks + 1
    mids = pl.num_programs(2)
    high = pl.num_programs(0)
    turn = lax.axis_index("turn")
    spot_h = (high - 1 - pl.program_id(0)) ^ (turn >> far + 1 & high - 1)
    spot_m = (mids - 1 - pl.program_id(2)) ^ (turn >> 1 & mids - 1)
    spot_v = (1 - pl.program_id(1)) ^ bit(turn, far)
    own_u = bit(turn, 0)

    @pl.when((pl.program_id(0) == 0) & (pl.program_id(1) == 0) & (pl.program_id(2) == 0))
    def _():
        rows = lax.broadcasted_iota(jnp.int32, (half, half), 0)
        cols = lax.broadcasted_iota(jnp.int32, (half, half), 1)
        taps = chirp_ref[...].astype(jnp.float32)
        tables = []
        for c in range(2):
            wide = jnp.broadcast_to(taps[c : c + 1], (half, half))
            tables.append(pltpu.roll(wide, 0, 1, stride=1, stride_axis=0).T)
        for m, mask in enumerate((rows >= cols, rows < cols)):
            re, im = (jnp.where(mask, t, 0.0) for t in tables)
            top = jnp.concatenate([re, im], axis=1)
            low = jnp.concatenate([-im, re], axis=1)
            full = jnp.concatenate([top, low], axis=0)
            weights[m * 2 * half : (m + 1) * 2 * half, :] = full.astype(jnp.bfloat16)
        if has_edge:
            for p in range(pulses):
                for c in range(2):
                    first = edge_ref[p, :, c * half : (c + 1) * half].astype(jnp.float32)
                    rows_ref[c, p : p + 1, :] = first[:1]
            edges = [rows_ref[c, :pulses, :] for c in range(2)]
            carry[...] = jnp.concatenate(edges, axis=1).astype(jnp.bfloat16)
        else:
            carry[...] = jnp.zeros_like(carry)

    for p in range(pulses):
        for c in range(2):
            rows_ref[c, p * pitch : p * pitch + blocks, :] = echo_ref[
                p, :, c * half : (c + 1) * half
            ].astype(jnp.float32)
    turned = []
    for b in range(blocks):
        parts = [rows_ref[c, pl.ds(b, pulses, stride=pitch), :] for c in range(2)]
        turned.append(jnp.concatenate(parts, axis=1).astype(jnp.bfloat16))
    turned.append(carry[...])
    current = jnp.concatenate(turned[:-1], axis=0)
    after = jnp.concatenate(turned[1:], axis=0)
    total = jnp.dot(
        jnp.concatenate([current, after], axis=1),
        weights[...],
        preferred_element_type=jnp.float32,
    ).astype(jnp.bfloat16)
    carry[...] = turned[0]

    def block(b):
        return total[b * pulses : (b + 1) * pulses]

    if near_chain:
        for side in range(2):

            @pl.when(own_u == side)
            def _(side=side):
                for b in range(blocks):
                    ref = keep_ref if b // tile == side else send_ref
                    ref[0, 0, 0, b % tile] = block(b)
    else:
        for ref, mine in ((keep_ref, 0), (send_ref, 1)):

            @pl.when(spot_v == mine)
            def _(ref=ref):
                for b in range(blocks):
                    ref[spot_h, spot_m, b // tile ^ own_u, b % tile] = block(b)


def compress(chirp, echoes, high, mids, near_chain, far, first_high):
    pulses, blocks, width = echoes.shape
    half = width // 2
    tile = blocks // lax.axis_size("turn")
    if near_chain:
        shape = (high, 2, mids, tile, pulses, width)

        def place(h, v, m):
            turn = lax.axis_index("turn")
            spot_h = (high - 1 - h) ^ (turn >> far + 1 & high - 1)
            spot_m = (mids - 1 - m) ^ (turn >> 1 & mids - 1)
            return spot_h, (1 - v) ^ bit(turn, far), spot_m, 0, 0, 0

        spec = pl.BlockSpec((1, 1, 1) + shape[3:], place)
    else:
        shape = (high, mids, 2, tile, pulses, width)
        spec = pl.BlockSpec(shape, lambda h, v, m: (0, 0, 0, 0, 0, 0))
    def chunk(h, v, m):
        return 0, ((first_high + high - 1 - h) * 2 + 1 - v) * mids + mids - 1 - m, 0

    in_specs = [
        pl.BlockSpec((2, half), lambda h, v, m: (0, 0)),
        pl.BlockSpec((pulses, 2 * tile, width), chunk),
    ]
    operands = [chirp, echoes]
    has_edge = not near_chain
    if has_edge:
        after = (first_high + high) * 2 * mids
        in_specs.append(pl.BlockSpec((pulses, 2 * tile, width), lambda h, v, m: (0, after, 0)))
        operands.append(echoes)
    dims = (tile, pulses, half, near_chain, far)
    return pl.pallas_call(
        functools.partial(compress_kernel, dims, has_edge),
        grid=(high, 2, mids),
        in_specs=in_specs,
        out_specs=[spec, spec],
        out_shape=[jax.ShapeDtypeStruct(shape, jnp.bfloat16)] * 2,
        scratch_shapes=[
            pltpu.VMEM((2 * width, width), jnp.bfloat16),
            pltpu.VMEM((2, pulses * (2 * tile + 1), half), jnp.float32),
            pltpu.VMEM((pulses, width), jnp.bfloat16),
        ],
        compiler_params=pltpu.CompilerParams(
            vmem_limit_bytes=VMEM_BYTES if near_chain else 20 * 2**20
        ),
        cost_estimate=pl.CostEstimate(
            flops=2 * pulses * blocks * width * width,
            bytes_accessed=2 * pulses * blocks * width,
            transcendentals=0,
        ),
        name="compress",
    )(*operands)


def image_kernel(dims, data_ref, steer_ref, interp_ref, base_ref, step_ref, out_keep, out_send):
    leaf, each, half, beams, levels = dims
    rows = beams // leaf
    pair = 2
    piece = rows

    def turned(phase, re, im):
        c, s = phase
        return c * re - s * im, c * im + s * re

    bases = []
    for n in range(2 * levels):
        bases.append(jnp.broadcast_to(base_ref[0, n : n + 1, :], (half, beams)).T)

    def phased(level, block, first, re, im):
        cut = slice(first, first + piece)
        lanes = slice(block * half, (block + 1) * half)
        phase = turned(
            (bases[2 * level][cut], bases[2 * level + 1][cut]),
            step_ref[level, 0, cut, lanes],
            step_ref[level, 1, cut, lanes],
        )
        return turned(phase, re, im)

    for at in range(0, each, pair):
        parts = []
        for n in range(2):
            for c in range(2):
                cols = slice(c * half, (c + 1) * half)
                parts.append(
                    jnp.concatenate([data_ref[n, 0, at + i, :, cols] for i in range(pair)], axis=1)
                )
        raw = jnp.dot(
            steer_ref[...], jnp.concatenate(parts, axis=0), preferred_element_type=jnp.float32
        )
        re, im = raw[:beams], raw[beams:]
        for level in range(levels):
            columns = []
            for i in range(pair):
                lanes = slice(i * half, (i + 1) * half)
                pieces = []
                for first in range(0, beams, piece):
                    cut = slice(first, first + piece)
                    both = phased(level, at + i, first, re[cut, lanes], im[cut, lanes])
                    if level == levels - 1:
                        both = jnp.concatenate(both, axis=1)
                        g = first // rows
                        if g < leaf // 2:
                            out_keep[g, 0, at + i] = both.astype(jnp.bfloat16)
                        else:
                            out_send[g - leaf // 2, 0, at + i] = both.astype(jnp.bfloat16)
                        continue
                    both = jnp.concatenate(both, axis=1)
                    big = both.astype(jnp.bfloat16)
                    low = (both - big.astype(jnp.float32)).astype(jnp.bfloat16)
                    pieces.append((big, low))
                if pieces:
                    columns.append(
                        jnp.concatenate([p[0] for p in pieces] + [p[1] for p in pieces], axis=0)
                    )
            if columns:
                moved = jnp.dot(
                    interp_ref[level],
                    jnp.concatenate(columns, axis=1),
                    preferred_element_type=jnp.float32,
                )
                cuts = [moved[:, n * half : (n + 1) * half] for n in range(2 * pair)]
                re = jnp.concatenate(cuts[0::2], axis=1)
                im = jnp.concatenate(cuts[1::2], axis=1)


def backproject(data, steer, interp, base, step, leaf):
    _, count, each, pulses, width = data.shape
    half = width // 2
    beams = steer.shape[0] // 2
    rows = beams // leaf
    shape = (leaf // 2, count, each, rows, width)

    def block(n):
        return n % (count // 2) * 2 + n // (count // 2)

    out_spec = pl.BlockSpec((leaf // 2, 1) + shape[2:], lambda n: (0, n, 0, 0, 0))
    return pl.pallas_call(
        functools.partial(image_kernel, (leaf, each, half, beams, bits_of(leaf))),
        grid=(count,),
        in_specs=[
            pl.BlockSpec((2, 1, each, pulses, width), lambda n: (0, block(n), 0, 0, 0)),
            pl.BlockSpec(steer.shape, lambda n: (0, 0)),
            pl.BlockSpec(interp.shape, lambda n: (0, 0, 0)),
            pl.BlockSpec((1,) + base.shape[1:], lambda n: (block(n), 0, 0)),
            pl.BlockSpec(step.shape, lambda n: (0, 0, 0, 0)),
        ],
        out_specs=[out_spec, out_spec],
        out_shape=[
            jax.ShapeDtypeStruct(shape, jnp.bfloat16),
            jax.ShapeDtypeStruct(shape, jnp.bfloat16),
        ],
        compiler_params=pltpu.CompilerParams(vmem_limit_bytes=10 * 2**20),
        cost_estimate=pl.CostEstimate(
            flops=12 * beams * pulses * count * each * width,
            bytes_accessed=2 * data.size + 6 * count * each * beams * width // 2,
            transcendentals=0,
        ),
        name="image",
    )(data, steer, interp, base, step)


def fold(keep, got):
    stay, gone = (keep[:, n] + got[:, n].astype(jnp.float32) for n in range(2))
    return stay, gone.astype(jnp.bfloat16)


def interpolation(taps, beams):
    cells = jnp.arange(beams, dtype=jnp.int32)
    weights = jnp.array(WEIGHTS, jnp.float32)
    picks = taps[..., None] == cells
    return jnp.where(picks, weights[:, None], 0.0).sum(axis=-2)


def steering(slots, matrix, side, beams, pulses, scale):
    count = slots.shape[0]
    beam = jnp.arange(beams, dtype=jnp.int32)[:, None, None]
    place = jnp.arange(pulses, dtype=jnp.int32)
    slot = slots[None, :, None]
    cos, sin = unit(
        (2 * beam + 1 - beams) * (2 * place + 1 - pulses)
        + 3 * (beam + 1) * (2 * slot + 1) * (2 * place + 1),
        8 * pulses,
    )
    pair = jnp.concatenate([cos * scale, sin * scale], axis=2).astype(jnp.bfloat16)
    moved = jnp.dot(
        matrix.astype(jnp.bfloat16),
        pair.reshape(beams, count * 2 * pulses),
        preferred_element_type=jnp.float32,
    ).reshape(beams, count, 2 * pulses)
    re, im = moved[:, :, :pulses], moved[:, :, pulses:]
    row = jnp.arange(beams, dtype=jnp.int32)
    c, s = (t[:, None, None] for t in unit(row * row * (side + 1), PERIOD))
    re, im = c * re - s * im, c * im + s * re
    top = jnp.concatenate([re, -im], axis=2)
    low = jnp.concatenate([im, re], axis=2)
    return jnp.concatenate([top, low], axis=0).astype(jnp.bfloat16)


def per_device(echoes, chirp, taps, slots):
    leaf, turn = lax.axis_size("leaf"), lax.axis_size("turn")
    pulses, blocks, width = echoes.shape
    half = width // 2
    beams = taps.shape[2]
    levels = bits_of(leaf)
    far = (bits_of(turn) + 1) // 2 - 1
    top = bits_of(turn) - 1
    mids = 1 << far - 1
    high = turn >> far + 2
    tile = blocks // turn
    each = tile // 2
    rows = beams // leaf
    own_leaf, own_turn = lax.axis_index("leaf"), lax.axis_index("turn")

    keep_y, send_y = compress(chirp, echoes, high, mids, True, far, high)
    chirp, send_y = lax.optimization_barrier((chirp, send_y))
    got_y = swapped(send_y, "turn", 0)
    keep_z, send_z = compress(chirp, echoes, high, mids, False, far, 0)
    got_z = swapped(send_z, "turn", far)

    own_sides = [bit(own_leaf, level) for level in range(levels)]
    row = jnp.arange(beams, dtype=jnp.int32)
    part, place = row // rows, row % rows
    group = own_leaf ^ (2 * (part % (leaf // 2)) + part // (leaf // 2))
    orders = [row] * (levels - 1) + [group * rows + place]
    own_taps = [
        lax.dynamic_index_in_dim(taps[n], own_sides[n], 0, False) for n in range(levels)
    ]
    groups = own_taps[-1].reshape(leaf, rows, -1)
    own_taps[-1] = jnp.concatenate(
        [
            lax.dynamic_index_in_dim(groups, own_leaf ^ (2 * g + side), 0, False)
            for side in range(2)
            for g in range(leaf // 2)
        ],
        axis=0,
    )
    matrices = interpolation(jnp.stack(own_taps), beams)
    interp = jnp.concatenate([matrices[1:]] * 2, axis=-1).astype(jnp.bfloat16)
    scale = 1.0 / math.sqrt(2.0 * slots.shape[1] * pulses)
    wanted = own_turn ^ jnp.array([0, 1, 1 << far], jnp.int32)
    picked = jnp.arange(slots.shape[1], dtype=jnp.int32) == wanted[:, None]
    own_slots = jnp.where(picked, slots, 0).sum(axis=1)
    steer = steering(own_slots, matrices[0], own_sides[0], beams, pulses, scale)
    steer_y = steer[:, :2].reshape(2 * beams, 4 * pulses)
    steer_z = jnp.concatenate([steer[:, :1], steer[:, 2:]], axis=1).reshape(2 * beams, 4 * pulses)

    leans = jnp.stack([2 * order + 1 - beams for order in orders])
    bins = jnp.arange(each * half, dtype=jnp.int32) + 1
    slopes = jnp.stack([(2 * own_sides[n] - 1) * (n + 2) for n in range(levels)])[:, None] * leans
    step = jnp.stack(unit(slopes[:, :, None] * bins, PERIOD), axis=1)
    squares = jnp.stack(
        [orders[n] * orders[n] * (own_sides[n] + 1) * (1 if n else 0) for n in range(levels)]
    )

    def bases(tiles):
        parts = (2 * tiles[:, None] + jnp.arange(2, dtype=jnp.int32)).reshape(-1)
        start = (parts * each * half)[:, None, None]
        both = jnp.stack(unit(slopes * start + squares, PERIOD), axis=2)
        return both.reshape(parts.shape[0], 2 * levels, beams)

    index = jnp.arange(turn // 4, dtype=jnp.int32)
    tiles_y = turn // 2 + 2 * (index ^ (own_turn >> 1 & turn // 4 - 1)) + bit(own_turn, 0)
    low_part = (index ^ own_turn) & (1 << far) - 1
    high_part = index >> far ^ (own_turn >> far + 1 & high - 1)
    tiles_z = (high_part * 2 + bit(own_turn, far)) * (1 << far) + low_part

    pieces = []
    for name, keep, got, steer_own, tiles in (
        ("y", keep_y, got_y, steer_y, tiles_y),
        ("z", keep_z, got_z, steer_z, tiles_z),
    ):
        shape = (turn // 2, each, pulses, width)
        data = jnp.stack([keep.reshape(shape), got.reshape(shape)])
        kept, sent = backproject(data, steer_own, interp, bases(tiles), step, leaf)
        gone = 0 if name == "y" else far
        arrived = swapped(sent, "leaf", 0)
        parts = (leaf // 2, 2, turn // 4, each, rows, width)
        kept, arrived = kept.reshape(parts), arrived.reshape(parts)
        pieces.append([(kept[:, n], arrived[:, n], gone) for n in range(2)])

    final = [[], []]
    for n in range(2):
        for chain in range(2):
            kept, arrived, gone = pieces[chain][n]
            leading = [("leaf", b) for b in range(levels - 1, 0, -1)]
            leading += [("turn", b) for b in range(top - 1, -1, -1) if b != gone]
            order = [("leaf", b) for b in range(1, levels)]
            rest = [("turn", b) for b in range(top) if b not in (0, far)]
            order = [("turn", 0)] + order if gone else order + [("turn", far)]
            for axis, b in order + rest:
                at = leading.index((axis, b))
                before, after = 1 << at, (1 << len(leading) - at - 1) * each
                leading.pop(at)
                split = (before, 2, after, rows, width)
                kept, sent = fold(kept.reshape(split), arrived.reshape(split))
                arrived = swapped(sent, axis, b)
            shape = (each, rows, width)
            total = kept.reshape(shape) + arrived.reshape(shape).astype(jnp.float32)
            final[n].append(total)
    upper = bit(own_turn, top) == 1
    sent = jnp.stack([jnp.where(upper, second, first) for first, second in final])
    kept = jnp.stack([jnp.where(upper, first, second) for first, second in final])
    shape = (tile, rows, width)
    got = swapped(sent.astype(jnp.bfloat16), "turn", top)
    total = kept.reshape(shape) + got.reshape(shape).astype(jnp.float32)
    return total.transpose(1, 0, 2).astype(jnp.bfloat16)


def solution(mesh):
    placed = (P(("leaf", "turn"), None, None), P(), P(), P("leaf", None))
    return jax.shard_map(
        per_device, mesh=mesh, in_specs=placed, out_specs=P("leaf", "turn", None), check_vma=False
    )
```
